32 devices in a mesh: sx: 16 (over z, x, core), sy: 2 (over y).
Axes of the slice: x: 2, y: 2, z: 4, core: 2. Of those that a mesh axis runs over, the one named last changes fastest.
Arguments:
- nodes: bfloat16 [16, 2, 1, 256, 256], P('sx', 'sy'), may hold values from -6 to 6
- grad_out: bfloat16 [16, 2, 1, 256, 256], P('sx', 'sy'), may hold values from -6 to 6
- w_query: bfloat16 [256, 256], replicated, as said below
- w_key: bfloat16 [256, 256], replicated, as said below
- w_value: bfloat16 [256, 256], replicated, may hold values from -0.375 to 0.375
- w_out: bfloat16 [256, 256], replicated, may hold values from -0.375 to 0.375
- w_up: bfloat16 [256, 512], replicated, may hold values from -0.375 to 0.375
- w_down: bfloat16 [512, 256], replicated, may hold values from -0.25 to 0.25
- counts: int32 [16, 2, 2], P('sx', 'sy'), may hold values from 64 to 128, as said below
- adjacency: int32 [16, 2, 2, 128, 128], P('sx', 'sy'), may hold values 0 or 1
- expander: int32 [16, 2, 3, 2, 128, 128], P('sx', 'sy'), may hold values 0 or 1
- pairing: int32 [16, 2, 3, 2], P('sx', 'sy'), may hold values from 0 to 1, each once within a row
- boundary: int32 [16, 2, 4, 128], P('sx', 'sy'), may hold values from 0 to 255, as said below
Outputs:
- layer_out: bfloat16 [16, 2, 1, 256, 256], P('sx', 'sy')
- grad_nodes: bfloat16 [16, 2, 1, 256, 256], P('sx', 'sy')
- grad_w_query: float32 [256, 256], replicated
- grad_w_key: float32 [256, 256], replicated
- grad_w_value: float32 [256, 256], replicated
- grad_w_out: float32 [256, 256], replicated
- grad_w_up: float32 [256, 512], replicated
- grad_w_down: float32 [512, 256], replicated
The draws below stay inside these ranges and needn't reach their ends.
Inputs may be any that keep to these rules, and one draw needn't show every extreme that they name: `counts`: some block holds 128 real nodes. `boundary`: the 128 slots of one side are distinct and hold real nodes. `w_query`: a projection of the normalized features. `w_key`: a projection of the normalized features.
All inputs are finite; a program needn't handle non-finite values. No bound on the sum of `adjacency` or of `expander` on one device may be relied on, other than what follows from the above.
Results may differ from the reference program's by a relative error of at most 0.014.
The reference program's roundings to bfloat16 on the way count: a program that leaves them out, or rounds other values in their place, can miss the bound.
Values may be sent and summed in bfloat16 or wider, within the bound.
No kernel may reach another device: no remote copies, remote signals or barrier semaphores. Data moves between devices by JAX's collectives and lax.ppermute only.
A program may use at most 64 MiB of HBM per device.

```python
import jax
import jax.numpy as jnp
from jax import lax

D = 256
FF = 512
HEADS = 8
HEAD_DIM = 32
BATCH = 1
BLOCK = 128
BLOCKS = 2
RIM = 128
NODES = 256
PX = 16
PY = 2


def common_counts(key):
    key = jax.random.fold_in(key, 11)
    key_first, key_second = jax.random.split(key)
    drawn_counts = jax.random.randint(key_first, (PX * PY * BLOCKS,), BLOCK // 2, BLOCK + 1)
    full_spot = jax.random.randint(key_second, (), 0, PX * PY * BLOCKS)
    drawn_counts = jnp.where(jnp.arange(PX * PY * BLOCKS) == full_spot, BLOCK, drawn_counts)
    return drawn_counts.reshape(PX, PY, BLOCKS).astype(jnp.int32)


def shared_base(key):
    key = jax.random.fold_in(key, 17)
    return jax.random.normal(key, (D, D), jnp.float32)


def draw_counts(key, part):
    shared_counts = common_counts(key)
    return shared_counts


def draw_boundary(key, part):
    usable = jnp.arange(NODES)[None, None, :] % BLOCK < jnp.repeat(common_counts(key), BLOCK, axis=2)
    key = jax.random.fold_in(key, 5)
    noise = jax.random.randint(key, (PX, PY, 4, NODES), 0, 2 ** 20)
    scores = noise * NODES + jnp.arange(NODES)
    scores = jnp.where(usable[:, :, None, :], scores, -1 - jnp.arange(NODES))
    return lax.top_k(scores, RIM)[1].astype(jnp.int32)


def draw_w_query(key, part):
    base = shared_base(key)
    return (base * D ** (-0.5)).astype(jnp.bfloat16)


def draw_w_key(key, part):
    key = jax.random.fold_in(key, 7)
    fresh_key = jax.random.fold_in(key, 0)
    fresh = jax.random.normal(fresh_key, (D, D), jnp.float32)
    return (fresh * D ** (-0.5)).astype(jnp.bfloat16)


def place_ends(result, rng, least, top_value):
    dims = result.shape
    index_at = [jax.random.randint(jax.random.fold_in(rng, axis), (), 0, dims[axis]) for axis in range(len(dims))]
    result = result.at[tuple(index_at)].set(least)
    longest = dims.index(max(dims))
    index_at[longest] = (index_at[longest] + 1) % dims[longest]
    return result.at[tuple(index_at)].set(top_value)


def level_of(rng, extent, shards, smallest, high):
    factor_of, own = 1.0, jax.random.fold_in(rng, 6)
    for position, blocks in shards:
        draws = jnp.exp(jax.random.uniform(jax.random.fold_in(own, position), (blocks,), jnp.float32, smallest / len(shards), high / len(shards)))
        factor_of = factor_of * jnp.repeat(draws, extent[position] // blocks).reshape([-1 if axis == position else 1 for axis in range(len(extent))])
    return factor_of


def normal_values(key, extent, scale, reach, shards=(), kind=jnp.bfloat16):
    values = scale * jax.random.normal(key, extent, jnp.float32)
    if shards:
        values = values * level_of(key, extent, shards, -0.22, 0.18)
    return jnp.clip(values, -reach, reach).astype(kind)


def setup_inputs(seed: int = 0) -> dict:
    key_of = jax.random.split(jax.random.key(seed), 14)
    nodes = normal_values(key_of[0], (PX, PY, BATCH, NODES, D), 1.0, 6.0, ((0, 16), (1, 2)))
    grad_out = normal_values(key_of[1], (PX, PY, BATCH, NODES, D), 1.0, 6.0, ((0, 16), (1, 2)))
    w_query = draw_w_query(jax.random.fold_in(key_of[13], 71), 0)
    w_key = draw_w_key(jax.random.fold_in(key_of[13], 71), 0)
    w_value = normal_values(key_of[4], (D, D), D ** -0.5, 0.375)
    w_out = normal_values(key_of[5], (D, D), D ** -0.5, 0.375)
    w_up = normal_values(key_of[6], (D, FF), D ** -0.5, 0.375)
    w_down = normal_values(key_of[7], (FF, D), FF ** -0.5, 0.25)
    counts = draw_counts(jax.random.fold_in(key_of[13], 71), 0)
    adjacency = place_ends((jax.random.randint(key_of[9], (PX, PY, BLOCKS, BLOCK, BLOCK), 0, BLOCK) < 4).astype(jnp.int32), jax.random.fold_in(key_of[9], 1), 0, 1)
    expander = place_ends((jax.random.randint(key_of[10], (PX, PY, 3, BLOCKS, BLOCK, BLOCK), 0, BLOCK) < 4).astype(jnp.int32), jax.random.fold_in(key_of[10], 1), 0, 1)
    pairing = jax.vmap(lambda own: jax.random.permutation(own, BLOCKS))(jax.random.split(key_of[11], PX * PY * 3)).reshape((PX, PY, 3, BLOCKS)).astype(jnp.int32)
    boundary = draw_boundary(jax.random.fold_in(key_of[13], 71), 0)
    return {"nodes": nodes, "grad_out": grad_out, "w_query": w_query, "w_key": w_key, "w_value": w_value, "w_out": w_out, "w_up": w_up, "w_down": w_down, "counts": counts, "adjacency": adjacency, "expander": expander, "pairing": pairing, "boundary": boundary}


EPSILON = 1e-06
NEG_FILL = -1e+30

def rms_forward(inputs):
    factor = lax.rsqrt(lax.optimization_barrier(jnp.mean(inputs * inputs, axis=-1, keepdims=True)) + EPSILON)
    return inputs * factor

def rms_backward(inputs, cotangent):
    factor = lax.rsqrt(lax.optimization_barrier(jnp.mean(inputs * inputs, axis=-1, keepdims=True)) + EPSILON)
    normed = inputs * factor
    return factor * (cotangent - normed * lax.optimization_barrier(jnp.mean(cotangent * normed, axis=-1, keepdims=True)))

def gelu_tanh(inputs):
    return jax.nn.gelu(inputs, approximate=True)

def gelu_backward(inputs, cotangent):
    return jax.vjp(gelu_tanh, inputs)[1](cotangent)[0]

def rounded(array):
    return lax.optimization_barrier(array.astype(jnp.bfloat16)).astype(jnp.float32)

def head_split(array):
    return array.reshape(array.shape[:-1] + (HEADS, HEAD_DIM)).astype(jnp.float32)

def head_merge(array):
    return array.reshape(array.shape[:-2] + (HEADS * HEAD_DIM,))

def attention_weights(queries, key_rows, key_mask, rim_keys, rim_mask):
    score_scale = HEAD_DIM ** (-0.5)
    head_queries = head_split(queries)
    main_scores = jnp.einsum('bnqhe,bnkhe->bnhqk', head_queries, head_split(key_rows)) * score_scale
    rim_scores = jnp.einsum('bnqhe,bnqshe->bnhqs', head_queries, head_split(rim_keys)) * score_scale
    main_scores = jnp.where(key_mask[None, :, None], main_scores, NEG_FILL)
    rim_scores = jnp.where(rim_mask[None, :, None], rim_scores, NEG_FILL)
    largest = jnp.maximum(lax.optimization_barrier(jnp.max(main_scores, axis=-1, keepdims=True)), lax.optimization_barrier(jnp.max(rim_scores, axis=-1, keepdims=True)))
    main_exp = jnp.exp(main_scores - largest)
    rim_exp = jnp.exp(rim_scores - largest)
    totals = lax.optimization_barrier(jnp.sum(main_exp, axis=-1, keepdims=True)) + lax.optimization_barrier(jnp.sum(rim_exp, axis=-1, keepdims=True))
    return (main_exp / totals, rim_exp / totals)

def attend(queries, key_rows, value_rows, key_mask, rim_keys, rim_values, rim_mask):
    main_prob, rim_prob = attention_weights(queries, key_rows, key_mask, rim_keys, rim_mask)
    mixed = jnp.einsum('bnhqk,bnkhe->bnqhe', rounded(main_prob), head_split(value_rows))
    mixed = mixed + jnp.einsum('bnhqs,bnqshe->bnqhe', rounded(rim_prob), head_split(rim_values))
    return head_merge(mixed).astype(jnp.bfloat16)

def attend_back(queries, key_rows, value_rows, key_mask, rim_keys, rim_values, rim_mask, out_grad):
    main_prob, rim_prob = attention_weights(queries, key_rows, key_mask, rim_keys, rim_mask)
    score_scale = HEAD_DIM ** (-0.5)
    upstream = head_split(out_grad)
    head_queries = head_split(queries)
    main_dot = jnp.einsum('bnqhe,bnkhe->bnhqk', upstream, head_split(value_rows))
    rim_dot = jnp.einsum('bnqhe,bnqshe->bnhqs', upstream, head_split(rim_values))
    inner = lax.optimization_barrier(jnp.sum(main_prob * main_dot, axis=-1, keepdims=True)) + lax.optimization_barrier(jnp.sum(rim_prob * rim_dot, axis=-1, keepdims=True))
    main_grad = rounded(main_prob * (main_dot - inner) * score_scale)
    rim_grad = rounded(rim_prob * (rim_dot - inner) * score_scale)
    query_grad = jnp.einsum('bnhqk,bnkhe->bnqhe', main_grad, head_split(key_rows))
    query_grad = query_grad + jnp.einsum('bnhqs,bnqshe->bnqhe', rim_grad, head_split(rim_keys))
    key_grad = jnp.einsum('bnhqk,bnqhe->bnkhe', main_grad, head_queries)
    value_grad = jnp.einsum('bnhqk,bnqhe->bnkhe', rounded(main_prob), upstream)
    rim_key_grad = jnp.einsum('bnhqs,bnqhe->bnqshe', rim_grad, head_queries)
    rim_value_grad = jnp.einsum('bnhqs,bnqhe->bnqshe', rounded(rim_prob), upstream)
    return (head_merge(query_grad), head_merge(key_grad), head_merge(value_grad), head_merge(rim_key_grad), head_merge(rim_value_grad))

def shift_grid(array, axis, step):
    length = array.shape[axis]
    moved = jnp.roll(array, step, axis=axis)
    source = jnp.arange(length) - step
    inside = (source >= 0) & (source < length)
    shape_list = [1] * array.ndim
    shape_list[axis] = length
    return jnp.where(inside.reshape(shape_list), moved, jnp.zeros_like(moved))

def partner_of(array, matching):
    if matching == 1:
        order = jnp.bitwise_xor(jnp.arange(PY), PY // 2)
        return jnp.take(array, order, axis=1)
    stride = PX // 2 if matching == 0 else PX // 4
    order = jnp.bitwise_xor(jnp.arange(PX), stride)
    return jnp.take(array, order, axis=0)

def flatten_grid(array):
    return array.reshape((PX * PY,) + array.shape[2:])

def gram_all(left, right):
    return jnp.einsum('xyzni,xyznj->ij', left.astype(jnp.float32), right.astype(jnp.float32))

def back_project(kv_rows, w_key, w_value):
    kv_bf = kv_rows.astype(jnp.bfloat16)
    first = jnp.dot(kv_bf[..., :D], w_key.T, preferred_element_type=jnp.float32)
    return first + jnp.dot(kv_bf[..., D:], w_value.T, preferred_element_type=jnp.float32)

def reference(nodes, grad_out, w_query, w_key, w_value, w_out, w_up, w_down, counts, adjacency, expander, pairing, boundary):
    node_shape = (PX, PY, BATCH, NODES, D)
    pair_shape = (PX, PY, BATCH, BLOCKS, BLOCK, 2 * D)
    node_slot = jnp.arange(NODES) % BLOCK
    usable = node_slot[None, None, :] < jnp.repeat(counts, BLOCK, axis=2)
    usable_float = usable.astype(jnp.float32)
    usable_blocks = usable.reshape(PX, PY, BLOCKS, BLOCK)
    usable_rows = usable_float[:, :, None, :, None]
    features = nodes.astype(jnp.float32)
    normed_in = rms_forward(features).astype(jnp.bfloat16)
    queries = jnp.dot(normed_in, w_query, preferred_element_type=jnp.float32).astype(jnp.bfloat16)
    key_rows = jnp.dot(normed_in, w_key, preferred_element_type=jnp.float32).astype(jnp.bfloat16)
    value_rows = jnp.dot(normed_in, w_value, preferred_element_type=jnp.float32).astype(jnp.bfloat16)
    joined = jnp.concatenate([key_rows, value_rows], axis=-1).astype(jnp.float32)
    identity = jnp.eye(BLOCK, dtype=bool)
    key_parts = [joined.reshape(pair_shape)]
    mask_parts = [(adjacency == 1) & usable_blocks[:, :, :, None, :] | identity]
    selections = []
    for matching in range(3):
        select_map = (pairing[:, :, matching, :, None] == jnp.arange(BLOCKS)).astype(jnp.float32)
        selections.append(select_map)
        far_rows = partner_of(joined.reshape(pair_shape), matching)
        key_parts.append(jnp.einsum('xybc,xyzcqe->xyzbqe', select_map, far_rows))
        far_usable = jnp.einsum('xybc,xycq->xybq', select_map, partner_of(usable_blocks.astype(jnp.float32), matching)) > 0.5
        mask_parts.append((expander[:, :, matching] == 1) & far_usable[:, :, :, None, :])
    all_joined = jnp.concatenate(key_parts, axis=4).astype(jnp.bfloat16)
    all_keys = all_joined[..., :D]
    all_values = all_joined[..., D:]
    all_masks = jnp.concatenate(mask_parts, axis=4)
    places = [(boundary[:, :, side, None, :] == jnp.arange(NODES)[:, None]).astype(jnp.float32) for side in range(4)]
    outgoing = [jnp.einsum('xynr,xyzne->xyzre', places[side], joined) for side in range(4)]
    arrived = [shift_grid(outgoing[1], 0, 1), shift_grid(outgoing[0], 0, -1), shift_grid(outgoing[3], 1, 1), shift_grid(outgoing[2], 1, -1)]
    ones_grid = jnp.ones((PX, PY), jnp.float32)
    exists = jnp.stack([shift_grid(ones_grid, 0, 1), shift_grid(ones_grid, 0, -1), shift_grid(ones_grid, 1, 1), shift_grid(ones_grid, 1, -1)], axis=-1) > 0.5
    rim_rows = [jnp.einsum('xynr,xyzre->xyzne', places[side], arrived[side]) for side in range(4)]
    rim_joined = jnp.stack(rim_rows, axis=4).astype(jnp.bfloat16).reshape(PX, PY, BATCH, BLOCKS, BLOCK, 4, 2 * D)
    rim_keys = rim_joined[..., :D]
    rim_values = rim_joined[..., D:]
    placed = jnp.stack([lax.optimization_barrier(jnp.sum(places[side], axis=3)) > 0.5 for side in range(4)], axis=-1)
    rim_mask = (placed & exists[:, :, None, :]).reshape(PX, PY, BLOCKS, BLOCK, 4)
    query_blocks = queries.reshape(PX, PY, BATCH, BLOCKS, BLOCK, D)
    pieces = (flatten_grid(query_blocks), flatten_grid(all_keys), flatten_grid(all_values), flatten_grid(all_masks), flatten_grid(rim_keys), flatten_grid(rim_values), flatten_grid(rim_mask))
    attended = lax.map(lambda inputs: attend(*inputs), pieces).reshape(node_shape)
    hidden_in = features + jnp.dot(attended, w_out, preferred_element_type=jnp.float32)
    normed_mid = rms_forward(hidden_in).astype(jnp.bfloat16)
    pre_act = jnp.dot(normed_mid, w_up, preferred_element_type=jnp.float32)
    activ = gelu_tanh(pre_act).astype(jnp.bfloat16)
    ffn_out = jnp.dot(activ, w_down, preferred_element_type=jnp.float32)
    layer_out = ((hidden_in + ffn_out) * usable_rows).astype(jnp.bfloat16)
    upstream = grad_out.astype(jnp.float32) * usable_rows
    upstream_bf = upstream.astype(jnp.bfloat16)
    grad_w_down = gram_all(activ, upstream_bf)
    grad_act = jnp.dot(upstream_bf, w_down.T, preferred_element_type=jnp.float32)
    grad_pre = gelu_backward(pre_act, grad_act).astype(jnp.bfloat16)
    grad_w_up = gram_all(normed_mid, grad_pre)
    grad_mid = jnp.dot(grad_pre, w_up.T, preferred_element_type=jnp.float32)
    grad_hidden = upstream + rms_backward(hidden_in, grad_mid)
    grad_hidden_bf = grad_hidden.astype(jnp.bfloat16)
    grad_w_out = gram_all(attended, grad_hidden_bf)
    grad_attended = jnp.dot(grad_hidden_bf, w_out.T, preferred_element_type=jnp.float32).astype(jnp.bfloat16)
    back_pieces = pieces + (flatten_grid(grad_attended.reshape(PX, PY, BATCH, BLOCKS, BLOCK, D)),)
    query_grad, key_grad, value_grad, rim_key_grad, rim_value_grad = lax.map(lambda inputs: attend_back(*inputs), back_pieces)
    joined_grad = rounded(jnp.concatenate([key_grad, value_grad], axis=-1)).reshape(PX, PY, BATCH, BLOCKS, 4 * BLOCK, 2 * D)
    kv_total = joined_grad[:, :, :, :, :BLOCK].reshape(PX, PY, BATCH, NODES, 2 * D)
    node_back = back_project(kv_total, w_key, w_value)
    for matching in range(3):
        piece = joined_grad[:, :, :, :, (matching + 1) * BLOCK:(matching + 2) * BLOCK]
        back = jnp.einsum('xybc,xyzbqe->xyzcqe', selections[matching], piece)
        far_back = partner_of(back, matching).reshape(PX, PY, BATCH, NODES, 2 * D)
        kv_total = kv_total + far_back
        node_back = node_back + rounded(back_project(far_back, w_key, w_value))
    rim_grad = rounded(jnp.concatenate([rim_key_grad, rim_value_grad], axis=-1)).reshape(PX, PY, BATCH, NODES, 4, 2 * D)
    outgoing_grads = [jnp.einsum('xynr,xyzne->xyzre', places[side], rim_grad[:, :, :, :, side]) for side in range(4)]
    returned = [shift_grid(outgoing_grads[1], 0, 1), shift_grid(outgoing_grads[0], 0, -1), shift_grid(outgoing_grads[3], 1, 1), shift_grid(outgoing_grads[2], 1, -1)]
    for side in range(4):
        kv_total = kv_total + jnp.einsum('xynr,xyzre->xyzne', places[side], returned[side])
        projected_rim = rounded(back_project(returned[side], w_key, w_value))
        node_back = node_back + jnp.einsum('xynr,xyzre->xyzne', places[side], projected_rim)
    query_total = query_grad.reshape(node_shape).astype(jnp.bfloat16)
    grad_w_query = gram_all(normed_in, query_total)
    grad_w_key = gram_all(normed_in, kv_total[..., :D])
    grad_w_value = gram_all(normed_in, kv_total[..., D:])
    grad_normed = jnp.dot(query_total, w_query.T, preferred_element_type=jnp.float32) + node_back
    grad_nodes = (grad_hidden + rms_backward(features, grad_normed)).astype(jnp.bfloat16)
    return (layer_out, grad_nodes, grad_w_query, grad_w_key, grad_w_value, grad_w_out, grad_w_up, grad_w_down)
```

```python
import math

import jax
import jax.numpy as jnp
from jax import lax
from jax.experimental import pallas as pl
from jax.experimental.pallas import tpu as pltpu
from jax.sharding import PartitionSpec as P

HEADS = 8
HEAD_DIM = 32
EPSILON = 1e-06
NEG_FILL = -1e30
AXES = ("sx", "sy")
EXTRA = 16
MATCHINGS = 3
SIDES = 4
F32 = jnp.float32
BF16 = jnp.bfloat16
GELU_C = math.sqrt(2.0 / math.pi)
GELU_A = 0.044715


def nn(a, b):
    return lax.dot_general(a, b, (((1,), (0,)), ((), ())), preferred_element_type=F32)


def nt(a, b):
    return lax.dot_general(a, b, (((1,), (1,)), ((), ())), preferred_element_type=F32)


def tn(a, b):
    return lax.dot_general(a, b, (((0,), (0,)), ((), ())), preferred_element_type=F32)


def iota(shape, dim):
    return lax.broadcasted_iota(jnp.int32, shape, dim)


def to_bf(mask):
    return jnp.where(mask, 1.0, 0.0).astype(BF16)


def flip(value):
    return jnp.transpose(value.astype(F32), (1, 0))


def from_behind(block, axis, distance):
    devices = range(lax.axis_size(axis))
    return lax.ppermute(block, axis, [(i - distance, i) for i in devices if i - distance in devices])


def xor_permute(value, mask):
    count = lax.axis_size("sx") * lax.axis_size("sy")
    return lax.ppermute(value, AXES, [(i, i ^ mask) for i in range(count)])


def call(kernel, outs, args, smem=0, scratch=(), limit=48, flops=0, nbytes=0):
    specs = [pl.BlockSpec(memory_space=pltpu.SMEM)] * smem
    specs += [pl.BlockSpec(memory_space=pltpu.VMEM)] * (len(args) - smem)
    return pl.pallas_call(
        kernel,
        out_shape=[jax.ShapeDtypeStruct(s, d) for s, d in outs],
        in_specs=specs,
        out_specs=[pl.BlockSpec(memory_space=pltpu.VMEM)] * len(outs),
        scratch_shapes=list(scratch),
        compiler_params=pltpu.CompilerParams(vmem_limit_bytes=limit * 2**20),
        cost_estimate=pl.CostEstimate(flops=flops, bytes_accessed=nbytes, transcendentals=0),
    )(*args)


def prepare_kernel(counts, nodes, boundary, pack, *rims):
    count, width = nodes.shape
    blocks = counts.shape[0]
    size = count // blocks
    feats = nodes[...].astype(F32)
    normed = (feats * lax.rsqrt(jnp.mean(feats * feats, axis=1, keepdims=True) + EPSILON)).astype(BF16)
    pack[0:count, :] = normed
    lane = iota((EXTRA, count), 1)
    row = iota((EXTRA, count), 0)
    limit = jnp.zeros((EXTRA, count), jnp.int32)
    for b in range(blocks):
        limit = jnp.where(lane // size == b, counts[b], limit)
    extra = jnp.where((row == 0) & (lane % size < limit), 1.0, 0.0)
    rim = boundary.shape[1]
    slots = boundary[...].astype(F32)
    for side in range(SIDES):
        line = slots[side : side + 1, :]
        if count > rim:
            line = jnp.concatenate([line, jnp.zeros((1, count - rim), F32)], axis=1)
        extra = jnp.where(row == side + 1, line, extra)
    pack[count : count + EXTRA, :] = extra.astype(BF16)
    for side, out in enumerate(rims):
        place = to_bf(iota((count, rim), 0) == boundary[side : side + 1, :])
        out[...] = tn(place, normed).astype(BF16)


def head_rows(width, shape, dim):
    return iota(shape, dim) // HEAD_DIM


def main_kernel(merge_y, info, counts, pairing, nodes, gout, wq, wk, wv, wo, wup, wdown, adjacency, expander, boundary, *refs):
    packs = refs[: MATCHINGS + 1]
    rims = refs[MATCHINGS + 1 : MATCHINGS + 1 + (2 if merge_y else 4)]
    refs = refs[MATCHINGS + 1 + len(rims) :]
    layer_out, grad_hidden_out, grad_normed_out = refs[:3]
    backs = refs[3 : 3 + MATCHINGS]
    rim_outs = refs[3 + MATCHINGS : 3 + MATCHINGS + len(rims)]
    refs = refs[3 + MATCHINGS + len(rims) :]
    keep, send = refs[:2]
    grads, xcat, kvg, probs, pbf, sgrad, qstack, gstack = refs[2:]

    count, width = nodes.shape
    hidden_units = wup.shape[1]
    blocks = counts.shape[0]
    size = count // blocks
    keys = (MATCHINGS + 1) * size
    rim = boundary.shape[1]
    scale = HEAD_DIM**-0.5
    log2e = math.log2(math.e)

    normed = packs[0][0:count, :]
    feats = nodes[...].astype(F32)
    for b in range(blocks):
        xcat[b * keys : b * keys + size, :] = packs[0][b * size : (b + 1) * size, :]
        for m in range(MATCHINGS):
            start = pl.multiple_of(pairing[m, b] * size, size)
            lo = b * keys + (m + 1) * size
            xcat[lo : lo + size, :] = packs[m + 1][pl.ds(start, size), :]
    base = blocks * keys
    places, moves = [], [None, None, None, None]
    for s in range(SIDES):
        here = (iota((count, rim), 0) == boundary[s : s + 1, :]) & (info[s] > 0)
        places.append(to_bf(here))
    for s in range(SIDES):
        if merge_y and s >= 2:
            other = 3 if s == 2 else 2
            far_slots = packs[2][count : count + EXTRA, :].astype(F32)[other + 1 : other + 2, 0:rim]
            spots = to_bf(iota((count, rim), 0).astype(F32) == far_slots)
            moves[s] = nt(places[s], spots).astype(BF16)
            rows = nn(moves[s], packs[2][0:count, :])
        else:
            rows = nn(places[s], rims[s][...])
        xcat[base + s * count : base + (s + 1) * count, :] = rows.astype(BF16)

    queries = nn(normed, wq[...]).astype(BF16)
    queries_t = flip(queries).astype(BF16)
    wk_t = flip(wk[...]).astype(BF16)
    wv_t = flip(wv[...]).astype(BF16)
    key_rows, key_cols, value_rows, value_cols = [], [], [], []
    for b in range(blocks):
        rows = xcat[b * keys : (b + 1) * keys, :]
        key_rows.append(nn(rows, wk[...]).astype(BF16))
        value_rows.append(nn(rows, wv[...]).astype(BF16))
        key_cols.append(nt(wk_t, rows).astype(BF16))
        value_cols.append(nt(wv_t, rows).astype(BF16))
    rim_keys, rim_values = [], []
    for s in range(SIDES):
        rows = xcat[base + s * count : base + (s + 1) * count, :]
        rim_keys.append(nn(rows, wk[...]).astype(BF16).astype(F32))
        rim_values.append(nn(rows, wv[...]).astype(BF16).astype(F32))

    bias = []
    eye = iota((size, size), 0) == iota((size, size), 1)
    for b in range(blocks):
        parts = []
        for g in range(MATCHINGS + 1):
            flags = packs[g][count : count + EXTRA, :].astype(F32)[0:1, :]
            if g == 0:
                real = flags[:, b * size : (b + 1) * size] > 0.5
                mask = ((adjacency[b] == 1) & real) | eye
            else:
                pick = flags[:, 0:size]
                for c in range(1, blocks):
                    pick = jnp.where(pairing[g - 1, b] == c, flags[:, c * size : (c + 1) * size], pick)
                mask = (expander[g - 1, b] == 1) & (pick > 0.5)
            parts.append(flip(jnp.where(mask, 0.0, NEG_FILL)))
        bias.append(jnp.concatenate(parts, axis=0))

    spread = to_bf(head_rows(width, (HEADS, width), 1) == iota((HEADS, width), 0))

    def head_sums(product):
        high = product.astype(BF16)
        low = (product - high.astype(F32)).astype(BF16)
        return nt(spread, high) + nt(spread, low)

    queries_f = queries.astype(F32)
    ones = jnp.ones((HEADS, rim), BF16)
    rim_scores = []
    for s in range(SIDES):
        there = nt(ones, places[s]) > 0.5
        score = head_sums(queries_f * rim_keys[s]) * (scale * log2e)
        rim_scores.append(jnp.where(there, score, NEG_FILL))
    rim_top = jnp.maximum(jnp.maximum(rim_scores[0], rim_scores[1]), jnp.maximum(rim_scores[2], rim_scores[3]))

    row_head = head_rows(width, (width, size), 0)
    tops, sums = [], []
    att_blocks = []
    for b in range(blocks):
        cols = slice(b * size, (b + 1) * size)
        top_rows, inv_rows, att_rows = [], [], []
        for h in range(HEADS):
            own = queries_t[:, cols]
            masked = jnp.where(row_head == h, own, jnp.zeros_like(own))
            score = nn(key_rows[b], masked) * (scale * log2e) + bias[b]
            top = jnp.maximum(jnp.max(score, axis=0, keepdims=True), rim_top[h : h + 1, cols])
            grown = jnp.exp2(score - top)
            total = jnp.sum(grown, axis=0, keepdims=True)
            for s in range(SIDES):
                total = total + jnp.exp2(rim_scores[s][h : h + 1, cols] - top)
            inverse = 1.0 / total
            prob = grown * inverse
            at = slice(h * size, (h + 1) * size)
            probs[b, :, at] = prob
            prob_bf = prob.astype(BF16)
            pbf[b, :, at] = prob_bf
            att_rows.append(nn(value_cols[b][h * HEAD_DIM : (h + 1) * HEAD_DIM, :], prob_bf))
            top_rows.append(top)
            inv_rows.append(inverse)
        tops.append(jnp.concatenate(top_rows, axis=0))
        sums.append(jnp.concatenate(inv_rows, axis=0))
        att_blocks.append(jnp.concatenate(att_rows, axis=0))
    top_all = jnp.concatenate(tops, axis=1)
    inv_all = jnp.concatenate(sums, axis=1)
    mixed = flip(jnp.concatenate(att_blocks, axis=1))
    rim_probs = [jnp.exp2(rim_scores[s] - top_all) * inv_all for s in range(SIDES)]
    rim_wide = [tn(rim_probs[s].astype(BF16), spread) for s in range(SIDES)]
    for s in range(SIDES):
        mixed = mixed + rim_wide[s] * rim_values[s]
    attended = mixed.astype(BF16)

    slot = iota((count, width), 0)
    limit = jnp.zeros((count, width), jnp.int32)
    for b in range(blocks):
        limit = jnp.where(slot // size == b, counts[b], limit)
    usable = jnp.where(slot % size < limit, 1.0, 0.0)
    hidden = feats + nn(attended, wo[...])
    factor = lax.rsqrt(jnp.mean(hidden * hidden, axis=1, keepdims=True) + EPSILON)
    mid = hidden * factor
    normed_mid = mid.astype(BF16)
    pre = nn(normed_mid, wup[...])
    square = pre * pre
    bent = jnp.tanh(GELU_C * pre * (1.0 + GELU_A * square))
    half = 0.5 * (1.0 + bent)
    activ = (pre * half).astype(BF16)
    layer_out[...] = ((hidden + nn(activ, wdown[...])) * usable).astype(BF16)
    upstream = gout[...].astype(F32) * usable
    upstream_bf = upstream.astype(BF16)
    grads[4 * width + hidden_units * 1 : 4 * width + 2 * hidden_units, :] = tn(activ, upstream_bf)
    slope = half + 0.5 * pre * (1.0 - bent * bent) * (GELU_C * (1.0 + 3.0 * GELU_A * square))
    grad_pre = (slope * nt(upstream_bf, wdown[...])).astype(BF16)
    grad_up = tn(normed_mid, grad_pre)
    for part in range(hidden_units // width):
        lo = 4 * width + part * width
        grads[lo : lo + width, :] = grad_up[:, part * width : (part + 1) * width]
    grad_mid = nt(grad_pre, wup[...])
    grad_hidden = upstream + factor * (grad_mid - mid * jnp.mean(grad_mid * mid, axis=1, keepdims=True))
    grad_hidden_out[...] = grad_hidden
    grad_hidden_bf = grad_hidden.astype(BF16)
    grads[3 * width : 4 * width, :] = tn(attended, grad_hidden_bf)
    grad_att = nt(grad_hidden_bf, wo[...]).astype(BF16)
    grad_att_f = grad_att.astype(F32)
    grad_att_t = flip(grad_att).astype(BF16)

    lane_head = head_rows(width, (size, width), 1)
    rim_dots = [head_sums(grad_att_f * rim_values[s]) for s in range(SIDES)]
    rim_inner = rim_probs[0] * rim_dots[0]
    for s in range(1, SIDES):
        rim_inner = rim_inner + rim_probs[s] * rim_dots[s]
    inner_blocks, query_blocks = [], []
    for b in range(blocks):
        cols = slice(b * size, (b + 1) * size)
        inner_rows, query_rows = [], []
        for h in range(HEADS):
            own = grad_att_t[:, cols]
            masked = jnp.where(row_head == h, own, jnp.zeros_like(own))
            dots = nn(value_rows[b], masked)
            at = slice(h * size, (h + 1) * size)
            prob = probs[b, :, at]
            inner = jnp.sum(prob * dots, axis=0, keepdims=True) + rim_inner[h : h + 1, cols]
            graded = (prob * (dots - inner) * scale).astype(BF16)
            sgrad[b, :, at] = graded
            query_rows.append(nn(key_cols[b][h * HEAD_DIM : (h + 1) * HEAD_DIM, :], graded))
            inner_rows.append(inner)
            mine = queries[cols, :]
            qstack[at, :] = jnp.where(lane_head == h, mine, jnp.zeros_like(mine))
            mine = grad_att[cols, :]
            gstack[at, :] = jnp.where(lane_head == h, mine, jnp.zeros_like(mine))
        inner_blocks.append(jnp.concatenate(inner_rows, axis=0))
        query_blocks.append(jnp.concatenate(query_rows, axis=0))
        span = slice(b * keys, (b + 1) * keys)
        kvg[span, 0:width] = nn(sgrad[b], qstack[...]).astype(BF16)
        kvg[span, width : 2 * width] = nn(pbf[b], gstack[...]).astype(BF16)
    inner_all = jnp.concatenate(inner_blocks, axis=1)
    query_grad = flip(jnp.concatenate(query_blocks, axis=1))
    for s in range(SIDES):
        graded = (rim_probs[s] * (rim_dots[s] - inner_all) * scale).astype(BF16)
        wide = tn(graded, spread)
        query_grad = query_grad + wide * rim_keys[s]
        span = slice(base + s * count, base + (s + 1) * count)
        kvg[span, 0:width] = (wide * queries_f).astype(BF16)
        kvg[span, width : 2 * width] = (rim_wide[s] * grad_att_f).astype(BF16)
    query_total = query_grad.astype(BF16)

    own_rows = []
    extra_back = None
    for s in range(SIDES):
        span = slice(base + s * count, base + (s + 1) * count)
        back = (nn(kvg[span, 0:width], wk_t) + nn(kvg[span, width : 2 * width], wv_t)).astype(BF16)
        if merge_y and s >= 2:
            moved = tn(moves[s], back)
            extra_back = moved if extra_back is None else extra_back + moved
        else:
            rim_outs[s][...] = tn(places[s], back).astype(BF16)
    if merge_y:
        grads[0:count, :] = extra_back
    for b in range(blocks):
        span = slice(b * keys, (b + 1) * keys)
        back = nn(kvg[span, 0:width], wk_t) + nn(kvg[span, width : 2 * width], wv_t)
        own_rows.append(back[0:size])
        for m in range(MATCHINGS):
            start = pl.multiple_of(pairing[m, b] * size, size)
            piece = back[(m + 1) * size : (m + 2) * size]
            if merge_y and m == 1:
                piece = piece + grads[pl.ds(start, size), :]
            backs[m][pl.ds(start, size), :] = piece.astype(BF16)
    grad_normed_out[...] = nt(query_total, wq[...]) + jnp.concatenate(own_rows, axis=0)

    grads[0:width, :] = tn(normed, query_total)
    both = tn(xcat[...], kvg[...])
    grads[width : 2 * width, :] = both[:, 0:width]
    grads[2 * width : 3 * width, :] = both[:, width : 2 * width]

    half_rows = grads.shape[0] // 2
    mine = info[SIDES]
    keep[...] = grads[pl.ds(pl.multiple_of(mine * half_rows, half_rows), half_rows), :]
    send[...] = grads[pl.ds(pl.multiple_of((1 - mine) * half_rows, half_rows), half_rows), :].astype(BF16)


def nodes_kernel(merge_y, nodes, grad_hidden, grad_normed, boundary, *refs):
    out = refs[-1]
    backs, rims = refs[:MATCHINGS], refs[MATCHINGS:-1]
    count = nodes.shape[0]
    rim = boundary.shape[1]
    cot = grad_normed[...]
    for back in backs:
        cot = cot + back[...].astype(F32)
    for s, rows in enumerate(rims):
        place = to_bf(iota((count, rim), 0) == boundary[s : s + 1, :])
        cot = cot + nn(place, rows[...])
    feats = nodes[...].astype(F32)
    factor = lax.rsqrt(jnp.mean(feats * feats, axis=1, keepdims=True) + EPSILON)
    normed = feats * factor
    out[...] = (grad_hidden[...] + factor * (cot - normed * jnp.mean(cot * normed, axis=1, keepdims=True))).astype(BF16)


def reduce_kernel(place, parts, kept_rows, *refs):
    info, kept = refs[0], refs[1]
    received = refs[2 : 2 + kept_rows]
    outs = refs[2 + kept_rows : -1]
    total_ref = refs[-1]
    total = kept[...].astype(F32)
    for piece in received:
        total = total + piece[...].astype(F32)
    if parts == 1:
        outs[0][...] = total.astype(BF16)
        return
    total_ref[...] = total
    rows = total.shape[0] // parts
    mine = info[place]
    outs[0][...] = total_ref[pl.ds(pl.multiple_of(mine * rows, rows), rows), :]
    for d in range(1, parts):
        outs[d][...] = total_ref[pl.ds(pl.multiple_of((mine ^ d) * rows, rows), rows), :].astype(BF16)


def gather_kernel(place, *refs):
    info, pieces, out = refs[0], refs[1:-1], refs[-1]
    mine = info[place]
    rows = pieces[0].shape[0]
    for d, piece in enumerate(pieces):
        out[pl.ds(pl.multiple_of((mine ^ d) * rows, rows), rows), :] = piece[...]


def final_kernel(place, info, own, other, *refs):
    outs, full = refs[:-1], refs[-1]
    rows = own.shape[0]
    mine = info[place]
    full[pl.ds(pl.multiple_of(mine * rows, rows), rows), :] = own[...]
    full[pl.ds(pl.multiple_of((1 - mine) * rows, rows), rows), :] = other[...]
    width = full.shape[1]
    row = 0
    for out in outs:
        for part in range(out.shape[1] // width):
            out[:, part * width : (part + 1) * width] = full[row : row + out.shape[0], :].astype(F32)
            row += out.shape[0]


def bit_of(mask_bits, index):
    value = jnp.int32(0)
    for k, bit in enumerate(mask_bits):
        value = value | (((index >> bit) & 1) << k)
    return value


def offset_mask(bits, d):
    return sum(1 << bit for k, bit in enumerate(bits) if d >> k & 1)


def all_sum(info, keep, arrived, groups, core_mask):
    width = keep.shape[1]
    kept, pieces = keep, [arrived]
    for level, bits in enumerate(groups):
        parts = 2 ** len(bits)
        rows = kept.shape[0] // parts
        outs = [((rows, width), F32)] + [((rows, width), BF16)] * (parts - 1)
        made = call(
            lambda *r, level=level, parts=parts, n=len(pieces): reduce_kernel(SIDES + 1 + level, parts, n, *r),
            outs,
            [info, kept, *pieces],
            smem=1,
            scratch=[pltpu.VMEM(kept.shape, F32)],
        )
        kept = made[0]
        pieces = [xor_permute(made[d], offset_mask(bits, d)) for d in range(1, parts)]
    whole = call(
        lambda *r, n=len(pieces): reduce_kernel(0, 1, n, *r),
        [(kept.shape, BF16)],
        [info, kept, *pieces],
        smem=1,
        scratch=[pltpu.VMEM((8, 128), F32)],
    )[0]
    for level in reversed(range(len(groups))):
        bits = groups[level]
        parts = 2 ** len(bits)
        pieces = [whole] + [xor_permute(whole, offset_mask(bits, d)) for d in range(1, parts)]
        whole = call(
            lambda *r, level=level: gather_kernel(SIDES + 1 + level, *r),
            [((whole.shape[0] * parts, width), BF16)],
            [info, *pieces],
            smem=1,
        )[0]
    return whole, xor_permute(whole, core_mask)


def shards(nodes, grad_out, w_query, w_key, w_value, w_out, w_up, w_down, counts, adjacency, expander, pairing, boundary):
    batch, count, width = nodes.shape[2:]
    feats, gout = nodes.reshape(count, width), grad_out.reshape(count, width)
    counts, boundary, pairing = counts[0, 0], boundary[0, 0], pairing[0, 0]
    adjacency, expander = adjacency[0, 0], expander[0, 0]
    rim = boundary.shape[1]
    size_x, size_y = lax.axis_size("sx"), lax.axis_size("sy")
    bits_x, bits_y = size_x.bit_length() - 1, size_y.bit_length() - 1
    merge_y = size_y == 2
    partner = [1 << (bits_x - 1 + bits_y), 1 << (bits_y - 1), 1 << (bits_x - 2 + bits_y)]
    core_bit = bits_y
    rest = [bit for bit in range(bits_x + bits_y) if bit != core_bit]
    groups = [rest[i : i + 2] for i in range(0, len(rest), 2)]
    ix, iy = lax.axis_index("sx"), lax.axis_index("sy")
    index = ix * size_y + iy
    info = jnp.stack(
        [ix > 0, ix < size_x - 1, iy > 0, iy < size_y - 1]
        + [bit_of([core_bit], index)]
        + [bit_of(bits, index) for bits in groups]
    ).astype(jnp.int32)

    rim_count = 2 if merge_y else 4
    prepared = call(
        prepare_kernel,
        [((count + EXTRA, width), BF16)] + [((rim, width), BF16)] * rim_count,
        [counts, feats, boundary],
        smem=1,
    )
    pack, sent = prepared[0], prepared[1:]
    far = [xor_permute(pack, mask) for mask in partner]
    arrived = [from_behind(sent[1], "sx", 1), from_behind(sent[0], "sx", -1)]
    if not merge_y:
        arrived += [from_behind(sent[3], "sy", 1), from_behind(sent[2], "sy", -1)]

    blocks = counts.shape[0]
    size = count // blocks
    keys = (MATCHINGS + 1) * size
    units = w_up.shape[1]
    total_rows = 4 * width + 2 * units
    all_rows = blocks * keys + SIDES * count
    square = (count, width)
    made = call(
        lambda *r: main_kernel(merge_y, *r),
        [(square, BF16), (square, F32), (square, F32)]
        + [(square, BF16)] * MATCHINGS
        + [((rim, width), BF16)] * rim_count
        + [((total_rows // 2, width), F32), ((total_rows // 2, width), BF16)],
        [info, counts, pairing, feats, gout, w_query, w_key, w_value, w_out, w_up, w_down, adjacency, expander, boundary, pack, *far, *arrived],
        smem=3,
        scratch=[
            pltpu.VMEM((total_rows, width), F32),
            pltpu.VMEM((all_rows, width), BF16),
            pltpu.VMEM((all_rows, 2 * width), BF16),
            pltpu.VMEM((blocks, keys, HEADS * size), F32),
            pltpu.VMEM((blocks, keys, HEADS * size), BF16),
            pltpu.VMEM((blocks, keys, HEADS * size), BF16),
            pltpu.VMEM((HEADS * size, width), BF16),
            pltpu.VMEM((HEADS * size, width), BF16),
        ],
        flops=10**10,
        nbytes=8 * 2**20,
    )
    layer_out, grad_hidden, grad_normed = made[:3]
    backs = made[3 : 3 + MATCHINGS]
    rim_back = made[3 + MATCHINGS : 3 + MATCHINGS + rim_count]
    keep, send = made[-2:]

    core_mask = 1 << core_bit
    own, other = all_sum(info, keep, xor_permute(send, core_mask), groups, core_mask)
    returned = [xor_permute(back, mask) for back, mask in zip(backs, partner)]
    rims = [from_behind(rim_back[1], "sx", 1), from_behind(rim_back[0], "sx", -1)]
    if not merge_y:
        rims += [from_behind(rim_back[3], "sy", 1), from_behind(rim_back[2], "sy", -1)]
    grad_nodes = call(
        lambda *r: nodes_kernel(merge_y, *r),
        [(square, BF16)],
        [feats, grad_hidden, grad_normed, boundary, *returned, *rims],
    )[0]
    weights = call(
        lambda *r: final_kernel(SIDES, *r),
        [((width, width), F32)] * 4 + [((width, units), F32), ((units, width), F32)],
        [info, own, other],
        smem=1,
        scratch=[pltpu.VMEM((total_rows, width), BF16)],
    )
    return (layer_out.reshape(nodes.shape), grad_nodes.reshape(nodes.shape), *weights)


def solution(mesh):
    grid = lambda n: P("sx", "sy", *([None] * n))
    return jax.shard_map(
        shards,
        mesh=mesh,
        in_specs=(grid(3), grid(3), P(), P(), P(), P(), P(), P(), grid(1), grid(3), grid(4), grid(2), grid(2)),
        out_specs=(grid(3), grid(3), P(), P(), P(), P(), P(), P()),
        check_vma=False,
    )
```

```python
import math

import jax
import jax.numpy as jnp
from jax import lax
from jax.experimental import pallas as pl
from jax.experimental.pallas import tpu as pltpu
from jax.sharding import PartitionSpec as P

HEADS = 8
HEAD_DIM = 32
EPSILON = 1e-06
NEG_FILL = -1e30
AXES = ("sx", "sy")
EXTRA = 16
MATCHINGS = 3
SIDES = 4
F32 = jnp.float32
BF16 = jnp.bfloat16
GELU_C = math.sqrt(2.0 / math.pi)
GELU_A = 0.044715


def nn(a, b):
    return lax.dot_general(a, b, (((1,), (0,)), ((), ())), preferred_element_type=F32)


def nt(a, b):
    return lax.dot_general(a, b, (((1,), (1,)), ((), ())), preferred_element_type=F32)


def tn(a, b):
    return lax.dot_general(a, b, (((0,), (0,)), ((), ())), preferred_element_type=F32)


def iota(shape, dim):
    return lax.broadcasted_iota(jnp.int32, shape, dim)


def to_bf(mask):
    return jnp.where(mask, 1.0, 0.0).astype(BF16)


def flip(value):
    return jnp.transpose(value.astype(F32), (1, 0))


def pair_permute(value, odd_first):
    count = lax.axis_size("sx")
    pairs = [(i, i + 1) for i in range(1 if odd_first else 0, count - 1, 2)]
    return lax.ppermute(value, "sx", pairs + [(b, a) for a, b in pairs])


def from_behind(block, axis, distance):
    devices = range(lax.axis_size(axis))
    return lax.ppermute(block, axis, [(i - distance, i) for i in devices if i - distance in devices])


def xor_permute(value, mask):
    count = lax.axis_size("sx") * lax.axis_size("sy")
    return lax.ppermute(value, AXES, [(i, i ^ mask) for i in range(count)])


def call(kernel, outs, args, smem=0, hbm=0, scratch=(), limit=48, flops=0, nbytes=0):
    specs = [pl.BlockSpec(memory_space=pltpu.SMEM)] * smem
    specs += [pl.BlockSpec(memory_space=pltpu.HBM)] * hbm
    args = [pltpu.with_memory_space_constraint(a, pltpu.HBM) if smem <= i < smem + hbm else a for i, a in enumerate(args)]
    specs += [pl.BlockSpec(memory_space=pltpu.VMEM)] * (len(args) - smem - hbm)
    scratch = list(scratch)
    if hbm:
        scratch += [pltpu.VMEM(a.shape, a.dtype) for a in args[smem : smem + hbm]] + [pltpu.SemaphoreType.DMA((hbm,))]
    return pl.pallas_call(
        kernel,
        out_shape=[jax.ShapeDtypeStruct(s, d) for s, d in outs],
        in_specs=specs,
        out_specs=[pl.BlockSpec(memory_space=pltpu.VMEM)] * len(outs),
        scratch_shapes=list(scratch),
        compiler_params=pltpu.CompilerParams(vmem_limit_bytes=limit * 2**20),
        cost_estimate=pl.CostEstimate(flops=flops, bytes_accessed=nbytes, transcendentals=0),
    )(*args)


def fetched(sources, buffers, semaphores):
    copies = [pltpu.make_async_copy(a, b, semaphores.at[i]) for i, (a, b) in enumerate(zip(sources, buffers))]
    for copy in copies:
        copy.start()

    def ready(i):
        copies[i].wait()
        return buffers[i]

    return ready


def side_lines(boundary, odd):
    first, second = boundary[0:1, :], boundary[1:2, :]
    return [jnp.where(odd, first, second), jnp.where(odd, second, first), boundary[2:3, :], boundary[3:4, :]]


def prepare_kernel(info, counts, *refs):
    pack, rims = refs[2], refs[3:-3]
    ready = fetched(refs[:2], refs[-3:-1], refs[-1])
    nodes = ready(0)
    count, width = nodes.shape
    blocks = counts.shape[0]
    size = count // blocks
    feats = nodes[...].astype(F32)
    normed = (feats * lax.rsqrt(jnp.mean(feats * feats, axis=1, keepdims=True) + EPSILON)).astype(BF16)
    pack[0:count, :] = normed
    lane = iota((EXTRA, count), 1)
    row = iota((EXTRA, count), 0)
    limit = jnp.zeros((EXTRA, count), jnp.int32)
    for b in range(blocks):
        limit = jnp.where(lane // size == b, counts[b], limit)
    extra = jnp.where((row == 0) & (lane % size < limit), 1.0, 0.0)
    boundary = ready(1)
    rim = boundary.shape[1]
    slots = boundary[...].astype(F32)
    for side in range(SIDES):
        line = slots[side : side + 1, :]
        if count > rim:
            line = jnp.concatenate([line, jnp.zeros((1, count - rim), F32)], axis=1)
        extra = jnp.where(row == side + 1, line, extra)
    pack[count : count + EXTRA, :] = extra.astype(BF16)
    lines = side_lines(boundary, info[SIDES] > 0)
    for side, out in enumerate(rims):
        place = to_bf(iota((count, rim), 0) == lines[side])
        out[...] = tn(place, normed).astype(BF16)


def head_rows(width, shape, dim):
    return iota(shape, dim) // HEAD_DIM


def main_kernel(merge_y, info, counts, pairing, *refs):
    copied = 11
    ready = fetched(refs[:copied], refs[-copied - 1 : -1], refs[-1])
    nodes, boundary, wq, wk, wv, adjacency, expander, wo, wup, wdown, gout = refs[-copied - 1 : -1]
    refs = refs[copied : -copied - 1]
    packs = refs[: MATCHINGS + 1]
    rims = refs[MATCHINGS + 1 : MATCHINGS + 1 + (2 if merge_y else 4)]
    refs = refs[MATCHINGS + 1 + len(rims) :]
    layer_out, grad_hidden_out, grad_normed_out = refs[:3]
    backs = refs[3 : 3 + MATCHINGS]
    rim_outs = refs[3 + MATCHINGS : 3 + MATCHINGS + len(rims)]
    refs = refs[3 + MATCHINGS + len(rims) :]
    keep, send = refs[:2]
    grads, xcat, kvg, probs, pbf, sgrad, qstack, gstack = refs[2:]

    count, width = nodes.shape
    hidden_units = wup.shape[1]
    blocks = counts.shape[0]
    size = count // blocks
    keys = (MATCHINGS + 1) * size
    rim = boundary.shape[1]
    scale = HEAD_DIM**-0.5
    log2e = math.log2(math.e)

    normed = packs[0][0:count, :]
    ready(1)
    lines = side_lines(boundary, info[SIDES] > 0)
    for b in range(blocks):
        xcat[b * keys : b * keys + size, :] = packs[0][b * size : (b + 1) * size, :]
        for m in range(MATCHINGS):
            start = pl.multiple_of(pairing[m, b] * size, size)
            lo = b * keys + (m + 1) * size
            xcat[lo : lo + size, :] = packs[m + 1][pl.ds(start, size), :]
    base = blocks * keys
    places, moves = [], [None, None, None, None]
    for s in range(SIDES):
        here = (iota((count, rim), 0) == lines[s]) & (info[s] > 0)
        places.append(to_bf(here))
    for s in range(SIDES):
        if merge_y and s >= 2:
            other = 3 if s == 2 else 2
            far_slots = packs[2][count : count + EXTRA, :].astype(F32)[other + 1 : other + 2, 0:rim]
            spots = to_bf(iota((count, rim), 0).astype(F32) == far_slots)
            moves[s] = nt(places[s], spots).astype(BF16)
            rows = nn(moves[s], packs[2][0:count, :])
        else:
            rows = nn(places[s], rims[s][...])
        xcat[base + s * count : base + (s + 1) * count, :] = rows.astype(BF16)

    for i in (2, 3, 4):
        ready(i)
    queries = nn(normed, wq[...]).astype(BF16)
    queries_t = flip(queries).astype(BF16)
    wk_t = flip(wk[...]).astype(BF16)
    wv_t = flip(wv[...]).astype(BF16)
    key_rows, key_cols, value_rows, value_cols = [], [], [], []
    for b in range(blocks):
        rows = xcat[b * keys : (b + 1) * keys, :]
        key_rows.append(nn(rows, wk[...]).astype(BF16))
        value_rows.append(nn(rows, wv[...]).astype(BF16))
        key_cols.append(nt(wk_t, rows).astype(BF16))
        value_cols.append(nt(wv_t, rows).astype(BF16))
    rim_keys, rim_values = [], []
    for s in range(SIDES):
        rows = xcat[base + s * count : base + (s + 1) * count, :]
        rim_keys.append(nn(rows, wk[...]).astype(BF16).astype(F32))
        rim_values.append(nn(rows, wv[...]).astype(BF16).astype(F32))

    ready(5)
    ready(6)
    bias = []
    eye = iota((size, size), 0) == iota((size, size), 1)
    for b in range(blocks):
        parts = []
        for g in range(MATCHINGS + 1):
            flags = packs[g][count : count + EXTRA, :].astype(F32)[0:1, :]
            if g == 0:
                real = flags[:, b * size : (b + 1) * size] > 0.5
                mask = ((adjacency[b] == 1) & real) | eye
            else:
                pick = flags[:, 0:size]
                for c in range(1, blocks):
                    pick = jnp.where(pairing[g - 1, b] == c, flags[:, c * size : (c + 1) * size], pick)
                mask = (expander[g - 1, b] == 1) & (pick > 0.5)
            parts.append(flip(jnp.where(mask, 0.0, NEG_FILL)))
        bias.append(jnp.concatenate(parts, axis=0))

    spread = to_bf(head_rows(width, (HEADS, width), 1) == iota((HEADS, width), 0))

    def head_sums(product):
        high = product.astype(BF16)
        low = (product - high.astype(F32)).astype(BF16)
        return nt(spread, high) + nt(spread, low)

    queries_f = queries.astype(F32)
    ones = jnp.ones((HEADS, rim), BF16)
    rim_scores = []
    for s in range(SIDES):
        there = nt(ones, places[s]) > 0.5
        score = head_sums(queries_f * rim_keys[s]) * (scale * log2e)
        rim_scores.append(jnp.where(there, score, NEG_FILL))
    rim_top = jnp.maximum(jnp.maximum(rim_scores[0], rim_scores[1]), jnp.maximum(rim_scores[2], rim_scores[3]))

    row_head = head_rows(width, (width, size), 0)
    tops, sums = [], []
    att_blocks = []
    for b in range(blocks):
        cols = slice(b * size, (b + 1) * size)
        top_rows, inv_rows, att_rows = [], [], []
        own = queries_t[:, cols]
        for first in range(0, HEADS, 2):
            pair = (first, first + 1)
            masked = [jnp.where(row_head == h, own, jnp.zeros_like(own)) for h in pair]
            both = nn(key_rows[b], jnp.concatenate(masked, axis=1))
            for k, h in enumerate(pair):
                score = both[:, k * size : (k + 1) * size] * (scale * log2e) + bias[b]
                top = jnp.maximum(jnp.max(score, axis=0, keepdims=True), rim_top[h : h + 1, cols])
                grown = jnp.exp2(score - top)
                total = jnp.sum(grown, axis=0, keepdims=True)
                for s in range(SIDES):
                    total = total + jnp.exp2(rim_scores[s][h : h + 1, cols] - top)
                inverse = 1.0 / total
                prob = grown * inverse
                at = slice(h * size, (h + 1) * size)
                probs[b, :, at] = prob
                pbf[b, :, at] = prob.astype(BF16)
                top_rows.append(top)
                inv_rows.append(inverse)
            rows = slice(first * HEAD_DIM, (first + 2) * HEAD_DIM)
            wide = nn(value_cols[b][rows, :], pbf[b, :, first * size : (first + 2) * size])
            att_rows += [wide[0:HEAD_DIM, 0:size], wide[HEAD_DIM:, size:]]
        tops.append(jnp.concatenate(top_rows, axis=0))
        sums.append(jnp.concatenate(inv_rows, axis=0))
        att_blocks.append(jnp.concatenate(att_rows, axis=0))
    top_all = jnp.concatenate(tops, axis=1)
    inv_all = jnp.concatenate(sums, axis=1)
    mixed = flip(jnp.concatenate(att_blocks, axis=1))
    rim_probs = [jnp.exp2(rim_scores[s] - top_all) * inv_all for s in range(SIDES)]
    rim_wide = [tn(rim_probs[s].astype(BF16), spread) for s in range(SIDES)]
    for s in range(SIDES):
        mixed = mixed + rim_wide[s] * rim_values[s]
    attended = mixed.astype(BF16)

    slot = iota((count, width), 0)
    limit = jnp.zeros((count, width), jnp.int32)
    for b in range(blocks):
        limit = jnp.where(slot // size == b, counts[b], limit)
    usable = jnp.where(slot % size < limit, 1.0, 0.0)
    for i in (0, 7, 8, 9, 10):
        ready(i)
    feats = nodes[...].astype(F32)
    hidden = feats + nn(attended, wo[...])
    factor = lax.rsqrt(jnp.mean(hidden * hidden, axis=1, keepdims=True) + EPSILON)
    mid = hidden * factor
    normed_mid = mid.astype(BF16)
    pre = nn(normed_mid, wup[...])
    square = pre * pre
    bent = jnp.tanh(GELU_C * pre * (1.0 + GELU_A * square))
    half = 0.5 * (1.0 + bent)
    activ = (pre * half).astype(BF16)
    layer_out[...] = ((hidden + nn(activ, wdown[...])) * usable).astype(BF16)
    upstream = gout[...].astype(F32) * usable
    upstream_bf = upstream.astype(BF16)
    grads[4 * width + hidden_units * 1 : 4 * width + 2 * hidden_units, :] = tn(activ, upstream_bf)
    slope = half + 0.5 * pre * (1.0 - bent * bent) * (GELU_C * (1.0 + 3.0 * GELU_A * square))
    grad_pre = (slope * nt(upstream_bf, wdown[...])).astype(BF16)
    grad_up = tn(normed_mid, grad_pre)
    for part in range(hidden_units // width):
        lo = 4 * width + part * width
        grads[lo : lo + width, :] = grad_up[:, part * width : (part + 1) * width]
    grad_mid = nt(grad_pre, wup[...])
    grad_hidden = upstream + factor * (grad_mid - mid * jnp.mean(grad_mid * mid, axis=1, keepdims=True))
    grad_hidden_out[...] = grad_hidden
    grad_hidden_bf = grad_hidden.astype(BF16)
    grads[3 * width : 4 * width, :] = tn(attended, grad_hidden_bf)
    grad_att = nt(grad_hidden_bf, wo[...]).astype(BF16)
    grad_att_f = grad_att.astype(F32)
    grad_att_t = flip(grad_att).astype(BF16)

    lane_head = head_rows(width, (size, width), 1)
    rim_dots = [head_sums(grad_att_f * rim_values[s]) for s in range(SIDES)]
    rim_inner = rim_probs[0] * rim_dots[0]
    for s in range(1, SIDES):
        rim_inner = rim_inner + rim_probs[s] * rim_dots[s]
    inner_blocks, query_blocks = [], []
    for b in range(blocks):
        cols = slice(b * size, (b + 1) * size)
        inner_rows, query_rows = [], []
        own = grad_att_t[:, cols]
        for first in range(0, HEADS, 2):
            pair = (first, first + 1)
            masked = [jnp.where(row_head == h, own, jnp.zeros_like(own)) for h in pair]
            both = nn(value_rows[b], jnp.concatenate(masked, axis=1))
            for k, h in enumerate(pair):
                dots = both[:, k * size : (k + 1) * size]
                at = slice(h * size, (h + 1) * size)
                prob = probs[b, :, at]
                inner = jnp.sum(prob * dots, axis=0, keepdims=True) + rim_inner[h : h + 1, cols]
                sgrad[b, :, at] = (prob * (dots - inner) * scale).astype(BF16)
                inner_rows.append(inner)
                mine = queries[cols, :]
                qstack[at, :] = jnp.where(lane_head == h, mine, jnp.zeros_like(mine))
                mine = grad_att[cols, :]
                gstack[at, :] = jnp.where(lane_head == h, mine, jnp.zeros_like(mine))
            rows = slice(first * HEAD_DIM, (first + 2) * HEAD_DIM)
            wide = nn(key_cols[b][rows, :], sgrad[b, :, first * size : (first + 2) * size])
            query_rows += [wide[0:HEAD_DIM, 0:size], wide[HEAD_DIM:, size:]]
        inner_blocks.append(jnp.concatenate(inner_rows, axis=0))
        query_blocks.append(jnp.concatenate(query_rows, axis=0))
        span = slice(b * keys, (b + 1) * keys)
        kvg[span, 0:width] = nn(sgrad[b], qstack[...]).astype(BF16)
        kvg[span, width : 2 * width] = nn(pbf[b], gstack[...]).astype(BF16)
    inner_all = jnp.concatenate(inner_blocks, axis=1)
    query_grad = flip(jnp.concatenate(query_blocks, axis=1))
    for s in range(SIDES):
        graded = (rim_probs[s] * (rim_dots[s] - inner_all) * scale).astype(BF16)
        wide = tn(graded, spread)
        query_grad = query_grad + wide * rim_keys[s]
        span = slice(base + s * count, base + (s + 1) * count)
        kvg[span, 0:width] = (wide * queries_f).astype(BF16)
        kvg[span, width : 2 * width] = (rim_wide[s] * grad_att_f).astype(BF16)
    query_total = query_grad.astype(BF16)

    own_rows = []
    extra_back = None
    for s in range(SIDES):
        span = slice(base + s * count, base + (s + 1) * count)
        back = (nn(kvg[span, 0:width], wk_t) + nn(kvg[span, width : 2 * width], wv_t)).astype(BF16)
        if merge_y and s >= 2:
            moved = tn(moves[s], back)
            extra_back = moved if extra_back is None else extra_back + moved
        else:
            rim_outs[s][...] = tn(places[s], back).astype(BF16)
    if merge_y:
        grads[0:count, :] = extra_back
    for b in range(blocks):
        span = slice(b * keys, (b + 1) * keys)
        back = nn(kvg[span, 0:width], wk_t) + nn(kvg[span, width : 2 * width], wv_t)
        own_rows.append(back[0:size])
        for m in range(MATCHINGS):
            start = pl.multiple_of(pairing[m, b] * size, size)
            piece = back[(m + 1) * size : (m + 2) * size]
            if merge_y and m == 1:
                piece = piece + grads[pl.ds(start, size), :]
            backs[m][pl.ds(start, size), :] = piece.astype(BF16)
    grad_normed_out[...] = nt(query_total, wq[...]) + jnp.concatenate(own_rows, axis=0)

    grads[0:width, :] = tn(normed, query_total)
    both = tn(xcat[...], kvg[...])
    grads[width : 2 * width, :] = both[:, 0:width]
    grads[2 * width : 3 * width, :] = both[:, width : 2 * width]

    half_rows = grads.shape[0] // 2
    mine = info[SIDES]
    keep[...] = grads[pl.ds(pl.multiple_of(mine * half_rows, half_rows), half_rows), :]
    send[...] = grads[pl.ds(pl.multiple_of((1 - mine) * half_rows, half_rows), half_rows), :].astype(BF16)


def nodes_kernel(info, *refs):
    ready = fetched(refs[:2], refs[-3:-1], refs[-1])
    grad_hidden, grad_normed = refs[2:4]
    backs, rims, out = refs[4 : 4 + MATCHINGS], refs[4 + MATCHINGS : -4], refs[-4]
    nodes, boundary = ready(0), ready(1)
    lines = side_lines(boundary, info[SIDES] > 0)
    count = nodes.shape[0]
    rim = boundary.shape[1]
    cot = grad_normed[...]
    for back in backs:
        cot = cot + back[...].astype(F32)
    for s, rows in enumerate(rims):
        place = to_bf(iota((count, rim), 0) == lines[s])
        cot = cot + nn(place, rows[...])
    feats = nodes[...].astype(F32)
    factor = lax.rsqrt(jnp.mean(feats * feats, axis=1, keepdims=True) + EPSILON)
    normed = feats * factor
    out[...] = (grad_hidden[...] + factor * (cot - normed * jnp.mean(cot * normed, axis=1, keepdims=True))).astype(BF16)


def reduce_kernel(place, parts, kept_rows, *refs):
    info, kept = refs[0], refs[1]
    received = refs[2 : 2 + kept_rows]
    outs = refs[2 + kept_rows : -1]
    total_ref = refs[-1]
    total = kept[...].astype(F32)
    for piece in received:
        total = total + piece[...].astype(F32)
    if parts == 1:
        outs[0][...] = total.astype(BF16)
        return
    total_ref[...] = total
    rows = total.shape[0] // parts
    mine = info[place]
    outs[0][...] = total_ref[pl.ds(pl.multiple_of(mine * rows, rows), rows), :]
    for d in range(1, parts):
        outs[d][...] = total_ref[pl.ds(pl.multiple_of((mine ^ d) * rows, rows), rows), :].astype(BF16)


def gather_kernel(place, *refs):
    info, pieces, out = refs[0], refs[1:-1], refs[-1]
    mine = info[place]
    rows = pieces[0].shape[0]
    for d, piece in enumerate(pieces):
        out[pl.ds(pl.multiple_of((mine ^ d) * rows, rows), rows), :] = piece[...]


def final_kernel(place, info, own, other, *refs):
    outs, full = refs[:-1], refs[-1]
    rows = own.shape[0]
    mine = info[place]
    full[pl.ds(pl.multiple_of(mine * rows, rows), rows), :] = own[...]
    full[pl.ds(pl.multiple_of((1 - mine) * rows, rows), rows), :] = other[...]
    width = full.shape[1]
    row = 0
    for out in outs:
        for part in range(out.shape[1] // width):
            out[:, part * width : (part + 1) * width] = full[row : row + out.shape[0], :].astype(F32)
            row += out.shape[0]


def bit_of(mask_bits, index):
    value = jnp.int32(0)
    for k, bit in enumerate(mask_bits):
        value = value | (((index >> bit) & 1) << k)
    return value


def offset_mask(bits, d):
    return sum(1 << bit for k, bit in enumerate(bits) if d >> k & 1)


def all_sum(info, keep, arrived, groups, core_mask, riders):
    width = keep.shape[1]
    kept, pieces = keep, [arrived]
    riders, rode = list(riders), []

    def exchange(values, masks, several):
        batch = riders[:several]
        del riders[:several]
        if not batch:
            return [xor_permute(v, m) for v, m in zip(values, masks)]
        tied = lax.optimization_barrier((tuple(values), tuple(r[0] for r in batch)))
        moved = [xor_permute(v, m) for v, m in zip(tied[0], masks)]
        taken = [r[1](v) for r, v in zip(batch, tied[1])]
        moved, taken = lax.optimization_barrier((tuple(moved), tuple(taken)))
        rode.extend(taken)
        return list(moved)

    for level, bits in enumerate(groups):
        parts = 2 ** len(bits)
        rows = kept.shape[0] // parts
        outs = [((rows, width), F32)] + [((rows, width), BF16)] * (parts - 1)
        made = call(
            lambda *r, level=level, parts=parts, n=len(pieces): reduce_kernel(SIDES + 1 + level, parts, n, *r),
            outs,
            [info, kept, *pieces],
            smem=1,
            scratch=[pltpu.VMEM(kept.shape, F32)],
        )
        kept = made[0]
        pieces = exchange(made[1:], [offset_mask(bits, d) for d in range(1, parts)], 2)
    whole = call(
        lambda *r, n=len(pieces): reduce_kernel(0, 1, n, *r),
        [(kept.shape, BF16)],
        [info, kept, *pieces],
        smem=1,
        scratch=[pltpu.VMEM((8, 128), F32)],
    )[0]
    for level in reversed(range(len(groups))):
        bits = groups[level]
        parts = 2 ** len(bits)
        masks = [offset_mask(bits, d) for d in range(1, parts)]
        pieces = [whole] + exchange([whole] * len(masks), masks, 2 if level else len(riders))
        whole = call(
            lambda *r, level=level: gather_kernel(SIDES + 1 + level, *r),
            [((whole.shape[0] * parts, width), BF16)],
            [info, *pieces],
            smem=1,
        )[0]
    return whole, xor_permute(whole, core_mask), rode


def shards(nodes, grad_out, w_query, w_key, w_value, w_out, w_up, w_down, counts, adjacency, expander, pairing, boundary):
    batch, count, width = nodes.shape[2:]
    feats, gout = nodes.reshape(count, width), grad_out.reshape(count, width)
    counts, boundary, pairing = counts[0, 0], boundary[0, 0], pairing[0, 0]
    adjacency, expander = adjacency[0, 0], expander[0, 0]
    rim = boundary.shape[1]
    size_x, size_y = lax.axis_size("sx"), lax.axis_size("sy")
    bits_x, bits_y = size_x.bit_length() - 1, size_y.bit_length() - 1
    merge_y = size_y == 2
    partner = [1 << (bits_x - 1 + bits_y), 1 << (bits_y - 1), 1 << (bits_x - 2 + bits_y)]
    core_bit = bits_y
    rest = [bit for bit in range(bits_x + bits_y) if bit != core_bit]
    groups = [rest[i : i + 2] for i in range(0, len(rest), 2)]
    ix, iy = lax.axis_index("sx"), lax.axis_index("sy")
    index = ix * size_y + iy
    info = jnp.stack(
        [ix >= 0, jnp.where(ix % 2 == 0, ix > 0, ix < size_x - 1), iy > 0, iy < size_y - 1]
        + [bit_of([core_bit], index)]
        + [bit_of(bits, index) for bits in groups]
    ).astype(jnp.int32)

    rim_count = 2 if merge_y else 4
    prepared = call(
        prepare_kernel,
        [((count + EXTRA, width), BF16)] + [((rim, width), BF16)] * rim_count,
        [info, counts, feats, boundary],
        smem=2,
        hbm=2,
    )
    pack, sent = prepared[0], prepared[1:]
    far = [xor_permute(pack, mask) for mask in partner]
    arrived = [pair_permute(sent[0], False), pair_permute(sent[1], True)]
    if not merge_y:
        arrived += [from_behind(sent[3], "sy", 1), from_behind(sent[2], "sy", -1)]

    blocks = counts.shape[0]
    size = count // blocks
    keys = (MATCHINGS + 1) * size
    units = w_up.shape[1]
    total_rows = 4 * width + 2 * units
    all_rows = blocks * keys + SIDES * count
    square = (count, width)
    made = call(
        lambda *r: main_kernel(merge_y, *r),
        [(square, BF16), (square, F32), (square, F32)]
        + [(square, BF16)] * MATCHINGS
        + [((rim, width), BF16)] * rim_count
        + [((total_rows // 2, width), F32), ((total_rows // 2, width), BF16)],
        [info, counts, pairing, feats, boundary, w_query, w_key, w_value, adjacency, expander, w_out, w_up, w_down, gout, pack, *far, *arrived],
        smem=3,
        hbm=11,
        scratch=[
            pltpu.VMEM((total_rows, width), F32),
            pltpu.VMEM((all_rows, width), BF16),
            pltpu.VMEM((all_rows, 2 * width), BF16),
            pltpu.VMEM((blocks, keys, HEADS * size), F32),
            pltpu.VMEM((blocks, keys, HEADS * size), BF16),
            pltpu.VMEM((blocks, keys, HEADS * size), BF16),
            pltpu.VMEM((HEADS * size, width), BF16),
            pltpu.VMEM((HEADS * size, width), BF16),
        ],
        flops=10**10,
        nbytes=8 * 2**20,
    )
    layer_out, grad_hidden, grad_normed = made[:3]
    backs = made[3 : 3 + MATCHINGS]
    rim_back = made[3 + MATCHINGS : 3 + MATCHINGS + rim_count]
    keep, send = made[-2:]

    core_mask = 1 << core_bit
    riders = [(back, lambda v, mask=mask: xor_permute(v, mask)) for back, mask in zip(backs, partner)]
    riders += [(rim_back[0], lambda v: pair_permute(v, False)), (rim_back[1], lambda v: pair_permute(v, True))]
    if not merge_y:
        riders += [(rim_back[3], lambda v: from_behind(v, "sy", 1)), (rim_back[2], lambda v: from_behind(v, "sy", -1))]
    own, other, rode = all_sum(info, keep, xor_permute(send, core_mask), groups, core_mask, riders)
    returned, rims = rode[:MATCHINGS], rode[MATCHINGS:]
    grad_nodes = call(
        nodes_kernel,
        [(square, BF16)],
        [info, feats, boundary, grad_hidden, grad_normed, *returned, *rims],
        smem=1,
        hbm=2,
    )[0]
    weights = call(
        lambda *r: final_kernel(SIDES, *r),
        [((width, width), F32)] * 4 + [((width, units), F32), ((units, width), F32)],
        [info, own, other],
        smem=1,
        scratch=[pltpu.VMEM((total_rows, width), BF16)],
    )
    return (layer_out.reshape(nodes.shape), grad_nodes.reshape(nodes.shape), *weights)


def solution(mesh):
    grid = lambda n: P("sx", "sy", *([None] * n))
    return jax.shard_map(
        shards,
        mesh=mesh,
        in_specs=(grid(3), grid(3), P(), P(), P(), P(), P(), P(), grid(1), grid(3), grid(4), grid(2), grid(2)),
        out_specs=(grid(3), grid(3), P(), P(), P(), P(), P(), P()),
        check_vma=False,
    )
```

```python
import math

import jax
import jax.numpy as jnp
from jax import lax
from jax.experimental import pallas as pl
from jax.experimental.pallas import tpu as pltpu
from jax.sharding import PartitionSpec as P

HEADS = 8
HEAD_DIM = 32
EPSILON = 1e-06
NEG_FILL = -1e30
AXES = ("sx", "sy")
EXTRA = 16
MATCHINGS = 3
SIDES = 4
F32 = jnp.float32
BF16 = jnp.bfloat16
GELU_C = math.sqrt(2.0 / math.pi)
GELU_A = 0.044715


def nn(a, b):
    return lax.dot_general(a, b, (((1,), (0,)), ((), ())), preferred_element_type=F32)


def nt(a, b):
    return lax.dot_general(a, b, (((1,), (1,)), ((), ())), preferred_element_type=F32)


def tn(a, b):
    return lax.dot_general(a, b, (((0,), (0,)), ((), ())), preferred_element_type=F32)


def iota(shape, dim):
    return lax.broadcasted_iota(jnp.int32, shape, dim)


def to_bf(mask):
    return jnp.where(mask, 1.0, 0.0).astype(BF16)


def flip(value):
    return jnp.transpose(value.astype(F32), (1, 0))


def pair_permute(value, odd_first):
    count = lax.axis_size("sx")
    pairs = [(i, i + 1) for i in range(1 if odd_first else 0, count - 1, 2)]
    return lax.ppermute(value, "sx", pairs + [(b, a) for a, b in pairs])


def from_behind(block, axis, distance):
    devices = range(lax.axis_size(axis))
    return lax.ppermute(block, axis, [(i - distance, i) for i in devices if i - distance in devices])


def xor_permute(value, mask):
    count = lax.axis_size("sx") * lax.axis_size("sy")
    return lax.ppermute(value, AXES, [(i, i ^ mask) for i in range(count)])


def call(kernel, outs, args, smem=0, hbm=0, scratch=(), limit=16, flops=0, nbytes=0):
    specs = [pl.BlockSpec(memory_space=pltpu.SMEM)] * smem
    specs += [pl.BlockSpec(memory_space=pltpu.HBM)] * hbm
    args = [pltpu.with_memory_space_constraint(a, pltpu.HBM) if smem <= i < smem + hbm else a for i, a in enumerate(args)]
    specs += [pl.BlockSpec(memory_space=pltpu.VMEM)] * (len(args) - smem - hbm)
    scratch = list(scratch)
    if hbm:
        scratch += [(pltpu.SMEM if a.ndim == 1 else pltpu.VMEM)(a.shape, a.dtype) for a in args[smem : smem + hbm]] + [pltpu.SemaphoreType.DMA((hbm,))]
    return pl.pallas_call(
        kernel,
        out_shape=[jax.ShapeDtypeStruct(s, d) for s, d in outs],
        in_specs=specs,
        out_specs=[pl.BlockSpec(memory_space=pltpu.VMEM)] * len(outs),
        scratch_shapes=list(scratch),
        compiler_params=pltpu.CompilerParams(vmem_limit_bytes=limit * 2**20),
        cost_estimate=pl.CostEstimate(flops=flops, bytes_accessed=nbytes, transcendentals=0),
    )(*args)


def fetched(sources, buffers, semaphores):
    copies = [pltpu.make_async_copy(a, b, semaphores.at[i]) for i, (a, b) in enumerate(zip(sources, buffers))]
    for copy in copies:
        copy.start()

    def ready(i):
        copies[i].wait()
        return buffers[i]

    return ready


def side_lines(boundary, odd):
    first, second = boundary[0:1, :], boundary[1:2, :]
    return [jnp.where(odd, first, second), jnp.where(odd, second, first), boundary[2:3, :], boundary[3:4, :]]


def prepare_kernel(info, *refs):
    pack, rims = refs[3], refs[4:-4]
    ready = fetched(refs[:3], refs[-4:-1], refs[-1])
    counts = ready(2)
    nodes = ready(0)
    count, width = nodes.shape
    blocks = counts.shape[0]
    size = count // blocks
    feats = nodes[...].astype(F32)
    normed = (feats * lax.rsqrt(jnp.mean(feats * feats, axis=1, keepdims=True) + EPSILON)).astype(BF16)
    pack[0:count, :] = normed
    lane = iota((EXTRA, count), 1)
    row = iota((EXTRA, count), 0)
    limit = jnp.zeros((EXTRA, count), jnp.int32)
    for b in range(blocks):
        limit = jnp.where(lane // size == b, counts[b], limit)
    extra = jnp.where((row == 0) & (lane % size < limit), 1.0, 0.0)
    boundary = ready(1)
    rim = boundary.shape[1]
    slots = boundary[...].astype(F32)
    for side in range(SIDES):
        line = slots[side : side + 1, :]
        if count > rim:
            line = jnp.concatenate([line, jnp.zeros((1, count - rim), F32)], axis=1)
        extra = jnp.where(row == side + 1, line, extra)
    pack[count : count + EXTRA, :] = extra.astype(BF16)
    lines = side_lines(boundary, info[SIDES] > 0)
    for side, out in enumerate(rims):
        place = to_bf(iota((count, rim), 0) == lines[side])
        out[...] = tn(place, normed).astype(BF16)


def head_rows(shape, dim):
    return iota(shape, dim) // HEAD_DIM


def early_kernel(info, *refs):
    copied = 6
    ready = fetched(refs[:copied], refs[-copied - 1 : -1], refs[-1])
    boundary, wq, wk, wv, adjacency, expander = refs[-copied - 1 : -1]
    pack = refs[copied]
    refs = refs[copied + 1 : -copied - 1]
    squares, places, there = refs
    count, width = squares.shape[1:]
    blocks, size = adjacency.shape[0], adjacency.shape[2]
    rim = places.shape[2]
    normed = pack[0:count, :]
    ready(0)
    lines = side_lines(boundary, info[SIDES] > 0)
    ones = jnp.ones((HEADS, rim), BF16)
    for s in range(SIDES):
        place = to_bf((iota((count, rim), 0) == lines[s]) & (info[s] > 0))
        places[s] = place
        there[s] = nt(ones, place)
    ready(1)
    queries = nn(normed, wq[...]).astype(BF16)
    squares[0] = queries
    squares[9] = flip(queries).astype(BF16)
    for k, weight in enumerate((wk, wv)):
        ready(2 + k)
        squares[1 + k] = weight[...]
        turned = flip(weight[...]).astype(BF16)
        squares[3 + k] = turned
        squares[5 + k] = nn(normed, weight[...]).astype(BF16)
        squares[7 + k] = nt(turned, normed).astype(BF16)
    ready(4)
    ready(5)
    flags = pack[count : count + EXTRA, :].astype(F32)[0:1, :]
    eye = iota((size, size), 0) == iota((size, size), 1)
    for b in range(blocks):
        real = flags[:, b * size : (b + 1) * size] > 0.5
        mask = ((adjacency[b] == 1) & real) | eye
        cols = slice(b * size, (b + 1) * size)
        squares[10, 0:size, cols] = flip(jnp.where(mask, 0.0, NEG_FILL)).astype(BF16)
        for m in range(MATCHINGS):
            lo = (m + 1) * size
            squares[10 + lo // count, lo % count : lo % count + size, cols] = flip(jnp.where(expander[m, b] == 1, 0.0, NEG_FILL)).astype(BF16)


def main_kernel(merge_y, info, counts, pairing, *refs):
    copied = 5
    ready = fetched(refs[:copied], refs[-copied - 1 : -1], refs[-1])
    nodes, wo, wup, wdown, gout = refs[-copied - 1 : -1]
    refs = refs[copied : -copied - 1]
    squares, places, there = refs[:3]
    refs = refs[3:]
    weights, weights_t, own_rows, own_cols = (squares.at[i : i + 2] for i in (1, 3, 5, 7))
    packs = refs[: MATCHINGS + 1]
    rims = refs[MATCHINGS + 1 : MATCHINGS + 1 + (2 if merge_y else 4)]
    refs = refs[MATCHINGS + 1 + len(rims) :]
    keep, send, kvg, moves, query_out, hidden_out, activ_out, grad_hidden_out = refs[:8]
    grads, xcat, probs, pbf, sgrad, qstack, gstack, real_cols = refs[8:]

    count, width = nodes.shape
    hidden_units = wup.shape[1]
    blocks = counts.shape[0]
    size = count // blocks
    keys = (MATCHINGS + 1) * size
    rim = places.shape[2]
    scale = HEAD_DIM**-0.5
    log2e = math.log2(math.e)

    normed = packs[0][0:count, :]
    bias = []
    for m in range(MATCHINGS):
        real_cols[m] = flip(packs[m + 1][count : count + EXTRA, :])
    for b in range(blocks):
        xcat[b * keys : b * keys + size, :] = packs[0][b * size : (b + 1) * size, :]
        for m in range(MATCHINGS):
            start = pl.multiple_of(pairing[m, b] * size, size)
            lo = b * keys + (m + 1) * size
            xcat[lo : lo + size, :] = packs[m + 1][pl.ds(start, size), :]
            real = real_cols[m, pl.ds(start, size), :][:, 0:1]
            at = (m + 1) * size
            kept = squares[10 + at // count, at % count : at % count + size, b * size : (b + 1) * size]
            bias.append(kept.astype(F32) + jnp.where(real > 0.5, 0.0, NEG_FILL))
    base = blocks * keys
    for s in range(SIDES):
        if merge_y and s >= 2:
            other = 3 if s == 2 else 2
            far_slots = packs[2][count : count + EXTRA, :].astype(F32)[other + 1 : other + 2, 0:rim]
            spots = to_bf(iota((count, rim), 0).astype(F32) == far_slots)
            move = nt(places[s], spots).astype(BF16)
            moves[s - 2] = move
            rows = nn(move, packs[2][0:count, :])
        else:
            rows = nn(places[s], rims[s][...])
        xcat[base + s * count : base + (s + 1) * count, :] = rows.astype(BF16)

    queries = squares[0]
    key_rows, key_cols, value_rows, value_cols = [], [], [], []
    for b in range(blocks):
        rows = xcat[b * keys + size : (b + 1) * keys, :]
        own = slice(b * size, (b + 1) * size)
        key_rows.append(jnp.concatenate([own_rows[0, own, :], nn(rows, weights[0]).astype(BF16)], axis=0))
        value_rows.append(jnp.concatenate([own_rows[1, own, :], nn(rows, weights[1]).astype(BF16)], axis=0))
        key_cols.append(jnp.concatenate([own_cols[0, :, own], nt(weights_t[0], rows).astype(BF16)], axis=1))
        value_cols.append(jnp.concatenate([own_cols[1, :, own], nt(weights_t[1], rows).astype(BF16)], axis=1))
    rim_keys, rim_values = [], []
    for s in range(SIDES):
        rows = xcat[base + s * count : base + (s + 1) * count, :]
        rim_keys.append(nn(rows, weights[0]).astype(BF16).astype(F32))
        rim_values.append(nn(rows, weights[1]).astype(BF16).astype(F32))
    bias = [
        jnp.concatenate([squares[10, 0:size, b * size : (b + 1) * size].astype(F32)] + bias[b * MATCHINGS : (b + 1) * MATCHINGS], axis=0)
        for b in range(blocks)
    ]

    spread = to_bf(head_rows((HEADS, width), 1) == iota((HEADS, width), 0))

    def head_sums(product):
        high = product.astype(BF16)
        low = (product - high.astype(F32)).astype(BF16)
        return nt(spread, high) + nt(spread, low)

    queries_f = queries.astype(F32)
    rim_scores = []
    for s in range(SIDES):
        score = head_sums(queries_f * rim_keys[s]) * (scale * log2e)
        rim_scores.append(jnp.where(there[s] > 0.5, score, NEG_FILL))
    rim_top = jnp.maximum(jnp.maximum(rim_scores[0], rim_scores[1]), jnp.maximum(rim_scores[2], rim_scores[3]))

    row_head = head_rows((width, size), 0)
    tops, sums = [], []
    att_blocks = []
    for b in range(blocks):
        cols = slice(b * size, (b + 1) * size)
        top_rows, inv_rows, att_rows = [], [], []
        own = squares[9, :, cols]
        for first in range(0, HEADS, 2):
            pair = (first, first + 1)
            masked = [jnp.where(row_head == h, own, jnp.zeros_like(own)) for h in pair]
            both = nn(key_rows[b], jnp.concatenate(masked, axis=1))
            for k, h in enumerate(pair):
                score = both[:, k * size : (k + 1) * size] * (scale * log2e) + bias[b]
                top = jnp.maximum(jnp.max(score, axis=0, keepdims=True), rim_top[h : h + 1, cols])
                grown = jnp.exp2(score - top)
                total = jnp.sum(grown, axis=0, keepdims=True)
                for s in range(SIDES):
                    total = total + jnp.exp2(rim_scores[s][h : h + 1, cols] - top)
                inverse = 1.0 / total
                prob = grown * inverse
                at = slice(h * size, (h + 1) * size)
                probs[b, :, at] = prob
                pbf[b, :, at] = prob.astype(BF16)
                top_rows.append(top)
                inv_rows.append(inverse)
            rows = slice(first * HEAD_DIM, (first + 2) * HEAD_DIM)
            wide = nn(value_cols[b][rows, :], pbf[b, :, first * size : (first + 2) * size])
            att_rows += [wide[0:HEAD_DIM, 0:size], wide[HEAD_DIM:, size:]]
        tops.append(jnp.concatenate(top_rows, axis=0))
        sums.append(jnp.concatenate(inv_rows, axis=0))
        att_blocks.append(jnp.concatenate(att_rows, axis=0))
    top_all = jnp.concatenate(tops, axis=1)
    inv_all = jnp.concatenate(sums, axis=1)
    mixed = flip(jnp.concatenate(att_blocks, axis=1))
    rim_probs = [jnp.exp2(rim_scores[s] - top_all) * inv_all for s in range(SIDES)]
    rim_wide = [tn(rim_probs[s].astype(BF16), spread) for s in range(SIDES)]
    for s in range(SIDES):
        mixed = mixed + rim_wide[s] * rim_values[s]
    attended = mixed.astype(BF16)

    slot = iota((count, width), 0)
    limit = jnp.zeros((count, width), jnp.int32)
    for b in range(blocks):
        limit = jnp.where(slot // size == b, counts[b], limit)
    usable = jnp.where(slot % size < limit, 1.0, 0.0)
    for i in range(copied):
        ready(i)
    feats = nodes[...].astype(F32)
    hidden = feats + nn(attended, wo[...])
    factor = lax.rsqrt(jnp.mean(hidden * hidden, axis=1, keepdims=True) + EPSILON)
    mid = hidden * factor
    normed_mid = mid.astype(BF16)
    pre = nn(normed_mid, wup[...])
    square = pre * pre
    bent = jnp.tanh(GELU_C * pre * (1.0 + GELU_A * square))
    half = 0.5 * (1.0 + bent)
    activ = (pre * half).astype(BF16)
    hidden_out[...] = hidden
    activ_out[...] = activ
    upstream = gout[...].astype(F32) * usable
    upstream_bf = upstream.astype(BF16)
    grads[4 * width + hidden_units * 1 : 4 * width + 2 * hidden_units, :] = tn(activ, upstream_bf)
    slope = half + 0.5 * pre * (1.0 - bent * bent) * (GELU_C * (1.0 + 3.0 * GELU_A * square))
    grad_pre = (slope * nt(upstream_bf, wdown[...])).astype(BF16)
    grad_up = tn(normed_mid, grad_pre)
    for part in range(hidden_units // width):
        lo = 4 * width + part * width
        grads[lo : lo + width, :] = grad_up[:, part * width : (part + 1) * width]
    grad_mid = nt(grad_pre, wup[...])
    grad_hidden = upstream + factor * (grad_mid - mid * jnp.mean(grad_mid * mid, axis=1, keepdims=True))
    grad_hidden_out[...] = grad_hidden
    grad_hidden_bf = grad_hidden.astype(BF16)
    grads[3 * width : 4 * width, :] = tn(attended, grad_hidden_bf)
    grad_att = nt(grad_hidden_bf, wo[...]).astype(BF16)
    grad_att_f = grad_att.astype(F32)
    grad_att_t = flip(grad_att).astype(BF16)

    lane_head = head_rows((size, width), 1)
    rim_dots = [head_sums(grad_att_f * rim_values[s]) for s in range(SIDES)]
    rim_inner = rim_probs[0] * rim_dots[0]
    for s in range(1, SIDES):
        rim_inner = rim_inner + rim_probs[s] * rim_dots[s]
    inner_blocks, query_blocks = [], []
    for b in range(blocks):
        cols = slice(b * size, (b + 1) * size)
        inner_rows, query_rows = [], []
        own = grad_att_t[:, cols]
        own = grad_att_t[:, cols]
        for first in range(0, HEADS, 2):
            pair = (first, first + 1)
            masked = [jnp.where(row_head == h, own, jnp.zeros_like(own)) for h in pair]
            both = nn(value_rows[b], jnp.concatenate(masked, axis=1))
            for k, h in enumerate(pair):
                dots = both[:, k * size : (k + 1) * size]
                at = slice(h * size, (h + 1) * size)
                prob = probs[b, :, at]
                inner = jnp.sum(prob * dots, axis=0, keepdims=True) + rim_inner[h : h + 1, cols]
                sgrad[b, :, at] = (prob * (dots - inner) * scale).astype(BF16)
                inner_rows.append(inner)
                mine = queries[cols, :]
                qstack[at, :] = jnp.where(lane_head == h, mine, jnp.zeros_like(mine))
                mine = grad_att[cols, :]
                gstack[at, :] = jnp.where(lane_head == h, mine, jnp.zeros_like(mine))
            rows = slice(first * HEAD_DIM, (first + 2) * HEAD_DIM)
            wide = nn(key_cols[b][rows, :], sgrad[b, :, first * size : (first + 2) * size])
            query_rows += [wide[0:HEAD_DIM, 0:size], wide[HEAD_DIM:, size:]]
        inner_blocks.append(jnp.concatenate(inner_rows, axis=0))
        query_blocks.append(jnp.concatenate(query_rows, axis=0))
        span = slice(b * keys, (b + 1) * keys)
        kvg[span, 0:width] = nn(sgrad[b], qstack[...]).astype(BF16)
        kvg[span, width : 2 * width] = nn(pbf[b], gstack[...]).astype(BF16)
    inner_all = jnp.concatenate(inner_blocks, axis=1)
    query_grad = flip(jnp.concatenate(query_blocks, axis=1))
    for s in range(SIDES):
        graded = (rim_probs[s] * (rim_dots[s] - inner_all) * scale).astype(BF16)
        wide = tn(graded, spread)
        query_grad = query_grad + wide * rim_keys[s]
        span = slice(base + s * count, base + (s + 1) * count)
        kvg[span, 0:width] = (wide * queries_f).astype(BF16)
        kvg[span, width : 2 * width] = (rim_wide[s] * grad_att_f).astype(BF16)
    query_total = query_grad.astype(BF16)

    query_out[...] = query_total
    grads[0:width, :] = tn(normed, query_total)
    both = tn(xcat[...], kvg[...])
    grads[width : 2 * width, :] = both[:, 0:width]
    grads[2 * width : 3 * width, :] = both[:, width : 2 * width]

    half_rows = grads.shape[0] // 2
    mine = info[SIDES]
    keep[...] = grads[pl.ds(pl.multiple_of(mine * half_rows, half_rows), half_rows), :]
    send[...] = grads[pl.ds(pl.multiple_of((1 - mine) * half_rows, half_rows), half_rows), :].astype(BF16)


def back_kernel(merge_y, counts, pairing, *refs):
    copied = 2
    ready = fetched(refs[:copied], refs[-copied - 1 : -1], refs[-1])
    wq, wdown = refs[-copied - 1 : -1]
    refs = refs[copied : -copied - 1]
    kvg, moves, query_total, hidden, activ, places, squares = refs[:7]
    layer_out, grad_normed_out, *rest = refs[7:]
    backs, rim_outs, extra = rest[:MATCHINGS], rest[MATCHINGS:-1], rest[-1]
    count, width = hidden.shape
    blocks = counts.shape[0]
    size = count // blocks
    keys = (MATCHINGS + 1) * size
    base = blocks * keys
    wk_t, wv_t = squares[3], squares[4]
    own_rows = []
    extra_back = None
    for s in range(SIDES):
        span = slice(base + s * count, base + (s + 1) * count)
        back = (nn(kvg[span, 0:width], wk_t) + nn(kvg[span, width : 2 * width], wv_t)).astype(BF16)
        if merge_y and s >= 2:
            moved = tn(moves[s - 2], back)
            extra_back = moved if extra_back is None else extra_back + moved
        else:
            rim_outs[s][...] = tn(places[s], back).astype(BF16)
    if merge_y:
        extra[...] = extra_back
    for b in range(blocks):
        span = slice(b * keys, (b + 1) * keys)
        back = nn(kvg[span, 0:width], wk_t) + nn(kvg[span, width : 2 * width], wv_t)
        own_rows.append(back[0:size])
        for m in range(MATCHINGS):
            start = pl.multiple_of(pairing[m, b] * size, size)
            piece = back[(m + 1) * size : (m + 2) * size]
            if merge_y and m == 1:
                piece = piece + extra[pl.ds(start, size), :]
            backs[m][pl.ds(start, size), :] = piece.astype(BF16)
    ready(0)
    grad_normed_out[...] = nt(query_total[...], wq[...]) + jnp.concatenate(own_rows, axis=0)
    slot = iota((count, width), 0)
    limit = jnp.zeros((count, width), jnp.int32)
    for b in range(blocks):
        limit = jnp.where(slot // size == b, counts[b], limit)
    usable = jnp.where(slot % size < limit, 1.0, 0.0)
    ready(1)
    layer_out[...] = ((hidden[...] + nn(activ[...], wdown[...])) * usable).astype(BF16)


def nodes_kernel(info, *refs):
    ready = fetched(refs[:2], refs[-3:-1], refs[-1])
    grad_hidden, grad_normed = refs[2:4]
    backs, rims, out = refs[4 : 4 + MATCHINGS], refs[4 + MATCHINGS : -4], refs[-4]
    nodes, boundary = ready(0), ready(1)
    lines = side_lines(boundary, info[SIDES] > 0)
    count = nodes.shape[0]
    rim = boundary.shape[1]
    cot = grad_normed[...]
    for back in backs:
        cot = cot + back[back.shape[0] - count :, :].astype(F32)
    for s, rows in enumerate(rims):
        place = to_bf(iota((count, rim), 0) == lines[s])
        cot = cot + nn(place, rows[...])
    feats = nodes[...].astype(F32)
    factor = lax.rsqrt(jnp.mean(feats * feats, axis=1, keepdims=True) + EPSILON)
    normed = feats * factor
    out[...] = (grad_hidden[...] + factor * (cot - normed * jnp.mean(cot * normed, axis=1, keepdims=True))).astype(BF16)


def lay_out(outs, values, riders):
    for out, value, rider in zip(outs, values, riders):
        out[0 : value.shape[0], :] = value
        if rider is not None:
            out[value.shape[0] :, :] = rider[...]


def reduce_kernel(place, parts, kept_rows, riding, *refs):
    info, kept = refs[0], refs[1]
    received = refs[2 : 2 + kept_rows]
    count = sum(riding)
    riders = iter(refs[2 + kept_rows : 2 + kept_rows + count])
    riders = [next(riders) if r else None for r in riding]
    outs = refs[2 + kept_rows + count : -1]
    total_ref = refs[-1]
    rows = kept.shape[0]
    total = kept[...].astype(F32)
    for piece in received:
        total = total + piece[0:rows, :].astype(F32)
    if parts == 1:
        lay_out(outs, [total.astype(BF16)] * len(outs), riders)
        return
    total_ref[...] = total
    rows = rows // parts
    mine = info[place]
    outs[0][...] = total_ref[pl.ds(pl.multiple_of(mine * rows, rows), rows), :]
    pieces = [total_ref[pl.ds(pl.multiple_of((mine ^ d) * rows, rows), rows), :].astype(BF16) for d in range(1, parts)]
    lay_out(outs[1:], pieces, riders)


def gather_kernel(place, rows, parts, riding, *refs):
    info, pieces = refs[0], refs[1 : 1 + parts]
    count = sum(riding)
    riders = iter(refs[1 + parts : 1 + parts + count])
    riders = [next(riders) if r else None for r in riding]
    outs = refs[1 + parts + count :]
    mine = info[place]
    for d, piece in enumerate(pieces):
        outs[0][pl.ds(pl.multiple_of((mine ^ d) * rows, rows), rows), :] = piece[0:rows, :]
    lay_out(outs[1:], [outs[0][...]] * (len(outs) - 1), riders[1:])


def final_kernel(place, info, own, other, *refs):
    outs, full = refs[:-1], refs[-1]
    rows = own.shape[0]
    mine = info[place]
    full[pl.ds(pl.multiple_of(mine * rows, rows), rows), :] = own[...]
    full[pl.ds(pl.multiple_of((1 - mine) * rows, rows), rows), :] = other[...]
    width = full.shape[1]
    row = 0
    for out in outs:
        for part in range(out.shape[1] // width):
            out[:, part * width : (part + 1) * width] = full[row : row + out.shape[0], :].astype(F32)
            row += out.shape[0]


def bit_of(mask_bits, index):
    value = jnp.int32(0)
    for k, bit in enumerate(mask_bits):
        value = value | (((index >> bit) & 1) << k)
    return value


def offset_mask(bits, d):
    return sum(1 << bit for k, bit in enumerate(bits) if d >> k & 1)


def all_sum(info, keep, arrived, groups, core_mask, late, riders, loose):
    width = keep.shape[1]
    kept, pieces = keep, [arrived]
    extras = None
    moved_riders, moved_loose = {}, []
    levels = len(groups)

    def carried(stage, masks):
        found = [next((i for st, m, i in riders if st == stage and m == mask), None) for mask in masks]
        return found, [extras[i] for i in found if i is not None]

    def exchange(stage, values, masks, found):
        batch = [(extras[i], route) for i, route in loose.get(stage, [])]
        if batch:
            values, arrays = lax.optimization_barrier((tuple(values), tuple(a for a, _ in batch)))
        moved = [xor_permute(v, m) for v, m in zip(values, masks)]
        if batch:
            moved, taken = lax.optimization_barrier((tuple(moved), tuple(r(a) for a, (_, r) in zip(arrays, batch))))
            moved_loose.extend(taken)
        for i, piece in zip(found, moved):
            if i is not None:
                moved_riders[i] = piece
        return list(moved)

    def message(rows, rider):
        return ((rows + (0 if rider is None else extras[rider].shape[0]), width), BF16)

    for level, bits in enumerate(groups):
        parts = 2 ** len(bits)
        rows = kept.shape[0] // parts
        masks = [offset_mask(bits, d) for d in range(1, parts)]
        found, cargo = carried(("sum", level), masks)
        made = call(
            lambda *r, level=level, parts=parts, n=len(pieces), riding=[i is not None for i in found]: reduce_kernel(
                SIDES + 1 + level, parts, n, riding, *r
            ),
            [((rows, width), F32)] + [message(rows, i) for i in found],
            [info, kept, *pieces, *cargo],
            smem=1,
            scratch=[pltpu.VMEM(kept.shape, F32)],
        )
        if level == 0:
            made, extras = late(made)
        kept = made[0]
        pieces = exchange(("sum", level), made[1:], masks, found)
    masks = [offset_mask(groups[-1], d) for d in range(1, 2 ** len(groups[-1]))]
    found, cargo = carried(("spread", levels - 1), masks)
    riding = [None] + [i for i in found if i is not None]
    made = call(
        lambda *r, n=len(pieces), riding=[i is not None for i in riding]: reduce_kernel(0, 1, n, riding, *r),
        [message(kept.shape[0], i) for i in riding],
        [info, kept, *pieces, *cargo],
        smem=1,
        scratch=[pltpu.VMEM((8, 128), F32)],
    )
    for level in reversed(range(levels)):
        whole, laden = made[0], iter(made[1:])
        values = [whole if i is None else next(laden) for i in found]
        pieces = [whole] + exchange(("spread", level), values, masks, found)
        rows = whole.shape[0]
        found, cargo = [], []
        if level:
            masks_next = [offset_mask(groups[level - 1], d) for d in range(1, 2 ** len(groups[level - 1]))]
            found, cargo = carried(("spread", level - 1), masks_next)
        riding = [None] + [i for i in found if i is not None]
        made = call(
            lambda *r, level=level, rows=rows, n=len(pieces), riding=[i is not None for i in riding]: gather_kernel(
                SIDES + 1 + level, rows, n, riding, *r
            ),
            [message(rows * len(pieces), i) for i in riding],
            [info, *pieces, *cargo],
            smem=1,
        )
        masks = masks_next if level else None
    whole = made[0]
    return whole, xor_permute(whole, core_mask), moved_riders, moved_loose


def shards(nodes, grad_out, w_query, w_key, w_value, w_out, w_up, w_down, counts, adjacency, expander, pairing, boundary):
    batch, count, width = nodes.shape[2:]
    feats, gout = nodes.reshape(count, width), grad_out.reshape(count, width)
    counts, boundary, pairing = counts[0, 0], boundary[0, 0], pairing[0, 0]
    adjacency, expander = adjacency[0, 0], expander[0, 0]
    rim = boundary.shape[1]
    size_x, size_y = lax.axis_size("sx"), lax.axis_size("sy")
    bits_x, bits_y = size_x.bit_length() - 1, size_y.bit_length() - 1
    merge_y = size_y == 2
    partner = [1 << (bits_x - 1 + bits_y), 1 << (bits_y - 1), 1 << (bits_x - 2 + bits_y)]
    core_bit = bits_y
    rest = [bit for bit in range(bits_x + bits_y) if bit != core_bit]
    groups = [rest[i : i + 2] for i in range(0, len(rest), 2)]
    ix, iy = lax.axis_index("sx"), lax.axis_index("sy")
    index = ix * size_y + iy
    info = jnp.stack(
        [ix >= 0, jnp.where(ix % 2 == 0, ix > 0, ix < size_x - 1), iy > 0, iy < size_y - 1]
        + [bit_of([core_bit], index)]
        + [bit_of(bits, index) for bits in groups]
    ).astype(jnp.int32)

    rim_count = 2 if merge_y else 4
    prepared = call(
        prepare_kernel,
        [((count + EXTRA, width), BF16)] + [((rim, width), BF16)] * rim_count,
        [info, feats, boundary, counts],
        smem=1,
        hbm=3,
    )
    pack, sent = prepared[0], prepared[1:]
    far = [xor_permute(pack, mask) for mask in partner]
    arrived = [pair_permute(sent[0], False), pair_permute(sent[1], True)]
    if not merge_y:
        arrived += [from_behind(sent[3], "sy", 1), from_behind(sent[2], "sy", -1)]

    blocks = counts.shape[0]
    size = count // blocks
    keys = (MATCHINGS + 1) * size
    units = w_up.shape[1]
    total_rows = 4 * width + 2 * units
    all_rows = blocks * keys + SIDES * count
    square = (count, width)
    heads_wide = HEADS * size
    early = call(
        early_kernel,
        [
            ((10 + keys // count, *square), BF16),
            ((SIDES, count, rim), BF16),
            ((SIDES, HEADS, count), F32),
        ],
        [info, boundary, w_query, w_key, w_value, adjacency, expander, pack],
        smem=1,
        hbm=6,
        flops=2 * 10**9,
        nbytes=4 * 2**20,
    )
    places, squares = early[1], early[0]
    moves_shape = (2, count, count)
    made = call(
        lambda *r: main_kernel(merge_y, *r),
        [
            ((total_rows // 2, width), F32),
            ((total_rows // 2, width), BF16),
            ((all_rows, 2 * width), BF16),
            (moves_shape, BF16),
            (square, BF16),
            (square, F32),
            ((count, units), BF16),
            (square, F32),
        ],
        [info, counts, pairing, feats, w_out, w_up, w_down, gout, *early, pack, *far, *arrived],
        smem=3,
        hbm=5,
        scratch=[
            pltpu.VMEM((total_rows, width), F32),
            pltpu.VMEM((all_rows, width), BF16),
            pltpu.VMEM((blocks, keys, heads_wide), F32),
            pltpu.VMEM((blocks, keys, heads_wide), BF16),
            pltpu.VMEM((blocks, keys, heads_wide), BF16),
            pltpu.VMEM((heads_wide, width), BF16),
            pltpu.VMEM((heads_wide, width), BF16),
            pltpu.VMEM((MATCHINGS, count, EXTRA), F32),
        ],
        limit=32,
        flops=10**10,
        nbytes=8 * 2**20,
    )
    keep, send, kvg, moves, query_total, hidden, activ, grad_hidden = made
    finished = []

    def late(values):
        values, gradients = lax.optimization_barrier((tuple(values), kvg))
        results = call(
            lambda *r: back_kernel(merge_y, *r),
            [(square, BF16), (square, F32)] + [(square, BF16)] * MATCHINGS + [((rim, width), BF16)] * rim_count,
            [counts, pairing, w_query, w_down, gradients, moves, query_total, hidden, activ, places, squares],
            smem=2,
            hbm=2,
            scratch=[pltpu.VMEM(square, F32)],
            flops=2 * 10**9,
            nbytes=4 * 2**20,
        )
        finished.extend(results[:2])
        return values, results[2:]

    core_mask = 1 << core_bit
    level_of = {1 << bit: level for level, bits in enumerate(groups) for bit in bits}
    riders = [
        (("sum" if m == 0 else "spread", level_of[mask]), mask, m) for m, mask in enumerate(partner)
    ]
    last = ("spread", 0)
    routes = {("spread", len(groups) - 1): [(MATCHINGS + 1, lambda v: pair_permute(v, True))]}
    routes.setdefault(last, []).append((MATCHINGS, lambda v: pair_permute(v, False)))
    if not merge_y:
        routes[last].append((MATCHINGS + 3, lambda v: from_behind(v, "sy", 1)))
        routes[last].append((MATCHINGS + 2, lambda v: from_behind(v, "sy", -1)))
    own, other, rode, loose = all_sum(info, keep, xor_permute(send, core_mask), groups, core_mask, late, riders, routes)
    layer_out, grad_normed = finished
    returned = [rode[m] for m in range(MATCHINGS)]
    rims = [loose[1], loose[0]] + list(loose[2:])
    grad_nodes = call(
        nodes_kernel,
        [(square, BF16)],
        [info, feats, boundary, grad_hidden, grad_normed, *returned, *rims],
        smem=1,
        hbm=2,
    )[0]
    weights = call(
        lambda *r: final_kernel(SIDES, *r),
        [((width, width), F32)] * 4 + [((width, units), F32), ((units, width), F32)],
        [info, own, other],
        smem=1,
        scratch=[pltpu.VMEM((total_rows, width), BF16)],
    )
    return (layer_out.reshape(nodes.shape), grad_nodes.reshape(nodes.shape), *weights)


def solution(mesh):
    grid = lambda n: P("sx", "sy", *([None] * n))
    return jax.shard_map(
        shards,
        mesh=mesh,
        in_specs=(grid(3), grid(3), P(), P(), P(), P(), P(), P(), grid(1), grid(3), grid(4), grid(2), grid(2)),
        out_specs=(grid(3), grid(3), P(), P(), P(), P(), P(), P()),
        check_vma=False,
    )
```

```python
import math

import jax
import jax.numpy as jnp
from jax import lax
from jax.experimental import pallas as pl
from jax.experimental.pallas import tpu as pltpu
from jax.sharding import PartitionSpec as P

HEADS = 8
HEAD_DIM = 32
EPSILON = 1e-06
NEG_FILL = -1e30
AXES = ("sx", "sy")
EXTRA = 16
MATCHINGS = 3
SIDES = 4
F32 = jnp.float32
BF16 = jnp.bfloat16
GELU_C = math.sqrt(2.0 / math.pi)
GELU_A = 0.044715


def nn(a, b):
    return lax.dot_general(a, b, (((1,), (0,)), ((), ())), preferred_element_type=F32)


def nt(a, b):
    return lax.dot_general(a, b, (((1,), (1,)), ((), ())), preferred_element_type=F32)


def tn(a, b):
    return lax.dot_general(a, b, (((0,), (0,)), ((), ())), preferred_element_type=F32)


def iota(shape, dim):
    return lax.broadcasted_iota(jnp.int32, shape, dim)


def to_bf(mask):
    return jnp.where(mask, 1.0, 0.0).astype(BF16)


def flip(value):
    return jnp.transpose(value.astype(F32), (1, 0))


def pair_permute(value, odd_first):
    count = lax.axis_size("sx")
    pairs = [(i, i + 1) for i in range(1 if odd_first else 0, count - 1, 2)]
    return lax.ppermute(value, "sx", pairs + [(b, a) for a, b in pairs])


def from_behind(block, axis, distance):
    devices = range(lax.axis_size(axis))
    return lax.ppermute(block, axis, [(i - distance, i) for i in devices if i - distance in devices])


def xor_permute(value, mask):
    count = lax.axis_size("sx") * lax.axis_size("sy")
    return lax.ppermute(value, AXES, [(i, i ^ mask) for i in range(count)])


def call(kernel, outs, args, smem=0, hbm=0, scratch=(), limit=16, flops=0, nbytes=0):
    specs = [pl.BlockSpec(memory_space=pltpu.SMEM)] * smem
    specs += [pl.BlockSpec(memory_space=pltpu.HBM)] * hbm
    args = [pltpu.with_memory_space_constraint(a, pltpu.HBM) if smem <= i < smem + hbm else a for i, a in enumerate(args)]
    specs += [pl.BlockSpec(memory_space=pltpu.VMEM)] * (len(args) - smem - hbm)
    scratch = list(scratch)
    if hbm:
        scratch += [(pltpu.SMEM if a.ndim == 1 else pltpu.VMEM)(a.shape, a.dtype) for a in args[smem : smem + hbm]] + [pltpu.SemaphoreType.DMA((hbm,))]
    return pl.pallas_call(
        kernel,
        out_shape=[jax.ShapeDtypeStruct(s, d) for s, d in outs],
        in_specs=specs,
        out_specs=[pl.BlockSpec(memory_space=pltpu.VMEM)] * len(outs),
        scratch_shapes=list(scratch),
        compiler_params=pltpu.CompilerParams(vmem_limit_bytes=limit * 2**20),
        cost_estimate=pl.CostEstimate(flops=flops, bytes_accessed=nbytes, transcendentals=0),
    )(*args)


def fetched(sources, buffers, semaphores):
    copies = [pltpu.make_async_copy(a, b, semaphores.at[i]) for i, (a, b) in enumerate(zip(sources, buffers))]
    for copy in copies:
        copy.start()

    def ready(i):
        copies[i].wait()
        return buffers[i]

    return ready


def side_lines(boundary, odd):
    first, second = boundary[0:1, :], boundary[1:2, :]
    return [jnp.where(odd, first, second), jnp.where(odd, second, first), boundary[2:3, :], boundary[3:4, :]]


def prepare_kernel(info, *refs):
    pack, rims = refs[3], refs[4:-4]
    ready = fetched(refs[:3], refs[-4:-1], refs[-1])
    counts = ready(2)
    nodes = ready(0)
    count, width = nodes.shape
    blocks = counts.shape[0]
    size = count // blocks
    feats = nodes[...].astype(F32)
    normed = (feats * lax.rsqrt(jnp.mean(feats * feats, axis=1, keepdims=True) + EPSILON)).astype(BF16)
    pack[0:count, :] = normed
    lane = iota((EXTRA, count), 1)
    row = iota((EXTRA, count), 0)
    limit = jnp.zeros((EXTRA, count), jnp.int32)
    for b in range(blocks):
        limit = jnp.where(lane // size == b, counts[b], limit)
    extra = jnp.where((row == 0) & (lane % size < limit), 1.0, 0.0)
    boundary = ready(1)
    rim = boundary.shape[1]
    slots = boundary[...].astype(F32)
    for side in range(SIDES):
        line = slots[side : side + 1, :]
        if count > rim:
            line = jnp.concatenate([line, jnp.zeros((1, count - rim), F32)], axis=1)
        extra = jnp.where(row == side + 1, line, extra)
    pack[count : count + EXTRA, :] = extra.astype(BF16)
    lines = side_lines(boundary, info[SIDES] > 0)
    for side, out in enumerate(rims):
        place = to_bf(iota((count, rim), 0) == lines[side])
        out[...] = tn(place, normed).astype(BF16)


def head_rows(shape, dim):
    return iota(shape, dim) // HEAD_DIM


def early_kernel(info, *refs):
    copied = 6
    ready = fetched(refs[:copied], refs[-copied - 1 : -1], refs[-1])
    boundary, wq, wk, wv, adjacency, expander = refs[-copied - 1 : -1]
    pack = refs[copied]
    refs = refs[copied + 1 : -copied - 1]
    squares, places, there = refs
    count, width = squares.shape[1:]
    blocks, size = adjacency.shape[0], adjacency.shape[2]
    rim = places.shape[2]
    normed = pack[0:count, :]
    ready(0)
    lines = side_lines(boundary, info[SIDES] > 0)
    ones = jnp.ones((HEADS, rim), BF16)
    for s in range(SIDES):
        place = to_bf((iota((count, rim), 0) == lines[s]) & (info[s] > 0))
        places[s] = place
        there[s] = nt(ones, place)
    ready(1)
    queries = nn(normed, wq[...]).astype(BF16)
    squares[0] = queries
    squares[9] = flip(queries).astype(BF16)
    for k, weight in enumerate((wk, wv)):
        ready(2 + k)
        squares[1 + k] = weight[...]
        turned = flip(weight[...]).astype(BF16)
        squares[3 + k] = turned
        squares[5 + k] = nn(normed, weight[...]).astype(BF16)
        squares[7 + k] = nt(turned, normed).astype(BF16)
    ready(4)
    ready(5)
    flags = pack[count : count + EXTRA, :].astype(F32)[0:1, :]
    eye = iota((size, size), 0) == iota((size, size), 1)
    for b in range(blocks):
        real = flags[:, b * size : (b + 1) * size] > 0.5
        mask = ((adjacency[b] == 1) & real) | eye
        cols = slice(b * size, (b + 1) * size)
        squares[10, 0:size, cols] = flip(jnp.where(mask, 0.0, NEG_FILL)).astype(BF16)
        for m in range(MATCHINGS):
            lo = (m + 1) * size
            squares[10 + lo // count, lo % count : lo % count + size, cols] = flip(jnp.where(expander[m, b] == 1, 0.0, NEG_FILL)).astype(BF16)


def main_kernel(merge_y, info, counts, pairing, *refs):
    copied = 5
    ready = fetched(refs[:copied], refs[-copied - 1 : -1], refs[-1])
    nodes, wo, wup, wdown, gout = refs[-copied - 1 : -1]
    refs = refs[copied : -copied - 1]
    squares, places, there = refs[:3]
    refs = refs[3:]
    weights, weights_t, own_rows, own_cols = (squares.at[i : i + 2] for i in (1, 3, 5, 7))
    packs = [refs[0], *refs[MATCHINGS:0:-1]]
    rims = refs[MATCHINGS + 1 : MATCHINGS + 1 + (2 if merge_y else 4)]
    refs = refs[MATCHINGS + 1 + len(rims) :]
    keep, send, kvg, moves, query_out, hidden_out, activ_out, grad_hidden_out = refs[:8]
    grads, xcat, probs, pbf, sgrad, qstack, gstack, real_cols = refs[8:]

    count, width = nodes.shape
    hidden_units = wup.shape[1]
    blocks = counts.shape[0]
    size = count // blocks
    keys = (MATCHINGS + 1) * size
    rim = places.shape[2]
    scale = HEAD_DIM**-0.5
    log2e = math.log2(math.e)

    normed = packs[0][0:count, :]
    bias = []
    for m in range(MATCHINGS):
        real_cols[m] = flip(packs[m + 1][count : count + EXTRA, :])
    for b in range(blocks):
        xcat[b * keys : b * keys + size, :] = packs[0][b * size : (b + 1) * size, :]
        for m in range(MATCHINGS):
            start = pl.multiple_of(pairing[m, b] * size, size)
            lo = b * keys + (m + 1) * size
            xcat[lo : lo + size, :] = packs[m + 1][pl.ds(start, size), :]
            real = real_cols[m, pl.ds(start, size), :][:, 0:1]
            at = (m + 1) * size
            kept = squares[10 + at // count, at % count : at % count + size, b * size : (b + 1) * size]
            bias.append(kept.astype(F32) + jnp.where(real > 0.5, 0.0, NEG_FILL))
    base = blocks * keys
    for s in range(SIDES):
        if merge_y and s >= 2:
            other = 3 if s == 2 else 2
            far_slots = packs[2][count : count + EXTRA, :].astype(F32)[other + 1 : other + 2, 0:rim]
            spots = to_bf(iota((count, rim), 0).astype(F32) == far_slots)
            move = nt(places[s], spots).astype(BF16)
            moves[s - 2] = move
            rows = nn(move, packs[2][0:count, :])
        else:
            rows = nn(places[s], rims[s][...])
        xcat[base + s * count : base + (s + 1) * count, :] = rows.astype(BF16)

    queries = squares[0]
    key_rows, key_cols, value_rows, value_cols = [], [], [], []
    for b in range(blocks):
        rows = xcat[b * keys + size : (b + 1) * keys, :]
        own = slice(b * size, (b + 1) * size)
        key_rows.append(jnp.concatenate([own_rows[0, own, :], nn(rows, weights[0]).astype(BF16)], axis=0))
        value_rows.append(jnp.concatenate([own_rows[1, own, :], nn(rows, weights[1]).astype(BF16)], axis=0))
        key_cols.append(jnp.concatenate([own_cols[0, :, own], nt(weights_t[0], rows).astype(BF16)], axis=1))
        value_cols.append(jnp.concatenate([own_cols[1, :, own], nt(weights_t[1], rows).astype(BF16)], axis=1))
    rim_keys, rim_values = [], []
    for s in range(SIDES):
        rows = xcat[base + s * count : base + (s + 1) * count, :]
        rim_keys.append(nn(rows, weights[0]).astype(BF16).astype(F32))
        rim_values.append(nn(rows, weights[1]).astype(BF16).astype(F32))
    bias = [
        jnp.concatenate([squares[10, 0:size, b * size : (b + 1) * size].astype(F32)] + bias[b * MATCHINGS : (b + 1) * MATCHINGS], axis=0)
        for b in range(blocks)
    ]

    spread = to_bf(head_rows((HEADS, width), 1) == iota((HEADS, width), 0))

    def head_sums(product):
        high = product.astype(BF16)
        low = (product - high.astype(F32)).astype(BF16)
        return nt(spread, high) + nt(spread, low)

    queries_f = queries.astype(F32)
    rim_scores = []
    for s in range(SIDES):
        score = head_sums(queries_f * rim_keys[s]) * (scale * log2e)
        rim_scores.append(jnp.where(there[s] > 0.5, score, NEG_FILL))
    rim_top = jnp.maximum(jnp.maximum(rim_scores[0], rim_scores[1]), jnp.maximum(rim_scores[2], rim_scores[3]))

    row_head = head_rows((width, size), 0)
    tops, sums = [], []
    att_blocks = []
    for b in range(blocks):
        cols = slice(b * size, (b + 1) * size)
        top_rows, inv_rows, att_rows = [], [], []
        own = squares[9, :, cols]
        for first in range(0, HEADS, 2):
            pair = (first, first + 1)
            masked = [jnp.where(row_head == h, own, jnp.zeros_like(own)) for h in pair]
            both = nn(key_rows[b], jnp.concatenate(masked, axis=1))
            for k, h in enumerate(pair):
                score = both[:, k * size : (k + 1) * size] * (scale * log2e) + bias[b]
                top = jnp.maximum(jnp.max(score, axis=0, keepdims=True), rim_top[h : h + 1, cols])
                grown = jnp.exp2(score - top)
                total = jnp.sum(grown, axis=0, keepdims=True)
                for s in range(SIDES):
                    total = total + jnp.exp2(rim_scores[s][h : h + 1, cols] - top)
                inverse = 1.0 / total
                prob = grown * inverse
                at = slice(h * size, (h + 1) * size)
                probs[b, :, at] = prob
                pbf[b, :, at] = prob.astype(BF16)
                top_rows.append(top)
                inv_rows.append(inverse)
            rows = slice(first * HEAD_DIM, (first + 2) * HEAD_DIM)
            wide = nn(value_cols[b][rows, :], pbf[b, :, first * size : (first + 2) * size])
            att_rows += [wide[0:HEAD_DIM, 0:size], wide[HEAD_DIM:, size:]]
        tops.append(jnp.concatenate(top_rows, axis=0))
        sums.append(jnp.concatenate(inv_rows, axis=0))
        att_blocks.append(jnp.concatenate(att_rows, axis=0))
    top_all = jnp.concatenate(tops, axis=1)
    inv_all = jnp.concatenate(sums, axis=1)
    mixed = flip(jnp.concatenate(att_blocks, axis=1))
    rim_probs = [jnp.exp2(rim_scores[s] - top_all) * inv_all for s in range(SIDES)]
    rim_wide = [tn(rim_probs[s].astype(BF16), spread) for s in range(SIDES)]
    for s in range(SIDES):
        mixed = mixed + rim_wide[s] * rim_values[s]
    attended = mixed.astype(BF16)

    slot = iota((count, width), 0)
    limit = jnp.zeros((count, width), jnp.int32)
    for b in range(blocks):
        limit = jnp.where(slot // size == b, counts[b], limit)
    usable = jnp.where(slot % size < limit, 1.0, 0.0)
    for i in range(copied):
        ready(i)
    feats = nodes[...].astype(F32)
    hidden = feats + nn(attended, wo[...])
    factor = lax.rsqrt(jnp.mean(hidden * hidden, axis=1, keepdims=True) + EPSILON)
    mid = hidden * factor
    normed_mid = mid.astype(BF16)
    pre = nn(normed_mid, wup[...])
    square = pre * pre
    bent = jnp.tanh(GELU_C * pre * (1.0 + GELU_A * square))
    half = 0.5 * (1.0 + bent)
    activ = (pre * half).astype(BF16)
    hidden_out[...] = hidden
    activ_out[...] = activ
    upstream = gout[...].astype(F32) * usable
    upstream_bf = upstream.astype(BF16)
    grads[4 * width + hidden_units * 1 : 4 * width + 2 * hidden_units, :] = tn(activ, upstream_bf)
    slope = half + 0.5 * pre * (1.0 - bent * bent) * (GELU_C * (1.0 + 3.0 * GELU_A * square))
    grad_pre = (slope * nt(upstream_bf, wdown[...])).astype(BF16)
    grad_up = tn(normed_mid, grad_pre)
    for part in range(hidden_units // width):
        lo = 4 * width + part * width
        grads[lo : lo + width, :] = grad_up[:, part * width : (part + 1) * width]
    grad_mid = nt(grad_pre, wup[...])
    grad_hidden = upstream + factor * (grad_mid - mid * jnp.mean(grad_mid * mid, axis=1, keepdims=True))
    grad_hidden_out[...] = grad_hidden
    grad_hidden_bf = grad_hidden.astype(BF16)
    grads[3 * width : 4 * width, :] = tn(attended, grad_hidden_bf)
    grad_att = nt(grad_hidden_bf, wo[...]).astype(BF16)
    grad_att_f = grad_att.astype(F32)
    grad_att_t = flip(grad_att).astype(BF16)

    lane_head = head_rows((size, width), 1)
    rim_dots = [head_sums(grad_att_f * rim_values[s]) for s in range(SIDES)]
    rim_inner = rim_probs[0] * rim_dots[0]
    for s in range(1, SIDES):
        rim_inner = rim_inner + rim_probs[s] * rim_dots[s]
    inner_blocks, query_blocks = [], []
    for b in range(blocks):
        cols = slice(b * size, (b + 1) * size)
        inner_rows, query_rows = [], []
        own = grad_att_t[:, cols]
        own = grad_att_t[:, cols]
        for first in range(0, HEADS, 2):
            pair = (first, first + 1)
            masked = [jnp.where(row_head == h, own, jnp.zeros_like(own)) for h in pair]
            both = nn(value_rows[b], jnp.concatenate(masked, axis=1))
            for k, h in enumerate(pair):
                dots = both[:, k * size : (k + 1) * size]
                at = slice(h * size, (h + 1) * size)
                prob = probs[b, :, at]
                inner = jnp.sum(prob * dots, axis=0, keepdims=True) + rim_inner[h : h + 1, cols]
                sgrad[b, :, at] = (prob * (dots - inner) * scale).astype(BF16)
                inner_rows.append(inner)
                mine = queries[cols, :]
                qstack[at, :] = jnp.where(lane_head == h, mine, jnp.zeros_like(mine))
                mine = grad_att[cols, :]
                gstack[at, :] = jnp.where(lane_head == h, mine, jnp.zeros_like(mine))
            rows = slice(first * HEAD_DIM, (first + 2) * HEAD_DIM)
            wide = nn(key_cols[b][rows, :], sgrad[b, :, first * size : (first + 2) * size])
            query_rows += [wide[0:HEAD_DIM, 0:size], wide[HEAD_DIM:, size:]]
        inner_blocks.append(jnp.concatenate(inner_rows, axis=0))
        query_blocks.append(jnp.concatenate(query_rows, axis=0))
        span = slice(b * keys, (b + 1) * keys)
        kvg[span, 0:width] = nn(sgrad[b], qstack[...]).astype(BF16)
        kvg[span, width : 2 * width] = nn(pbf[b], gstack[...]).astype(BF16)
    inner_all = jnp.concatenate(inner_blocks, axis=1)
    query_grad = flip(jnp.concatenate(query_blocks, axis=1))
    for s in range(SIDES):
        graded = (rim_probs[s] * (rim_dots[s] - inner_all) * scale).astype(BF16)
        wide = tn(graded, spread)
        query_grad = query_grad + wide * rim_keys[s]
        span = slice(base + s * count, base + (s + 1) * count)
        kvg[span, 0:width] = (wide * queries_f).astype(BF16)
        kvg[span, width : 2 * width] = (rim_wide[s] * grad_att_f).astype(BF16)
    query_total = query_grad.astype(BF16)

    query_out[...] = query_total
    grads[0:width, :] = tn(normed, query_total)
    both = tn(xcat[...], kvg[...])
    grads[width : 2 * width, :] = both[:, 0:width]
    grads[2 * width : 3 * width, :] = both[:, width : 2 * width]

    half_rows = grads.shape[0] // 2
    mine = info[SIDES]
    keep[...] = grads[pl.ds(pl.multiple_of(mine * half_rows, half_rows), half_rows), :]
    send[...] = grads[pl.ds(pl.multiple_of((1 - mine) * half_rows, half_rows), half_rows), :].astype(BF16)


def back_kernel(merge_y, pairing, *refs):
    kvg, moves, places, squares = refs[:4]
    own_out, *rest = refs[4:]
    backs, rim_outs, extra = rest[:MATCHINGS], rest[MATCHINGS:-1], rest[-1]
    count, width = own_out.shape
    blocks = pairing.shape[1]
    size = count // blocks
    keys = (MATCHINGS + 1) * size
    base = blocks * keys
    wk_t, wv_t = squares[3], squares[4]
    extra_back = None
    for s in range(SIDES):
        span = slice(base + s * count, base + (s + 1) * count)
        back = (nn(kvg[span, 0:width], wk_t) + nn(kvg[span, width : 2 * width], wv_t)).astype(BF16)
        if merge_y and s >= 2:
            moved = tn(moves[s - 2], back)
            extra_back = moved if extra_back is None else extra_back + moved
        else:
            rim_outs[s][...] = tn(places[s], back).astype(BF16)
    if merge_y:
        extra[...] = extra_back
    for b in range(blocks):
        span = slice(b * keys, (b + 1) * keys)
        back = nn(kvg[span, 0:width], wk_t) + nn(kvg[span, width : 2 * width], wv_t)
        own_out[b * size : (b + 1) * size, :] = back[0:size]
        for m in range(MATCHINGS):
            start = pl.multiple_of(pairing[m, b] * size, size)
            piece = back[(m + 1) * size : (m + 2) * size]
            if merge_y and m == 1:
                piece = piece + extra[pl.ds(start, size), :]
            backs[m][pl.ds(start, size), :] = piece.astype(BF16)


def output_kernel(counts, *refs):
    copied = 4
    ready = fetched(refs[:copied], refs[-copied - 1 : -1], refs[-1])
    wq, wdown, nodes, boundary = refs[-copied - 1 : -1]
    own_back, query_total, hidden, activ = refs[copied : copied + 4]
    layer_out, grad_normed_out, nodes_out, boundary_out = refs[copied + 4 : -copied - 1]
    count, width = hidden.shape
    blocks = counts.shape[0]
    size = count // blocks
    slot = iota((count, width), 0)
    limit = jnp.zeros((count, width), jnp.int32)
    for b in range(blocks):
        limit = jnp.where(slot // size == b, counts[b], limit)
    usable = jnp.where(slot % size < limit, 1.0, 0.0)
    ready(0)
    grad_normed_out[...] = nt(query_total[...], wq[...]) + own_back[...]
    ready(1)
    layer_out[...] = ((hidden[...] + nn(activ[...], wdown[...])) * usable).astype(BF16)
    ready(2)
    nodes_out[...] = nodes[...]
    ready(3)
    boundary_out[...] = boundary[...]


def nodes_kernel(info, *refs):
    nodes, boundary, grad_hidden, grad_normed = refs[:4]
    backs, rims, out = refs[4 : 4 + MATCHINGS], refs[4 + MATCHINGS : -1], refs[-1]
    lines = side_lines(boundary, info[SIDES] > 0)
    count = nodes.shape[0]
    rim = boundary.shape[1]
    cot = grad_normed[...]
    for back in backs:
        cot = cot + back[...].astype(F32)
    for s, rows in enumerate(rims):
        place = to_bf(iota((count, rim), 0) == lines[s])
        cot = cot + nn(place, rows[...])
    feats = nodes[...].astype(F32)
    factor = lax.rsqrt(jnp.mean(feats * feats, axis=1, keepdims=True) + EPSILON)
    normed = feats * factor
    out[...] = (grad_hidden[...] + factor * (cot - normed * jnp.mean(cot * normed, axis=1, keepdims=True))).astype(BF16)


def reduce_kernel(place, parts, *refs):
    info, kept, received = refs[0], refs[1], refs[2 : -1 - parts]
    outs, total_ref = refs[-1 - parts : -1], refs[-1]
    total = kept[...].astype(F32)
    for piece in received:
        total = total + piece[...].astype(F32)
    if parts == 1:
        outs[0][...] = total.astype(BF16)
        return
    total_ref[...] = total
    rows = total.shape[0] // parts
    mine = info[place]
    outs[0][...] = total_ref[pl.ds(pl.multiple_of(mine * rows, rows), rows), :]
    for d in range(1, parts):
        outs[d][...] = total_ref[pl.ds(pl.multiple_of((mine ^ d) * rows, rows), rows), :].astype(BF16)


def gather_kernel(place, *refs):
    info, pieces, out = refs[0], [refs[1], *refs[-2:1:-1]], refs[-1]
    mine = info[place]
    rows = pieces[0].shape[0]
    for d, piece in enumerate(pieces):
        out[pl.ds(pl.multiple_of((mine ^ d) * rows, rows), rows), :] = piece[...]


def final_kernel(place, info, own, other, *refs):
    outs, full = refs[:-1], refs[-1]
    rows = own.shape[0]
    mine = info[place]
    full[pl.ds(pl.multiple_of(mine * rows, rows), rows), :] = own[...]
    full[pl.ds(pl.multiple_of((1 - mine) * rows, rows), rows), :] = other[...]
    width = full.shape[1]
    row = 0
    for out in outs:
        for part in range(out.shape[1] // width):
            out[:, part * width : (part + 1) * width] = full[row : row + out.shape[0], :].astype(F32)
            row += out.shape[0]


def bit_of(mask_bits, index):
    value = jnp.int32(0)
    for k, bit in enumerate(mask_bits):
        value = value | (((index >> bit) & 1) << k)
    return value


def offset_mask(bits, d):
    return sum(1 << bit for k, bit in enumerate(bits) if d >> k & 1)


def all_sum(info, keep, arrived, groups, core_mask, beside, store):
    width = keep.shape[1]
    kept, pieces = keep, [arrived]
    stage = 0

    def exchange(values, masks, whole):
        nonlocal stage
        work = beside.get(stage)
        stage += 1
        if work is None:
            return whole, [xor_permute(v, m) for v, m in zip(values, masks)]
        values, waited = work(tuple(values))
        moved = [xor_permute(v, m) for v, m in zip(values[::-1], masks[::-1])][::-1]
        moved, done = lax.optimization_barrier((tuple(moved[::-1]), waited()))
        store.update(done)
        return whole, list(moved[::-1])

    for level, bits in enumerate(groups):
        parts = 2 ** len(bits)
        rows = kept.shape[0] // parts
        made = call(
            lambda *r, level=level, parts=parts: reduce_kernel(SIDES + 1 + level, parts, *r),
            [((rows, width), F32)] + [((rows, width), BF16)] * (parts - 1),
            [info, kept, *pieces[::-1]],
            smem=1,
            scratch=[pltpu.VMEM(kept.shape, F32)],
        )
        kept, pieces = exchange(made[1:], [offset_mask(bits, d) for d in range(1, parts)], made[0])
    whole = call(
        lambda *r: reduce_kernel(0, 1, *r),
        [(kept.shape, BF16)],
        [info, kept, *pieces[::-1]],
        smem=1,
        scratch=[pltpu.VMEM((8, 128), F32)],
    )[0]
    for level in reversed(range(len(groups))):
        masks = [offset_mask(groups[level], d) for d in range(1, 2 ** len(groups[level]))]
        whole, pieces = exchange([whole] * len(masks), masks, whole)
        whole = call(
            lambda *r, level=level: gather_kernel(SIDES + 1 + level, *r),
            [((whole.shape[0] * (1 + len(masks)), width), BF16)],
            [info, whole, *pieces[::-1]],
            smem=1,
        )[0]
    return whole, xor_permute(whole, core_mask)


def shards(nodes, grad_out, w_query, w_key, w_value, w_out, w_up, w_down, counts, adjacency, expander, pairing, boundary):
    batch, count, width = nodes.shape[2:]
    feats, gout = nodes.reshape(count, width), grad_out.reshape(count, width)
    counts, boundary, pairing = counts[0, 0], boundary[0, 0], pairing[0, 0]
    adjacency, expander = adjacency[0, 0], expander[0, 0]
    rim = boundary.shape[1]
    size_x, size_y = lax.axis_size("sx"), lax.axis_size("sy")
    bits_x, bits_y = size_x.bit_length() - 1, size_y.bit_length() - 1
    merge_y = size_y == 2
    partner = [1 << (bits_x - 1 + bits_y), 1 << (bits_y - 1), 1 << (bits_x - 2 + bits_y)]
    core_bit = bits_y
    rest = [bit for bit in range(bits_x + bits_y) if bit != core_bit]
    groups = [rest[i : i + 2] for i in range(0, len(rest), 2)]
    ix, iy = lax.axis_index("sx"), lax.axis_index("sy")
    index = ix * size_y + iy
    info = jnp.stack(
        [ix >= 0, jnp.where(ix % 2 == 0, ix > 0, ix < size_x - 1), iy > 0, iy < size_y - 1]
        + [bit_of([core_bit], index)]
        + [bit_of(bits, index) for bits in groups]
    ).astype(jnp.int32)

    rim_count = 2 if merge_y else 4
    prepared = call(
        prepare_kernel,
        [((count + EXTRA, width), BF16)] + [((rim, width), BF16)] * rim_count,
        [info, feats, boundary, counts],
        smem=1,
        hbm=3,
    )
    pack, sent = prepared[0], prepared[1:]
    arrived = [pair_permute(sent[0], False), pair_permute(sent[1], True)]
    if not merge_y:
        arrived += [from_behind(sent[3], "sy", 1), from_behind(sent[2], "sy", -1)]
    far = [xor_permute(pack, mask) for mask in reversed(partner)][::-1]

    blocks = counts.shape[0]
    size = count // blocks
    keys = (MATCHINGS + 1) * size
    units = w_up.shape[1]
    total_rows = 4 * width + 2 * units
    all_rows = blocks * keys + SIDES * count
    square = (count, width)
    heads_wide = HEADS * size
    early = call(
        early_kernel,
        [
            ((10 + keys // count, *square), BF16),
            ((SIDES, count, rim), BF16),
            ((SIDES, HEADS, count), F32),
        ],
        [info, boundary, w_query, w_key, w_value, adjacency, expander, pack],
        smem=1,
        hbm=6,
        flops=2 * 10**9,
        nbytes=4 * 2**20,
    )
    places, squares = early[1], early[0]
    moves_shape = (2, count, count)
    made = call(
        lambda *r: main_kernel(merge_y, *r),
        [
            ((total_rows // 2, width), F32),
            ((total_rows // 2, width), BF16),
            ((all_rows, 2 * width), BF16),
            (moves_shape, BF16),
            (square, BF16),
            (square, F32),
            ((count, units), BF16),
            (square, F32),
        ],
        [info, counts, pairing, feats, w_out, w_up, w_down, gout, *early, pack, *far[::-1], *arrived],
        smem=3,
        hbm=5,
        scratch=[
            pltpu.VMEM((total_rows, width), F32),
            pltpu.VMEM((all_rows, width), BF16),
            pltpu.VMEM((blocks, keys, heads_wide), F32),
            pltpu.VMEM((blocks, keys, heads_wide), BF16),
            pltpu.VMEM((blocks, keys, heads_wide), BF16),
            pltpu.VMEM((heads_wide, width), BF16),
            pltpu.VMEM((heads_wide, width), BF16),
            pltpu.VMEM((MATCHINGS, count, EXTRA), F32),
        ],
        limit=32,
        flops=10**10,
        nbytes=8 * 2**20,
    )
    keep, send, kvg, moves, query_total, hidden, activ, grad_hidden = made
    store = {}

    def first_stage(values):
        values, gradients = lax.optimization_barrier((values, kvg))
        store["back"] = call(
            lambda *r: back_kernel(merge_y, *r),
            [(square, F32)] + [(square, BF16)] * MATCHINGS + [((rim, width), BF16)] * rim_count,
            [pairing, gradients, moves, places, squares],
            smem=1,
            scratch=[pltpu.VMEM(square, F32)],
            flops=2 * 10**9,
            nbytes=4 * 2**20,
        )

        def waited():
            back = store["back"]
            store["m0"] = xor_permute(back[1], partner[0])
            store["m2"] = xor_permute(back[3], partner[2])
            return {}

        return values, waited

    def second_stage(values):
        back = store["back"]
        values, own_back = lax.optimization_barrier((values, back[0]))
        store["out"] = call(
            output_kernel,
            [(square, BF16), (square, F32), (square, BF16), (boundary.shape, boundary.dtype)],
            [counts, w_query, w_down, feats, boundary, own_back, query_total, hidden, activ],
            smem=1,
            hbm=4,
            flops=10**9,
            nbytes=2 * 2**20,
        )

        def waited():
            cargo = [back[2], *back[4:]]
            grad_normed, cargo = lax.optimization_barrier((store["out"][1], tuple(cargo)))
            store["grad_normed"] = grad_normed
            m1, near, beyond, *sides = cargo
            store["m1"] = xor_permute(m1, partner[1])
            store["rims"] = [pair_permute(near, False), pair_permute(beyond, True)]
            if sides:
                store["rims"] += [from_behind(sides[1], "sy", 1), from_behind(sides[0], "sy", -1)]
            return {}

        return values, waited

    def third_stage(values):
        return values, lambda: {"m0": store["m0"], "m2": store["m2"]}

    def fourth_stage(values):
        return values, lambda: {"m1": store["m1"], "rims": store["rims"]}

    core_mask = 1 << core_bit
    own, other = all_sum(
        info, keep, xor_permute(send, core_mask), groups, core_mask, {0: first_stage, 1: second_stage, 2: third_stage, 3: fourth_stage}, store
    )
    layer_out, _, nodes_near, boundary_near = store["out"]
    grad_normed = store["grad_normed"]
    returned = [store["m0"], store["m1"], store["m2"]]
    rims = store["rims"]
    grad_nodes = call(
        nodes_kernel,
        [(square, BF16)],
        [info, nodes_near, boundary_near, grad_hidden, grad_normed, *returned, *rims],
        smem=1,
    )[0]
    weights = call(
        lambda *r: final_kernel(SIDES, *r),
        [((width, width), F32)] * 4 + [((width, units), F32), ((units, width), F32)],
        [info, own, other],
        smem=1,
        scratch=[pltpu.VMEM((total_rows, width), BF16)],
    )
    return (layer_out.reshape(nodes.shape), grad_nodes.reshape(nodes.shape), *weights)


def solution(mesh):
    grid = lambda n: P("sx", "sy", *([None] * n))
    return jax.shard_map(
        shards,
        mesh=mesh,
        in_specs=(grid(3), grid(3), P(), P(), P(), P(), P(), P(), grid(1), grid(3), grid(4), grid(2), grid(2)),
        out_specs=(grid(3), grid(3), P(), P(), P(), P(), P(), P()),
        check_vma=False,
    )
```

```python
import math

import jax
import jax.numpy as jnp
from jax import lax
from jax.experimental import pallas as pl
from jax.experimental.pallas import tpu as pltpu
from jax.sharding import PartitionSpec as P

HEADS = 8
HEAD_DIM = 32
EPSILON = 1e-06
NEG_FILL = -1e30
AXES = ("sx", "sy")
EXTRA = 16
MATCHINGS = 3
SIDES = 4
F32 = jnp.float32
BF16 = jnp.bfloat16
GELU_C = math.sqrt(2.0 / math.pi)
GELU_A = 0.044715


def nn(a, b):
    return lax.dot_general(a, b, (((1,), (0,)), ((), ())), preferred_element_type=F32)


def nt(a, b):
    return lax.dot_general(a, b, (((1,), (1,)), ((), ())), preferred_element_type=F32)


def tn(a, b):
    return lax.dot_general(a, b, (((0,), (0,)), ((), ())), preferred_element_type=F32)


def iota(shape, dim):
    return lax.broadcasted_iota(jnp.int32, shape, dim)


def to_bf(mask):
    return jnp.where(mask, 1.0, 0.0).astype(BF16)


def flip(value):
    return jnp.transpose(value.astype(F32), (1, 0))


def pair_permute(value, odd_first):
    count = lax.axis_size("sx")
    pairs = [(i, i + 1) for i in range(1 if odd_first else 0, count - 1, 2)]
    return lax.ppermute(value, "sx", pairs + [(b, a) for a, b in pairs])


def from_behind(block, axis, distance):
    devices = range(lax.axis_size(axis))
    return lax.ppermute(block, axis, [(i - distance, i) for i in devices if i - distance in devices])


def xor_permute(value, mask):
    count = lax.axis_size("sx") * lax.axis_size("sy")
    return lax.ppermute(value, AXES, [(i, i ^ mask) for i in range(count)])


def call(kernel, outs, args, smem=0, hbm=0, scratch=(), limit=16, flops=0, nbytes=0):
    specs = [pl.BlockSpec(memory_space=pltpu.SMEM)] * smem
    specs += [pl.BlockSpec(memory_space=pltpu.HBM)] * hbm
    args = [pltpu.with_memory_space_constraint(a, pltpu.HBM) if smem <= i < smem + hbm else a for i, a in enumerate(args)]
    specs += [pl.BlockSpec(memory_space=pltpu.VMEM)] * (len(args) - smem - hbm)
    scratch = list(scratch)
    if hbm:
        scratch += [(pltpu.SMEM if a.ndim == 1 else pltpu.VMEM)(a.shape, a.dtype) for a in args[smem : smem + hbm]] + [pltpu.SemaphoreType.DMA((hbm,))]
    return pl.pallas_call(
        kernel,
        out_shape=[jax.ShapeDtypeStruct(s, d) for s, d in outs],
        in_specs=specs,
        out_specs=[pl.BlockSpec(memory_space=pltpu.VMEM)] * len(outs),
        scratch_shapes=list(scratch),
        compiler_params=pltpu.CompilerParams(vmem_limit_bytes=limit * 2**20),
        cost_estimate=pl.CostEstimate(flops=flops, bytes_accessed=nbytes, transcendentals=0),
    )(*args)


def fetched(sources, buffers, semaphores):
    copies = [pltpu.make_async_copy(a, b, semaphores.at[i]) for i, (a, b) in enumerate(zip(sources, buffers))]
    for copy in copies:
        copy.start()

    def ready(i):
        copies[i].wait()
        return buffers[i]

    return ready


def side_lines(boundary, odd):
    first, second = boundary[0:1, :], boundary[1:2, :]
    return [jnp.where(odd, first, second), jnp.where(odd, second, first), boundary[2:3, :], boundary[3:4, :]]


def prepare_kernel(info, *refs):
    pack, rims = refs[3], refs[4:-4]
    ready = fetched(refs[:3], refs[-4:-1], refs[-1])
    counts = ready(2)
    nodes = ready(0)
    count, width = nodes.shape
    blocks = counts.shape[0]
    size = count // blocks
    feats = nodes[...].astype(F32)
    normed = (feats * lax.rsqrt(jnp.mean(feats * feats, axis=1, keepdims=True) + EPSILON)).astype(BF16)
    pack[0:count, :] = normed
    lane = iota((EXTRA, count), 1)
    row = iota((EXTRA, count), 0)
    limit = jnp.zeros((EXTRA, count), jnp.int32)
    for b in range(blocks):
        limit = jnp.where(lane // size == b, counts[b], limit)
    extra = jnp.where((row == 0) & (lane % size < limit), 1.0, 0.0)
    boundary = ready(1)
    rim = boundary.shape[1]
    slots = boundary[...].astype(F32)
    for side in range(SIDES):
        line = slots[side : side + 1, :]
        if count > rim:
            line = jnp.concatenate([line, jnp.zeros((1, count - rim), F32)], axis=1)
        extra = jnp.where(row == side + 1, line, extra)
    pack[count : count + EXTRA, :] = extra.astype(BF16)
    lines = side_lines(boundary, info[SIDES] > 0)
    for side, out in enumerate(rims):
        place = to_bf(iota((count, rim), 0) == lines[side])
        out[...] = tn(place, normed).astype(BF16)


def head_rows(shape, dim):
    return iota(shape, dim) // HEAD_DIM


def early_kernel(info, *refs):
    copied = 6
    ready = fetched(refs[:copied], refs[-copied - 1 : -1], refs[-1])
    boundary, wq, wk, wv, adjacency, expander = refs[-copied - 1 : -1]
    pack = refs[copied]
    refs = refs[copied + 1 : -copied - 1]
    squares, places, there = refs
    count, width = squares.shape[1:]
    blocks, size = adjacency.shape[0], adjacency.shape[2]
    rim = places.shape[2]
    normed = pack[0:count, :]
    ready(0)
    lines = side_lines(boundary, info[SIDES] > 0)
    ones = jnp.ones((HEADS, rim), BF16)
    for s in range(SIDES):
        place = to_bf((iota((count, rim), 0) == lines[s]) & (info[s] > 0))
        places[s] = place
        there[s] = nt(ones, place)
    ready(1)
    queries = nn(normed, wq[...]).astype(BF16)
    squares[0] = queries
    squares[9] = flip(queries).astype(BF16)
    for k, weight in enumerate((wk, wv)):
        ready(2 + k)
        squares[1 + k] = weight[...]
        turned = flip(weight[...]).astype(BF16)
        squares[3 + k] = turned
        squares[5 + k] = nn(normed, weight[...]).astype(BF16)
        squares[7 + k] = nt(turned, normed).astype(BF16)
    ready(4)
    ready(5)
    flags = pack[count : count + EXTRA, :].astype(F32)[0:1, :]
    eye = iota((size, size), 0) == iota((size, size), 1)
    for b in range(blocks):
        real = flags[:, b * size : (b + 1) * size] > 0.5
        mask = ((adjacency[b] == 1) & real) | eye
        cols = slice(b * size, (b + 1) * size)
        squares[10, 0:size, cols] = flip(jnp.where(mask, 0.0, NEG_FILL)).astype(BF16)
        for m in range(MATCHINGS):
            lo = (m + 1) * size
            squares[10 + lo // count, lo % count : lo % count + size, cols] = flip(jnp.where(expander[m, b] == 1, 0.0, NEG_FILL)).astype(BF16)


def main_kernel(merge_y, info, counts, pairing, *refs):
    copied = 5
    ready = fetched(refs[:copied], refs[-copied - 1 : -1], refs[-1])
    nodes, wo, wup, wdown, gout = refs[-copied - 1 : -1]
    refs = refs[copied : -copied - 1]
    squares, places, there = refs[:3]
    refs = refs[3:]
    weights, weights_t, own_rows, own_cols = (squares.at[i : i + 2] for i in (1, 3, 5, 7))
    packs = [refs[0], *refs[MATCHINGS:0:-1]]
    rims = refs[MATCHINGS + 1 : MATCHINGS + 1 + (2 if merge_y else 4)]
    refs = refs[MATCHINGS + 1 + len(rims) :]
    keep, send, kvg, moves, query_out, hidden_out, activ_out, grad_hidden_out = refs[:8]
    grads, xcat, probs, dotted, pbf, sgrad, qstack, gstack, across, near_rows, near_cols, real_cols = refs[8:]

    count, width = nodes.shape
    hidden_units = wup.shape[1]
    blocks = counts.shape[0]
    size = count // blocks
    keys = (MATCHINGS + 1) * size
    rim = places.shape[2]
    scale = HEAD_DIM**-0.5
    log2e = math.log2(math.e)

    normed = packs[0][0:count, :]
    bias = []
    for m in range(MATCHINGS):
        real_cols[m] = flip(packs[m + 1][count : count + EXTRA, :])
    for b in range(blocks):
        xcat[b * keys : b * keys + size, :] = packs[0][b * size : (b + 1) * size, :]
        for m in range(MATCHINGS):
            start = pl.multiple_of(pairing[m, b] * size, size)
            lo = b * keys + (m + 1) * size
            xcat[lo : lo + size, :] = packs[m + 1][pl.ds(start, size), :]
            real = real_cols[m, pl.ds(start, size), :][:, 0:1]
            at = (m + 1) * size
            kept = squares[10 + at // count, at % count : at % count + size, b * size : (b + 1) * size]
            bias.append(kept.astype(F32) + jnp.where(real > 0.5, 0.0, NEG_FILL))
    base = blocks * keys
    for s in range(SIDES):
        if merge_y and s >= 2:
            other = 3 if s == 2 else 2
            far_slots = packs[2][count : count + EXTRA, :].astype(F32)[other + 1 : other + 2, 0:rim]
            spots = to_bf(iota((count, rim), 0).astype(F32) == far_slots)
            move = nt(places[s], spots).astype(BF16)
            moves[s - 2] = move
            rows = nn(move, packs[2][0:count, :])
        else:
            rows = nn(places[s], rims[s][...])
        xcat[base + s * count : base + (s + 1) * count, :] = rows.astype(BF16)

    queries = squares[0]
    for b in range(blocks):
        rows = xcat[b * keys + size : (b + 1) * keys, :]
        own = slice(b * size, (b + 1) * size)
        for k in range(2):
            near_rows[k, b, 0:size, :] = own_rows[k, own, :]
            near_rows[k, b, size:keys, :] = nn(rows, weights[k]).astype(BF16)
            near_cols[k, b, :, 0:size] = own_cols[k, :, own]
            near_cols[k, b, :, size:keys] = nt(weights_t[k], rows).astype(BF16)
    row_head = head_rows((width, size), 0)
    lane_head = head_rows((size, width), 1)
    for b in range(blocks):
        own, own_t = queries[b * size : (b + 1) * size, :], squares[9, :, b * size : (b + 1) * size]
        for h in range(HEADS):
            at = slice(h * size, (h + 1) * size)
            across[b, :, at] = jnp.where(row_head == h, own_t, jnp.zeros_like(own_t))
            qstack[b, at, :] = jnp.where(lane_head == h, own, jnp.zeros_like(own))
    rim_keys, rim_values = [], []
    for s in range(SIDES):
        rows = xcat[base + s * count : base + (s + 1) * count, :]
        rim_keys.append(nn(rows, weights[0]).astype(BF16).astype(F32))
        rim_values.append(nn(rows, weights[1]).astype(BF16).astype(F32))
    bias = [
        [squares[10, 0:size, b * size : (b + 1) * size].astype(F32)] + bias[b * MATCHINGS : (b + 1) * MATCHINGS]
        for b in range(blocks)
    ]

    spread = to_bf(head_rows((HEADS, width), 1) == iota((HEADS, width), 0))

    def head_sums(product):
        high = product.astype(BF16)
        low = (product - high.astype(F32)).astype(BF16)
        return nt(spread, high) + nt(spread, low)

    queries_f = queries.astype(F32)
    rim_scores = []
    for s in range(SIDES):
        score = head_sums(queries_f * rim_keys[s]) * (scale * log2e)
        rim_scores.append(jnp.where(there[s] > 0.5, score, NEG_FILL))
    rim_top = jnp.maximum(jnp.maximum(rim_scores[0], rim_scores[1]), jnp.maximum(rim_scores[2], rim_scores[3]))

    pairs = [(b, first) for b in range(blocks) for first in range(0, HEADS, 2)]
    groups = MATCHINGS + 1

    def folded(value, combine):
        part = value[0:8]
        for lo in range(8, value.shape[0], 8):
            part = combine(part, value[lo : lo + 8])
        return part

    def both_heads(table, b, first):
        cols = slice(b * size, (b + 1) * size)
        return jnp.concatenate([table[first : first + 1, cols], table[first + 1 : first + 2, cols]], axis=1)

    tops, sums, inverses, att_parts = {}, {}, {}, {}

    def make_scores(u, c):
        b, first = pairs[u]
        at = slice(first * size, (first + 2) * size)
        rows = slice(c * size, (c + 1) * size)
        score = nn(near_rows[0, b, rows, :], across[b, :, at]) * (scale * log2e)
        score = score + jnp.concatenate([bias[b][c], bias[b][c]], axis=1)
        probs[b, rows, at] = score
        part = folded(score, jnp.maximum)
        tops[u] = part if c == 0 else jnp.maximum(tops[u], part)
        if c == groups - 1:
            tops[u] = jnp.maximum(jnp.max(tops[u], axis=0, keepdims=True), both_heads(rim_top, b, first))

    def make_exp(u, c):
        b, first = pairs[u]
        at = slice(first * size, (first + 2) * size)
        rows = slice(c * size, (c + 1) * size)
        grown = jnp.exp2(probs[b, rows, at] - tops[u])
        probs[b, rows, at] = grown
        part = folded(grown, jnp.add)
        sums[u] = part if c == 0 else sums[u] + part
        if c == groups - 1:
            total = jnp.sum(sums[u], axis=0, keepdims=True)
            for s in range(SIDES):
                total = total + jnp.exp2(both_heads(rim_scores[s], b, first) - tops[u])
            inverses[u] = 1.0 / total

    def make_probs(u, c):
        b, first = pairs[u]
        at = slice(first * size, (first + 2) * size)
        rows = slice(c * size, (c + 1) * size)
        prob = probs[b, rows, at] * inverses[u]
        probs[b, rows, at] = prob
        pbf[b, rows, at] = prob.astype(BF16)

    def make_mix(u):
        b, first = pairs[u]
        rows = slice(first * HEAD_DIM, (first + 2) * HEAD_DIM)
        wide = nn(near_cols[1, b, rows, :], pbf[b, :, first * size : (first + 2) * size])
        att_parts[u] = [wide[0:HEAD_DIM, 0:size], wide[HEAD_DIM:, size:]]

    def staggered(stages, last):
        for t in range(len(pairs) + len(stages)):
            for c in range(groups):
                for late, stage in enumerate(stages):
                    if 0 <= t - late < len(pairs):
                        stage(t - late, c)
            if 0 <= t - len(stages) < len(pairs):
                last(t - len(stages))

    staggered([make_scores, make_exp, make_probs], make_mix)

    def by_block(values):
        per = HEADS // 2
        return jnp.concatenate(
            [jnp.concatenate(sum((values[b * per + i] for i in range(per)), []), axis=0) for b in range(blocks)], axis=1
        )

    def halves(values):
        return {u: [v[:, 0:size], v[:, size:]] for u, v in values.items()}

    top_all = by_block(halves(tops))
    inv_all = by_block(halves(inverses))
    mixed = flip(by_block(att_parts))
    rim_probs = [jnp.exp2(rim_scores[s] - top_all) * inv_all for s in range(SIDES)]
    rim_wide = [tn(rim_probs[s].astype(BF16), spread) for s in range(SIDES)]
    for s in range(SIDES):
        mixed = mixed + rim_wide[s] * rim_values[s]
    attended = mixed.astype(BF16)

    slot = iota((count, width), 0)
    limit = jnp.zeros((count, width), jnp.int32)
    for b in range(blocks):
        limit = jnp.where(slot // size == b, counts[b], limit)
    usable = jnp.where(slot % size < limit, 1.0, 0.0)
    for i in range(copied):
        ready(i)
    feats = nodes[...].astype(F32)
    hidden = feats + nn(attended, wo[...])
    factor = lax.rsqrt(jnp.mean(hidden * hidden, axis=1, keepdims=True) + EPSILON)
    mid = hidden * factor
    normed_mid = mid.astype(BF16)
    pre = nn(normed_mid, wup[...])
    square = pre * pre
    bent = jnp.tanh(GELU_C * pre * (1.0 + GELU_A * square))
    half = 0.5 * (1.0 + bent)
    activ = (pre * half).astype(BF16)
    hidden_out[...] = hidden
    activ_out[...] = activ
    upstream = gout[...].astype(F32) * usable
    upstream_bf = upstream.astype(BF16)
    grads[4 * width + hidden_units * 1 : 4 * width + 2 * hidden_units, :] = tn(activ, upstream_bf)
    slope = half + 0.5 * pre * (1.0 - bent * bent) * (GELU_C * (1.0 + 3.0 * GELU_A * square))
    grad_pre = (slope * nt(upstream_bf, wdown[...])).astype(BF16)
    grad_up = tn(normed_mid, grad_pre)
    for part in range(hidden_units // width):
        lo = 4 * width + part * width
        grads[lo : lo + width, :] = grad_up[:, part * width : (part + 1) * width]
    grad_mid = nt(grad_pre, wup[...])
    grad_hidden = upstream + factor * (grad_mid - mid * jnp.mean(grad_mid * mid, axis=1, keepdims=True))
    grad_hidden_out[...] = grad_hidden
    grad_hidden_bf = grad_hidden.astype(BF16)
    grads[3 * width : 4 * width, :] = tn(attended, grad_hidden_bf)
    grad_att = nt(grad_hidden_bf, wo[...]).astype(BF16)
    grad_att_f = grad_att.astype(F32)
    grad_att_t = flip(grad_att).astype(BF16)

    rim_dots = [head_sums(grad_att_f * rim_values[s]) for s in range(SIDES)]
    rim_inner = rim_probs[0] * rim_dots[0]
    for s in range(1, SIDES):
        rim_inner = rim_inner + rim_probs[s] * rim_dots[s]
    for b in range(blocks):
        own, own_t = grad_att[b * size : (b + 1) * size, :], grad_att_t[:, b * size : (b + 1) * size]
        for h in range(HEADS):
            at = slice(h * size, (h + 1) * size)
            across[b, :, at] = jnp.where(row_head == h, own_t, jnp.zeros_like(own_t))
            gstack[b, at, :] = jnp.where(lane_head == h, own, jnp.zeros_like(own))
    inners, query_parts = {}, {}

    def make_dots(u, c):
        b, first = pairs[u]
        at = slice(first * size, (first + 2) * size)
        rows = slice(c * size, (c + 1) * size)
        dots = nn(near_rows[1, b, rows, :], across[b, :, at])
        dotted[b, rows, at] = dots
        part = folded(probs[b, rows, at] * dots, jnp.add)
        inners[u] = part if c == 0 else inners[u] + part
        if c == groups - 1:
            inners[u] = jnp.sum(inners[u], axis=0, keepdims=True) + both_heads(rim_inner, b, first)

    def make_grads(u, c):
        b, first = pairs[u]
        at = slice(first * size, (first + 2) * size)
        rows = slice(c * size, (c + 1) * size)
        sgrad[b, rows, at] = (probs[b, rows, at] * (dotted[b, rows, at] - inners[u]) * scale).astype(BF16)

    def make_query(u):
        b, first = pairs[u]
        rows = slice(first * HEAD_DIM, (first + 2) * HEAD_DIM)
        wide = nn(near_cols[0, b, rows, :], sgrad[b, :, first * size : (first + 2) * size])
        query_parts[u] = [wide[0:HEAD_DIM, 0:size], wide[HEAD_DIM:, size:]]

    staggered([make_dots, make_grads], make_query)
    for b in range(blocks):
        span = slice(b * keys, (b + 1) * keys)
        kvg[span, 0:width] = nn(sgrad[b], qstack[b]).astype(BF16)
        kvg[span, width : 2 * width] = nn(pbf[b], gstack[b]).astype(BF16)
    inner_all = by_block(halves(inners))
    query_grad = flip(by_block(query_parts))
    for s in range(SIDES):
        graded = (rim_probs[s] * (rim_dots[s] - inner_all) * scale).astype(BF16)
        wide = tn(graded, spread)
        query_grad = query_grad + wide * rim_keys[s]
        span = slice(base + s * count, base + (s + 1) * count)
        kvg[span, 0:width] = (wide * queries_f).astype(BF16)
        kvg[span, width : 2 * width] = (rim_wide[s] * grad_att_f).astype(BF16)
    query_total = query_grad.astype(BF16)

    query_out[...] = query_total
    grads[0:width, :] = tn(normed, query_total)
    both = tn(xcat[...], kvg[...])
    grads[width : 2 * width, :] = both[:, 0:width]
    grads[2 * width : 3 * width, :] = both[:, width : 2 * width]

    half_rows = grads.shape[0] // 2
    mine = info[SIDES]
    keep[...] = grads[pl.ds(pl.multiple_of(mine * half_rows, half_rows), half_rows), :]
    send[...] = grads[pl.ds(pl.multiple_of((1 - mine) * half_rows, half_rows), half_rows), :].astype(BF16)


def back_kernel(merge_y, pairing, *refs):
    kvg, moves, places, squares = refs[:4]
    own_out, *rest = refs[4:]
    backs, rim_outs, extra = rest[:MATCHINGS], rest[MATCHINGS:-1], rest[-1]
    count, width = own_out.shape
    blocks = pairing.shape[1]
    size = count // blocks
    keys = (MATCHINGS + 1) * size
    base = blocks * keys
    wk_t, wv_t = squares[3], squares[4]
    extra_back = None
    for s in range(SIDES):
        span = slice(base + s * count, base + (s + 1) * count)
        back = (nn(kvg[span, 0:width], wk_t) + nn(kvg[span, width : 2 * width], wv_t)).astype(BF16)
        if merge_y and s >= 2:
            moved = tn(moves[s - 2], back)
            extra_back = moved if extra_back is None else extra_back + moved
        else:
            rim_outs[s][...] = tn(places[s], back).astype(BF16)
    if merge_y:
        extra[...] = extra_back
    for b in range(blocks):
        span = slice(b * keys, (b + 1) * keys)
        back = nn(kvg[span, 0:width], wk_t) + nn(kvg[span, width : 2 * width], wv_t)
        own_out[b * size : (b + 1) * size, :] = back[0:size]
        for m in range(MATCHINGS):
            start = pl.multiple_of(pairing[m, b] * size, size)
            piece = back[(m + 1) * size : (m + 2) * size]
            if merge_y and m == 1:
                piece = piece + extra[pl.ds(start, size), :]
            backs[m][pl.ds(start, size), :] = piece.astype(BF16)


def output_kernel(counts, *refs):
    copied = 4
    ready = fetched(refs[:copied], refs[-copied - 1 : -1], refs[-1])
    wq, wdown, nodes, boundary = refs[-copied - 1 : -1]
    own_back, query_total, hidden, activ = refs[copied : copied + 4]
    layer_out, grad_normed_out, nodes_out, boundary_out = refs[copied + 4 : -copied - 1]
    count, width = hidden.shape
    blocks = counts.shape[0]
    size = count // blocks
    slot = iota((count, width), 0)
    limit = jnp.zeros((count, width), jnp.int32)
    for b in range(blocks):
        limit = jnp.where(slot // size == b, counts[b], limit)
    usable = jnp.where(slot % size < limit, 1.0, 0.0)
    ready(0)
    grad_normed_out[...] = nt(query_total[...], wq[...]) + own_back[...]
    ready(1)
    layer_out[...] = ((hidden[...] + nn(activ[...], wdown[...])) * usable).astype(BF16)
    ready(2)
    nodes_out[...] = nodes[...]
    ready(3)
    boundary_out[...] = boundary[...]


def nodes_kernel(info, *refs):
    nodes, boundary, grad_hidden, grad_normed = refs[:4]
    backs, rims, out = refs[4 : 4 + MATCHINGS], refs[4 + MATCHINGS : -1], refs[-1]
    lines = side_lines(boundary, info[SIDES] > 0)
    count = nodes.shape[0]
    rim = boundary.shape[1]
    cot = grad_normed[...]
    for back in backs:
        cot = cot + back[...].astype(F32)
    for s, rows in enumerate(rims):
        place = to_bf(iota((count, rim), 0) == lines[s])
        cot = cot + nn(place, rows[...])
    feats = nodes[...].astype(F32)
    factor = lax.rsqrt(jnp.mean(feats * feats, axis=1, keepdims=True) + EPSILON)
    normed = feats * factor
    out[...] = (grad_hidden[...] + factor * (cot - normed * jnp.mean(cot * normed, axis=1, keepdims=True))).astype(BF16)


def reduce_kernel(place, parts, *refs):
    info, kept, received = refs[0], refs[1], refs[2 : -1 - parts]
    outs, total_ref = refs[-1 - parts : -1], refs[-1]
    total = kept[...].astype(F32)
    for piece in received:
        total = total + piece[...].astype(F32)
    if parts == 1:
        outs[0][...] = total.astype(BF16)
        return
    total_ref[...] = total
    rows = total.shape[0] // parts
    mine = info[place]
    outs[0][...] = total_ref[pl.ds(pl.multiple_of(mine * rows, rows), rows), :]
    for d in range(1, parts):
        outs[d][...] = total_ref[pl.ds(pl.multiple_of((mine ^ d) * rows, rows), rows), :].astype(BF16)


def gather_kernel(place, *refs):
    info, pieces, out = refs[0], [refs[1], *refs[-2:1:-1]], refs[-1]
    mine = info[place]
    rows = pieces[0].shape[0]
    for d, piece in enumerate(pieces):
        out[pl.ds(pl.multiple_of((mine ^ d) * rows, rows), rows), :] = piece[...]


def final_kernel(place, info, own, other, *refs):
    outs, full = refs[:-1], refs[-1]
    rows = own.shape[0]
    mine = info[place]
    full[pl.ds(pl.multiple_of(mine * rows, rows), rows), :] = own[...]
    full[pl.ds(pl.multiple_of((1 - mine) * rows, rows), rows), :] = other[...]
    width = full.shape[1]
    row = 0
    for out in outs:
        for part in range(out.shape[1] // width):
            out[:, part * width : (part + 1) * width] = full[row : row + out.shape[0], :].astype(F32)
            row += out.shape[0]


def bit_of(mask_bits, index):
    value = jnp.int32(0)
    for k, bit in enumerate(mask_bits):
        value = value | (((index >> bit) & 1) << k)
    return value


def offset_mask(bits, d):
    return sum(1 << bit for k, bit in enumerate(bits) if d >> k & 1)


def all_sum(info, keep, arrived, groups, core_mask, beside, store):
    width = keep.shape[1]
    kept, pieces = keep, [arrived]
    stage = 0

    def exchange(values, masks, whole):
        nonlocal stage
        work = beside.get(stage)
        stage += 1
        if work is None:
            return whole, [xor_permute(v, m) for v, m in zip(values, masks)]
        values, waited = work(tuple(values))
        moved = [xor_permute(v, m) for v, m in zip(values[::-1], masks[::-1])][::-1]
        moved, done = lax.optimization_barrier((tuple(moved[::-1]), waited()))
        store.update(done)
        return whole, list(moved[::-1])

    for level, bits in enumerate(groups):
        parts = 2 ** len(bits)
        rows = kept.shape[0] // parts
        made = call(
            lambda *r, level=level, parts=parts: reduce_kernel(SIDES + 1 + level, parts, *r),
            [((rows, width), F32)] + [((rows, width), BF16)] * (parts - 1),
            [info, kept, *pieces[::-1]],
            smem=1,
            scratch=[pltpu.VMEM(kept.shape, F32)],
        )
        kept, pieces = exchange(made[1:], [offset_mask(bits, d) for d in range(1, parts)], made[0])
    whole = call(
        lambda *r: reduce_kernel(0, 1, *r),
        [(kept.shape, BF16)],
        [info, kept, *pieces[::-1]],
        smem=1,
        scratch=[pltpu.VMEM((8, 128), F32)],
    )[0]
    for level in reversed(range(len(groups))):
        masks = [offset_mask(groups[level], d) for d in range(1, 2 ** len(groups[level]))]
        whole, pieces = exchange([whole] * len(masks), masks, whole)
        whole = call(
            lambda *r, level=level: gather_kernel(SIDES + 1 + level, *r),
            [((whole.shape[0] * (1 + len(masks)), width), BF16)],
            [info, whole, *pieces[::-1]],
            smem=1,
        )[0]
    return whole, xor_permute(whole, core_mask)


def shards(nodes, grad_out, w_query, w_key, w_value, w_out, w_up, w_down, counts, adjacency, expander, pairing, boundary):
    batch, count, width = nodes.shape[2:]
    feats, gout = nodes.reshape(count, width), grad_out.reshape(count, width)
    counts, boundary, pairing = counts[0, 0], boundary[0, 0], pairing[0, 0]
    adjacency, expander = adjacency[0, 0], expander[0, 0]
    rim = boundary.shape[1]
    size_x, size_y = lax.axis_size("sx"), lax.axis_size("sy")
    bits_x, bits_y = size_x.bit_length() - 1, size_y.bit_length() - 1
    merge_y = size_y == 2
    partner = [1 << (bits_x - 1 + bits_y), 1 << (bits_y - 1), 1 << (bits_x - 2 + bits_y)]
    core_bit = bits_y
    rest = [bit for bit in range(bits_x + bits_y) if bit != core_bit]
    groups = [rest[i : i + 2] for i in range(0, len(rest), 2)]
    ix, iy = lax.axis_index("sx"), lax.axis_index("sy")
    index = ix * size_y + iy
    info = jnp.stack(
        [ix >= 0, jnp.where(ix % 2 == 0, ix > 0, ix < size_x - 1), iy > 0, iy < size_y - 1]
        + [bit_of([core_bit], index)]
        + [bit_of(bits, index) for bits in groups]
    ).astype(jnp.int32)

    rim_count = 2 if merge_y else 4
    prepared = call(
        prepare_kernel,
        [((count + EXTRA, width), BF16)] + [((rim, width), BF16)] * rim_count,
        [info, feats, boundary, counts],
        smem=1,
        hbm=3,
    )
    pack, sent = prepared[0], prepared[1:]
    arrived = [pair_permute(sent[0], False), pair_permute(sent[1], True)]
    if not merge_y:
        arrived += [from_behind(sent[3], "sy", 1), from_behind(sent[2], "sy", -1)]
    far = [xor_permute(pack, mask) for mask in reversed(partner)][::-1]

    blocks = counts.shape[0]
    size = count // blocks
    keys = (MATCHINGS + 1) * size
    units = w_up.shape[1]
    total_rows = 4 * width + 2 * units
    all_rows = blocks * keys + SIDES * count
    square = (count, width)
    heads_wide = HEADS * size
    early = call(
        early_kernel,
        [
            ((10 + keys // count, *square), BF16),
            ((SIDES, count, rim), BF16),
            ((SIDES, HEADS, count), F32),
        ],
        [info, boundary, w_query, w_key, w_value, adjacency, expander, pack],
        smem=1,
        hbm=6,
        flops=2 * 10**9,
        nbytes=4 * 2**20,
    )
    places, squares = early[1], early[0]
    moves_shape = (2, count, count)
    made = call(
        lambda *r: main_kernel(merge_y, *r),
        [
            ((total_rows // 2, width), F32),
            ((total_rows // 2, width), BF16),
            ((all_rows, 2 * width), BF16),
            (moves_shape, BF16),
            (square, BF16),
            (square, F32),
            ((count, units), BF16),
            (square, F32),
        ],
        [info, counts, pairing, feats, w_out, w_up, w_down, gout, *early, pack, *far[::-1], *arrived],
        smem=3,
        hbm=5,
        scratch=[
            pltpu.VMEM((total_rows, width), F32),
            pltpu.VMEM((all_rows, width), BF16),
            pltpu.VMEM((blocks, keys, heads_wide), F32),
            pltpu.VMEM((blocks, keys, heads_wide), F32),
            pltpu.VMEM((blocks, keys, heads_wide), BF16),
            pltpu.VMEM((blocks, keys, heads_wide), BF16),
            pltpu.VMEM((blocks, heads_wide, width), BF16),
            pltpu.VMEM((blocks, heads_wide, width), BF16),
            pltpu.VMEM((blocks, width, heads_wide), BF16),
            pltpu.VMEM((2, blocks, keys, width), BF16),
            pltpu.VMEM((2, blocks, width, keys), BF16),
            pltpu.VMEM((MATCHINGS, count, EXTRA), F32),
        ],
        limit=32,
        flops=10**10,
        nbytes=8 * 2**20,
    )
    keep, send, kvg, moves, query_total, hidden, activ, grad_hidden = made
    store = {}

    def first_stage(values):
        values, gradients = lax.optimization_barrier((values, kvg))
        store["back"] = call(
            lambda *r: back_kernel(merge_y, *r),
            [(square, F32)] + [(square, BF16)] * MATCHINGS + [((rim, width), BF16)] * rim_count,
            [pairing, gradients, moves, places, squares],
            smem=1,
            scratch=[pltpu.VMEM(square, F32)],
            flops=2 * 10**9,
            nbytes=4 * 2**20,
        )

        def waited():
            back = store["back"]
            store["m0"] = xor_permute(back[1], partner[0])
            store["m2"] = xor_permute(back[3], partner[2])
            return {}

        return values, waited

    def second_stage(values):
        back = store["back"]
        values, own_back = lax.optimization_barrier((values, back[0]))
        store["out"] = call(
            output_kernel,
            [(square, BF16), (square, F32), (square, BF16), (boundary.shape, boundary.dtype)],
            [counts, w_query, w_down, feats, boundary, own_back, query_total, hidden, activ],
            smem=1,
            hbm=4,
            flops=10**9,
            nbytes=2 * 2**20,
        )

        def waited():
            cargo = [back[2], *back[4:]]
            grad_normed, cargo = lax.optimization_barrier((store["out"][1], tuple(cargo)))
            store["grad_normed"] = grad_normed
            m1, near, beyond, *sides = cargo
            store["m1"] = xor_permute(m1, partner[1])
            store["rims"] = [pair_permute(near, False), pair_permute(beyond, True)]
            if sides:
                store["rims"] += [from_behind(sides[1], "sy", 1), from_behind(sides[0], "sy", -1)]
            return {}

        return values, waited

    def third_stage(values):
        return values, lambda: {"m0": store["m0"], "m2": store["m2"]}

    def fourth_stage(values):
        return values, lambda: {"m1": store["m1"], "rims": store["rims"]}

    core_mask = 1 << core_bit
    own, other = all_sum(
        info, keep, xor_permute(send, core_mask), groups, core_mask, {0: first_stage, 1: second_stage, 2: third_stage, 3: fourth_stage}, store
    )
    layer_out, _, nodes_near, boundary_near = store["out"]
    grad_normed = store["grad_normed"]
    returned = [store["m0"], store["m1"], store["m2"]]
    rims = store["rims"]
    grad_nodes = call(
        nodes_kernel,
        [(square, BF16)],
        [info, nodes_near, boundary_near, grad_hidden, grad_normed, *returned, *rims],
        smem=1,
    )[0]
    weights = call(
        lambda *r: final_kernel(SIDES, *r),
        [((width, width), F32)] * 4 + [((width, units), F32), ((units, width), F32)],
        [info, own, other],
        smem=1,
        scratch=[pltpu.VMEM((total_rows, width), BF16)],
    )
    return (layer_out.reshape(nodes.shape), grad_nodes.reshape(nodes.shape), *weights)


def solution(mesh):
    grid = lambda n: P("sx", "sy", *([None] * n))
    return jax.shard_map(
        shards,
        mesh=mesh,
        in_specs=(grid(3), grid(3), P(), P(), P(), P(), P(), P(), grid(1), grid(3), grid(4), grid(2), grid(2)),
        out_specs=(grid(3), grid(3), P(), P(), P(), P(), P(), P()),
        check_vma=False,
    )
```

```python
import math

import jax
import jax.numpy as jnp
from jax import lax
from jax.experimental import pallas as pl
from jax.experimental.pallas import tpu as pltpu
from jax.sharding import PartitionSpec as P

HEADS = 8
HEAD_DIM = 32
EPSILON = 1e-06
NEG_FILL = -1e30
AXES = ("sx", "sy")
EXTRA = 16
MATCHINGS = 3
STEPS = 2
SIDES = 4
F32 = jnp.float32
BF16 = jnp.bfloat16
GELU_C = math.sqrt(2.0 / math.pi)
GELU_A = 0.044715


def nn(a, b):
    return lax.dot_general(a, b, (((1,), (0,)), ((), ())), preferred_element_type=F32)


def nt(a, b):
    return lax.dot_general(a, b, (((1,), (1,)), ((), ())), preferred_element_type=F32)


def tn(a, b):
    return lax.dot_general(a, b, (((0,), (0,)), ((), ())), preferred_element_type=F32)


def iota(shape, dim):
    return lax.broadcasted_iota(jnp.int32, shape, dim)


def to_bf(mask):
    return jnp.where(mask, 1.0, 0.0).astype(BF16)


def flip(value):
    return jnp.transpose(value.astype(F32), (1, 0))


def pair_permute(value, odd_first):
    count = lax.axis_size("sx")
    pairs = [(i, i + 1) for i in range(1 if odd_first else 0, count - 1, 2)]
    return lax.ppermute(value, "sx", pairs + [(b, a) for a, b in pairs])


def from_behind(block, axis, distance):
    devices = range(lax.axis_size(axis))
    return lax.ppermute(block, axis, [(i - distance, i) for i in devices if i - distance in devices])


def xor_permute(value, mask):
    count = lax.axis_size("sx") * lax.axis_size("sy")
    return lax.ppermute(value, AXES, [(i, i ^ mask) for i in range(count)])


def call(kernel, outs, args, smem=0, hbm=0, scratch=(), limit=16, flops=0, nbytes=0, outside=False):
    specs = [pl.BlockSpec(memory_space=pltpu.SMEM)] * smem
    specs += [pl.BlockSpec(memory_space=pltpu.HBM)] * hbm
    args = [pltpu.with_memory_space_constraint(a, pltpu.HBM) if smem <= i < smem + hbm else a for i, a in enumerate(args)]
    specs += [pl.BlockSpec(memory_space=pltpu.VMEM)] * (len(args) - smem - hbm)
    scratch = list(scratch)
    if hbm:
        scratch += [(pltpu.SMEM if a.ndim == 1 else pltpu.VMEM)(a.shape, a.dtype) for a in args[smem : smem + hbm]] + [pltpu.SemaphoreType.DMA((hbm,))]
    return pl.pallas_call(
        kernel,
        out_shape=[jax.ShapeDtypeStruct(s, d) for s, d in outs],
        in_specs=specs,
        out_specs=[pl.BlockSpec(memory_space=pltpu.HBM if outside else pltpu.VMEM)] * len(outs),
        scratch_shapes=list(scratch),
        compiler_params=pltpu.CompilerParams(vmem_limit_bytes=limit * 2**20),
        cost_estimate=pl.CostEstimate(flops=flops, bytes_accessed=nbytes, transcendentals=0),
    )(*args)


def fetched(sources, buffers, semaphores):
    copies = [pltpu.make_async_copy(a, b, semaphores.at[i]) for i, (a, b) in enumerate(zip(sources, buffers))]
    for copy in copies:
        copy.start()

    def ready(i):
        copies[i].wait()
        return buffers[i]

    return ready


def side_lines(boundary, odd):
    first, second = boundary[0:1, :], boundary[1:2, :]
    return [jnp.where(odd, first, second), jnp.where(odd, second, first), boundary[2:3, :], boundary[3:4, :]]


def prepare_kernel(info, *refs):
    pack, rims = refs[3], refs[4:-4]
    ready = fetched(refs[:3], refs[-4:-1], refs[-1])
    counts = ready(2)
    nodes = ready(0)
    count, width = nodes.shape
    blocks = counts.shape[0]
    size = count // blocks
    feats = nodes[...].astype(F32)
    normed = (feats * lax.rsqrt(jnp.mean(feats * feats, axis=1, keepdims=True) + EPSILON)).astype(BF16)
    pack[0:count, :] = normed
    lane = iota((EXTRA, count), 1)
    row = iota((EXTRA, count), 0)
    limit = jnp.zeros((EXTRA, count), jnp.int32)
    for b in range(blocks):
        limit = jnp.where(lane // size == b, counts[b], limit)
    extra = jnp.where((row == 0) & (lane % size < limit), 1.0, 0.0)
    boundary = ready(1)
    rim = boundary.shape[1]
    slots = boundary[...].astype(F32)
    for side in range(SIDES):
        line = slots[side : side + 1, :]
        if count > rim:
            line = jnp.concatenate([line, jnp.zeros((1, count - rim), F32)], axis=1)
        extra = jnp.where(row == side + 1, line, extra)
    pack[count : count + EXTRA, :] = extra.astype(BF16)
    lines = side_lines(boundary, info[SIDES] > 0)
    for side, out in enumerate(rims):
        place = to_bf(iota((count, rim), 0) == lines[side])
        out[...] = tn(place, normed).astype(BF16)


def head_rows(shape, dim):
    return iota(shape, dim) // HEAD_DIM


def early_kernel(info, *refs):
    copied = 6
    ready = fetched(refs[:copied], refs[-copied - 1 : -1], refs[-1])
    boundary, wq, wk, wv, adjacency, expander = refs[-copied - 1 : -1]
    pack = refs[copied]
    refs = refs[copied + 1 : -copied - 1]
    squares, places, there = refs
    count, width = squares.shape[1:]
    blocks, size = adjacency.shape[0], adjacency.shape[2]
    rim = places.shape[2]
    normed = pack[0:count, :]
    ready(0)
    lines = side_lines(boundary, info[SIDES] > 0)
    ones = jnp.ones((HEADS, rim), BF16)
    for s in range(SIDES):
        place = to_bf((iota((count, rim), 0) == lines[s]) & (info[s] > 0))
        places[s] = place
        there[s] = nt(ones, place)
    ready(1)
    queries = nn(normed, wq[...]).astype(BF16)
    squares[0] = queries
    squares[9] = flip(queries).astype(BF16)
    for k, weight in enumerate((wk, wv)):
        ready(2 + k)
        squares[1 + k] = weight[...]
        turned = flip(weight[...]).astype(BF16)
        squares[3 + k] = turned
        squares[5 + k] = nn(normed, weight[...]).astype(BF16)
        squares[7 + k] = nt(turned, normed).astype(BF16)
    ready(4)
    ready(5)
    flags = pack[count : count + EXTRA, :].astype(F32)[0:1, :]
    eye = iota((size, size), 0) == iota((size, size), 1)
    for b in range(blocks):
        real = flags[:, b * size : (b + 1) * size] > 0.5
        mask = ((adjacency[b] == 1) & real) | eye
        cols = slice(b * size, (b + 1) * size)
        squares[10, 0:size, cols] = flip(jnp.where(mask, 0.0, NEG_FILL)).astype(BF16)
        for m in range(MATCHINGS):
            lo = (m + 1) * size
            squares[10 + lo // count, lo % count : lo % count + size, cols] = flip(jnp.where(expander[m, b] == 1, 0.0, NEG_FILL)).astype(BF16)


def main_kernel(merge_y, info, counts, pairing, *refs):
    copied = 5
    ready = fetched(refs[:copied], refs[-copied - 1 : -1], refs[-1])
    nodes, wo, wup, wdown, gout = refs[-copied - 1 : -1]
    refs = refs[copied : -copied - 1]
    squares, places, there = refs[:3]
    refs = refs[3:]
    weights, weights_t, own_rows, own_cols = (squares.at[i : i + 2] for i in (1, 3, 5, 7))
    packs = [refs[0], *refs[MATCHINGS:0:-1]]
    rims = refs[MATCHINGS + 1 : MATCHINGS + 1 + (2 if merge_y else 4)]
    refs = refs[MATCHINGS + 1 + len(rims) :]
    keep, send, kvg, moves, query_out, hidden_out, activ_out, grad_hidden_out = refs[:8]
    grads, xcat, grown, dotted, pbf, sgrad, qstack, gstack, across, near_rows, near_cols, real_cols = refs[8:]

    count, width = nodes.shape
    hidden_units = wup.shape[1]
    blocks = counts.shape[0]
    size = count // blocks
    keys = (MATCHINGS + 1) * size
    rim = places.shape[2]
    scale = HEAD_DIM**-0.5
    log2e = math.log2(math.e)

    normed = packs[0][0:count, :]
    bias = []
    for m in range(MATCHINGS):
        real_cols[m] = flip(packs[m + 1][count : count + EXTRA, :])
    for b in range(blocks):
        xcat[b * keys : b * keys + size, :] = packs[0][b * size : (b + 1) * size, :]
        for m in range(MATCHINGS):
            start = pl.multiple_of(pairing[m, b] * size, size)
            lo = b * keys + (m + 1) * size
            xcat[lo : lo + size, :] = packs[m + 1][pl.ds(start, size), :]
            real = real_cols[m, pl.ds(start, size), :][:, 0:1]
            at = (m + 1) * size
            kept = squares[10 + at // count, at % count : at % count + size, b * size : (b + 1) * size]
            bias.append(kept.astype(F32) + jnp.where(real > 0.5, 0.0, NEG_FILL))
    base = blocks * keys
    for s in range(SIDES):
        if merge_y and s >= 2:
            other = 3 if s == 2 else 2
            far_slots = packs[2][count : count + EXTRA, :].astype(F32)[other + 1 : other + 2, 0:rim]
            spots = to_bf(iota((count, rim), 0).astype(F32) == far_slots)
            move = nt(places[s], spots).astype(BF16)
            moves[s - 2] = move
            rows = nn(move, packs[2][0:count, :])
        else:
            rows = nn(places[s], rims[s][...])
        xcat[base + s * count : base + (s + 1) * count, :] = rows.astype(BF16)

    queries = squares[0]
    for b in range(blocks):
        rows = xcat[b * keys + size : (b + 1) * keys, :]
        own = slice(b * size, (b + 1) * size)
        for k in range(2):
            near_rows[k, b, 0:size, :] = own_rows[k, own, :]
            near_rows[k, b, size:keys, :] = nn(rows, weights[k]).astype(BF16)
            near_cols[k, b, :, 0:size] = own_cols[k, :, own]
            near_cols[k, b, :, size:keys] = nt(weights_t[k], rows).astype(BF16)
    row_head = head_rows((width, size), 0)
    lane_head = head_rows((size, width), 1)
    for b in range(blocks):
        own, own_t = queries[b * size : (b + 1) * size, :], squares[9, :, b * size : (b + 1) * size]
        for h in range(HEADS):
            at = slice(h * size, (h + 1) * size)
            across[b, :, at] = jnp.where(row_head == h, own_t, jnp.zeros_like(own_t))
            qstack[b, at, :] = jnp.where(lane_head == h, own, jnp.zeros_like(own))
    rim_keys, rim_values = [], []
    for s in range(SIDES):
        rows = xcat[base + s * count : base + (s + 1) * count, :]
        rim_keys.append(nn(rows, weights[0]).astype(BF16).astype(F32))
        rim_values.append(nn(rows, weights[1]).astype(BF16).astype(F32))
    bias = [
        [squares[10, 0:size, b * size : (b + 1) * size].astype(F32)] + bias[b * MATCHINGS : (b + 1) * MATCHINGS]
        for b in range(blocks)
    ]

    spread = to_bf(head_rows((HEADS, width), 1) == iota((HEADS, width), 0))

    def head_sums(product):
        high = product.astype(BF16)
        low = (product - high.astype(F32)).astype(BF16)
        return nt(spread, high) + nt(spread, low)

    queries_f = queries.astype(F32)
    rim_scores = []
    for s in range(SIDES):
        score = head_sums(queries_f * rim_keys[s]) * (scale * log2e)
        rim_scores.append(jnp.where(there[s] > 0.5, score, NEG_FILL))
    rim_top = jnp.maximum(jnp.maximum(rim_scores[0], rim_scores[1]), jnp.maximum(rim_scores[2], rim_scores[3]))

    pairs = [(b, first) for b in range(blocks) for first in range(0, HEADS, 2)]
    groups = STEPS
    chunk = keys // groups

    def folded(value, combine):
        part = value[0:8]
        for lo in range(8, value.shape[0], 8):
            part = combine(part, value[lo : lo + 8])
        return part

    def both_heads(table, b, first):
        cols = slice(b * size, (b + 1) * size)
        return jnp.concatenate([table[first : first + 1, cols], table[first + 1 : first + 2, cols]], axis=1)

    tops, sums, inverses, att_parts = {}, {}, {}, {}

    def make_scores(u, c):
        b, first = pairs[u]
        at = slice(first * size, (first + 2) * size)
        rows = slice(c * chunk, (c + 1) * chunk)
        score = nn(near_rows[0, b, rows, :], across[b, :, at]) * (scale * log2e)
        barred = jnp.concatenate(bias[b][c * chunk // size : (c + 1) * chunk // size], axis=0)
        score = score + jnp.concatenate([barred, barred], axis=1)
        grown[b, rows, at] = score
        part = folded(score, jnp.maximum)
        tops[u] = part if c == 0 else jnp.maximum(tops[u], part)
        if c == groups - 1:
            tops[u] = jnp.maximum(jnp.max(tops[u], axis=0, keepdims=True), both_heads(rim_top, b, first))

    def make_exp(u, c):
        b, first = pairs[u]
        at = slice(first * size, (first + 2) * size)
        rows = slice(c * chunk, (c + 1) * chunk)
        raised = jnp.exp2(grown[b, rows, at] - tops[u])
        grown[b, rows, at] = raised
        part = folded(raised, jnp.add)
        sums[u] = part if c == 0 else sums[u] + part
        if c == groups - 1:
            total = jnp.sum(sums[u], axis=0, keepdims=True)
            for s in range(SIDES):
                total = total + jnp.exp2(both_heads(rim_scores[s], b, first) - tops[u])
            inverses[u] = 1.0 / total

    def make_probs(u, c):
        b, first = pairs[u]
        at = slice(first * size, (first + 2) * size)
        rows = slice(c * chunk, (c + 1) * chunk)
        pbf[b, rows, at] = (grown[b, rows, at] * inverses[u]).astype(BF16)

    def make_mix(u):
        b, first = pairs[u]
        rows = slice(first * HEAD_DIM, (first + 2) * HEAD_DIM)
        wide = nn(near_cols[1, b, rows, :], pbf[b, :, first * size : (first + 2) * size])
        att_parts[u] = [wide[0:HEAD_DIM, 0:size], wide[HEAD_DIM:, size:]]

    def staggered(stages, last):
        for t in range(len(pairs) + len(stages)):
            for c in range(groups):
                for late, stage in enumerate(stages):
                    if 0 <= t - late < len(pairs):
                        stage(t - late, c)
            if 0 <= t - len(stages) < len(pairs):
                last(t - len(stages))

    staggered([make_scores, make_exp, make_probs], make_mix)

    def by_block(values):
        per = HEADS // 2
        return jnp.concatenate(
            [jnp.concatenate(sum((values[b * per + i] for i in range(per)), []), axis=0) for b in range(blocks)], axis=1
        )

    def halves(values):
        return {u: [v[:, 0:size], v[:, size:]] for u, v in values.items()}

    top_all = by_block(halves(tops))
    inv_all = by_block(halves(inverses))
    mixed = flip(by_block(att_parts))
    rim_probs = [jnp.exp2(rim_scores[s] - top_all) * inv_all for s in range(SIDES)]
    rim_wide = [tn(rim_probs[s].astype(BF16), spread) for s in range(SIDES)]
    for s in range(SIDES):
        mixed = mixed + rim_wide[s] * rim_values[s]
    attended = mixed.astype(BF16)

    slot = iota((count, width), 0)
    limit = jnp.zeros((count, width), jnp.int32)
    for b in range(blocks):
        limit = jnp.where(slot // size == b, counts[b], limit)
    usable = jnp.where(slot % size < limit, 1.0, 0.0)
    for i in range(copied):
        ready(i)
    feats = nodes[...].astype(F32)
    hidden = feats + nn(attended, wo[...])
    factor = lax.rsqrt(jnp.mean(hidden * hidden, axis=1, keepdims=True) + EPSILON)
    mid = hidden * factor
    normed_mid = mid.astype(BF16)
    pre = nn(normed_mid, wup[...])
    square = pre * pre
    bent = jnp.tanh(GELU_C * pre * (1.0 + GELU_A * square))
    half = 0.5 * (1.0 + bent)
    activ = (pre * half).astype(BF16)
    hidden_out[...] = hidden
    activ_out[...] = activ
    upstream = gout[...].astype(F32) * usable
    upstream_bf = upstream.astype(BF16)
    grads[4 * width + hidden_units * 1 : 4 * width + 2 * hidden_units, :] = tn(activ, upstream_bf)
    slope = half + 0.5 * pre * (1.0 - bent * bent) * (GELU_C * (1.0 + 3.0 * GELU_A * square))
    grad_pre = (slope * nt(upstream_bf, wdown[...])).astype(BF16)
    grad_up = tn(normed_mid, grad_pre)
    for part in range(hidden_units // width):
        lo = 4 * width + part * width
        grads[lo : lo + width, :] = grad_up[:, part * width : (part + 1) * width]
    grad_mid = nt(grad_pre, wup[...])
    grad_hidden = upstream + factor * (grad_mid - mid * jnp.mean(grad_mid * mid, axis=1, keepdims=True))
    grad_hidden_out[...] = grad_hidden
    grad_hidden_bf = grad_hidden.astype(BF16)
    grads[3 * width : 4 * width, :] = tn(attended, grad_hidden_bf)
    grad_att = nt(grad_hidden_bf, wo[...]).astype(BF16)
    grad_att_f = grad_att.astype(F32)
    grad_att_t = flip(grad_att).astype(BF16)

    rim_dots = [head_sums(grad_att_f * rim_values[s]) for s in range(SIDES)]
    rim_inner = rim_probs[0] * rim_dots[0]
    for s in range(1, SIDES):
        rim_inner = rim_inner + rim_probs[s] * rim_dots[s]
    for b in range(blocks):
        own, own_t = grad_att[b * size : (b + 1) * size, :], grad_att_t[:, b * size : (b + 1) * size]
        for h in range(HEADS):
            at = slice(h * size, (h + 1) * size)
            across[b, :, at] = jnp.where(row_head == h, own_t, jnp.zeros_like(own_t))
            gstack[b, at, :] = jnp.where(lane_head == h, own, jnp.zeros_like(own))
    inners, query_parts = {}, {}

    def make_dots(u, c):
        b, first = pairs[u]
        at = slice(first * size, (first + 2) * size)
        rows = slice(c * chunk, (c + 1) * chunk)
        dots = nn(near_rows[1, b, rows, :], across[b, :, at])
        dotted[b, rows, at] = dots
        part = folded(grown[b, rows, at] * dots, jnp.add)
        inners[u] = part if c == 0 else inners[u] + part
        if c == groups - 1:
            inners[u] = jnp.sum(inners[u], axis=0, keepdims=True) * inverses[u] + both_heads(rim_inner, b, first)

    def make_grads(u, c):
        b, first = pairs[u]
        at = slice(first * size, (first + 2) * size)
        rows = slice(c * chunk, (c + 1) * chunk)
        graded = grown[b, rows, at] * ((dotted[b, rows, at] - inners[u]) * (inverses[u] * scale))
        sgrad[b, rows, at] = graded.astype(BF16)

    def make_query(u):
        b, first = pairs[u]
        rows = slice(first * HEAD_DIM, (first + 2) * HEAD_DIM)
        wide = nn(near_cols[0, b, rows, :], sgrad[b, :, first * size : (first + 2) * size])
        query_parts[u] = [wide[0:HEAD_DIM, 0:size], wide[HEAD_DIM:, size:]]

    staggered([make_dots, make_grads], make_query)
    for b in range(blocks):
        span = slice(b * keys, (b + 1) * keys)
        kvg[span, 0:width] = nn(sgrad[b], qstack[b]).astype(BF16)
        kvg[span, width : 2 * width] = nn(pbf[b], gstack[b]).astype(BF16)
    inner_all = by_block(halves(inners))
    query_grad = flip(by_block(query_parts))
    for s in range(SIDES):
        graded = (rim_probs[s] * (rim_dots[s] - inner_all) * scale).astype(BF16)
        wide = tn(graded, spread)
        query_grad = query_grad + wide * rim_keys[s]
        span = slice(base + s * count, base + (s + 1) * count)
        kvg[span, 0:width] = (wide * queries_f).astype(BF16)
        kvg[span, width : 2 * width] = (rim_wide[s] * grad_att_f).astype(BF16)
    query_total = query_grad.astype(BF16)

    query_out[...] = query_total
    grads[0:width, :] = tn(normed, query_total)
    both = tn(xcat[...], kvg[...])
    grads[width : 2 * width, :] = both[:, 0:width]
    grads[2 * width : 3 * width, :] = both[:, width : 2 * width]

    half_rows = grads.shape[0] // 2
    mine = info[SIDES]
    keep[...] = grads[pl.ds(pl.multiple_of(mine * half_rows, half_rows), half_rows), :]
    send[...] = grads[pl.ds(pl.multiple_of((1 - mine) * half_rows, half_rows), half_rows), :].astype(BF16)


def back_kernel(merge_y, pairing, *refs):
    kvg, moves, places, squares = refs[:4]
    own_out, *rest = refs[4:]
    backs, rim_outs, extra = rest[:MATCHINGS], rest[MATCHINGS:-1], rest[-1]
    count, width = own_out.shape
    blocks = pairing.shape[1]
    size = count // blocks
    keys = (MATCHINGS + 1) * size
    base = blocks * keys
    wk_t, wv_t = squares[3], squares[4]
    extra_back = None
    for s in range(SIDES):
        span = slice(base + s * count, base + (s + 1) * count)
        back = (nn(kvg[span, 0:width], wk_t) + nn(kvg[span, width : 2 * width], wv_t)).astype(BF16)
        if merge_y and s >= 2:
            moved = tn(moves[s - 2], back)
            extra_back = moved if extra_back is None else extra_back + moved
        else:
            rim_outs[s][...] = tn(places[s], back).astype(BF16)
    if merge_y:
        extra[...] = extra_back
    for b in range(blocks):
        span = slice(b * keys, (b + 1) * keys)
        back = nn(kvg[span, 0:width], wk_t) + nn(kvg[span, width : 2 * width], wv_t)
        own_out[b * size : (b + 1) * size, :] = back[0:size]
        for m in range(MATCHINGS):
            start = pl.multiple_of(pairing[m, b] * size, size)
            piece = back[(m + 1) * size : (m + 2) * size]
            if merge_y and m == 1:
                piece = piece + extra[pl.ds(start, size), :]
            backs[m][pl.ds(start, size), :] = piece.astype(BF16)


def output_kernel(counts, *refs):
    copied = 4
    ready = fetched(refs[:copied], refs[-copied - 1 : -1], refs[-1])
    wq, wdown, nodes, boundary = refs[-copied - 1 : -1]
    own_back, query_total, hidden, activ = refs[copied : copied + 4]
    layer_out, grad_normed_out, nodes_out, boundary_out = refs[copied + 4 : -copied - 1]
    count, width = hidden.shape
    blocks = counts.shape[0]
    size = count // blocks
    slot = iota((count, width), 0)
    limit = jnp.zeros((count, width), jnp.int32)
    for b in range(blocks):
        limit = jnp.where(slot // size == b, counts[b], limit)
    usable = jnp.where(slot % size < limit, 1.0, 0.0)
    ready(0)
    grad_normed_out[...] = nt(query_total[...], wq[...]) + own_back[...]
    ready(1)
    layer_out[...] = ((hidden[...] + nn(activ[...], wdown[...])) * usable).astype(BF16)
    ready(2)
    nodes_out[...] = nodes[...]
    ready(3)
    boundary_out[...] = boundary[...]


def nodes_kernel(info, *refs):
    nodes, boundary, grad_hidden, grad_normed = refs[:4]
    backs, rims, out = refs[4 : 4 + MATCHINGS], refs[4 + MATCHINGS : -1], refs[-1]
    lines = side_lines(boundary, info[SIDES] > 0)
    count = nodes.shape[0]
    rim = boundary.shape[1]
    cot = grad_normed[...]
    for back in backs:
        cot = cot + back[...].astype(F32)
    for s, rows in enumerate(rims):
        place = to_bf(iota((count, rim), 0) == lines[s])
        cot = cot + nn(place, rows[...])
    feats = nodes[...].astype(F32)
    factor = lax.rsqrt(jnp.mean(feats * feats, axis=1, keepdims=True) + EPSILON)
    normed = feats * factor
    out[...] = (grad_hidden[...] + factor * (cot - normed * jnp.mean(cot * normed, axis=1, keepdims=True))).astype(BF16)


def reduce_kernel(place, parts, *refs):
    info, kept, received = refs[0], refs[1], refs[2 : -1 - parts]
    outs, total_ref = refs[-1 - parts : -1], refs[-1]
    total = kept[...].astype(F32)
    for piece in received:
        total = total + piece[...].astype(F32)
    if parts == 1:
        outs[0][...] = total.astype(BF16)
        return
    total_ref[...] = total
    rows = total.shape[0] // parts
    mine = info[place]
    outs[0][...] = total_ref[pl.ds(pl.multiple_of(mine * rows, rows), rows), :]
    for d in range(1, parts):
        outs[d][...] = total_ref[pl.ds(pl.multiple_of((mine ^ d) * rows, rows), rows), :].astype(BF16)


def gather_kernel(place, *refs):
    info, pieces, out = refs[0], [refs[1], *refs[-2:1:-1]], refs[-1]
    mine = info[place]
    rows = pieces[0].shape[0]
    for d, piece in enumerate(pieces):
        out[pl.ds(pl.multiple_of((mine ^ d) * rows, rows), rows), :] = piece[...]


def final_kernel(place, info, own, other, *refs):
    count = (len(refs) - 1) // 2
    outs, buffers, semaphores = refs[:count], refs[count:-1], refs[-1]
    rows, width = own.shape
    mine = info[place]
    row = 0
    copies = []
    for i, (out, buffer) in enumerate(zip(outs, buffers)):
        for part in range(buffer.shape[1] // width):
            half, lo = divmod(row, rows)
            span = slice(lo, lo + buffer.shape[0])
            value = jnp.where(mine == half, own[span, :].astype(F32), other[span, :].astype(F32))
            buffer[:, part * width : (part + 1) * width] = value
            row += buffer.shape[0]
        copies.append(pltpu.make_async_copy(buffer, out, semaphores.at[i]))
        copies[-1].start()
    for copy in copies:
        copy.wait()


def bit_of(mask_bits, index):
    value = jnp.int32(0)
    for k, bit in enumerate(mask_bits):
        value = value | (((index >> bit) & 1) << k)
    return value


def offset_mask(bits, d):
    return sum(1 << bit for k, bit in enumerate(bits) if d >> k & 1)


def all_sum(info, keep, arrived, groups, core_mask, beside, store):
    width = keep.shape[1]
    kept, pieces = keep, [arrived]
    stage = 0

    def exchange(values, masks, whole):
        nonlocal stage
        work = beside.get(stage)
        stage += 1
        if work is None:
            return whole, [xor_permute(v, m) for v, m in zip(values, masks)]
        values, waited = work(tuple(values))
        moved = [xor_permute(v, m) for v, m in zip(values[::-1], masks[::-1])][::-1]
        moved, done = lax.optimization_barrier((tuple(moved[::-1]), waited()))
        store.update(done)
        return whole, list(moved[::-1])

    for level, bits in enumerate(groups):
        parts = 2 ** len(bits)
        rows = kept.shape[0] // parts
        made = call(
            lambda *r, level=level, parts=parts: reduce_kernel(SIDES + 1 + level, parts, *r),
            [((rows, width), F32)] + [((rows, width), BF16)] * (parts - 1),
            [info, kept, *pieces[::-1]],
            smem=1,
            scratch=[pltpu.VMEM(kept.shape, F32)],
        )
        kept, pieces = exchange(made[1:], [offset_mask(bits, d) for d in range(1, parts)], made[0])
    whole = call(
        lambda *r: reduce_kernel(0, 1, *r),
        [(kept.shape, BF16)],
        [info, kept, *pieces[::-1]],
        smem=1,
        scratch=[pltpu.VMEM((8, 128), F32)],
    )[0]
    for level in reversed(range(len(groups))):
        masks = [offset_mask(groups[level], d) for d in range(1, 2 ** len(groups[level]))]
        whole, pieces = exchange([whole] * len(masks), masks, whole)
        whole = call(
            lambda *r, level=level: gather_kernel(SIDES + 1 + level, *r),
            [((whole.shape[0] * (1 + len(masks)), width), BF16)],
            [info, whole, *pieces[::-1]],
            smem=1,
        )[0]
    return whole, xor_permute(whole, core_mask)


def shards(nodes, grad_out, w_query, w_key, w_value, w_out, w_up, w_down, counts, adjacency, expander, pairing, boundary):
    batch, count, width = nodes.shape[2:]
    feats, gout = nodes.reshape(count, width), grad_out.reshape(count, width)
    counts, boundary, pairing = counts[0, 0], boundary[0, 0], pairing[0, 0]
    adjacency, expander = adjacency[0, 0], expander[0, 0]
    rim = boundary.shape[1]
    size_x, size_y = lax.axis_size("sx"), lax.axis_size("sy")
    bits_x, bits_y = size_x.bit_length() - 1, size_y.bit_length() - 1
    merge_y = size_y == 2
    partner = [1 << (bits_x - 1 + bits_y), 1 << (bits_y - 1), 1 << (bits_x - 2 + bits_y)]
    core_bit = bits_y
    rest = [bit for bit in range(bits_x + bits_y) if bit != core_bit]
    groups = [rest[i : i + 2] for i in range(0, len(rest), 2)]
    ix, iy = lax.axis_index("sx"), lax.axis_index("sy")
    index = ix * size_y + iy
    info = jnp.stack(
        [ix >= 0, jnp.where(ix % 2 == 0, ix > 0, ix < size_x - 1), iy > 0, iy < size_y - 1]
        + [bit_of([core_bit], index)]
        + [bit_of(bits, index) for bits in groups]
    ).astype(jnp.int32)

    rim_count = 2 if merge_y else 4
    prepared = call(
        prepare_kernel,
        [((count + EXTRA, width), BF16)] + [((rim, width), BF16)] * rim_count,
        [info, feats, boundary, counts],
        smem=1,
        hbm=3,
    )
    pack, sent = prepared[0], prepared[1:]
    arrived = [pair_permute(sent[0], False), pair_permute(sent[1], True)]
    if not merge_y:
        arrived += [from_behind(sent[3], "sy", 1), from_behind(sent[2], "sy", -1)]
    far = [xor_permute(pack, mask) for mask in reversed(partner)][::-1]

    blocks = counts.shape[0]
    size = count // blocks
    keys = (MATCHINGS + 1) * size
    units = w_up.shape[1]
    total_rows = 4 * width + 2 * units
    all_rows = blocks * keys + SIDES * count
    square = (count, width)
    heads_wide = HEADS * size
    early = call(
        early_kernel,
        [
            ((10 + keys // count, *square), BF16),
            ((SIDES, count, rim), BF16),
            ((SIDES, HEADS, count), F32),
        ],
        [info, boundary, w_query, w_key, w_value, adjacency, expander, pack],
        smem=1,
        hbm=6,
        flops=2 * 10**9,
        nbytes=4 * 2**20,
    )
    places, squares = early[1], early[0]
    moves_shape = (2, count, count)
    made = call(
        lambda *r: main_kernel(merge_y, *r),
        [
            ((total_rows // 2, width), F32),
            ((total_rows // 2, width), BF16),
            ((all_rows, 2 * width), BF16),
            (moves_shape, BF16),
            (square, BF16),
            (square, F32),
            ((count, units), BF16),
            (square, F32),
        ],
        [info, counts, pairing, feats, w_out, w_up, w_down, gout, *early, pack, *far[::-1], *arrived],
        smem=3,
        hbm=5,
        scratch=[
            pltpu.VMEM((total_rows, width), F32),
            pltpu.VMEM((all_rows, width), BF16),
            pltpu.VMEM((blocks, keys, heads_wide), F32),
            pltpu.VMEM((blocks, keys, heads_wide), F32),
            pltpu.VMEM((blocks, keys, heads_wide), BF16),
            pltpu.VMEM((blocks, keys, heads_wide), BF16),
            pltpu.VMEM((blocks, heads_wide, width), BF16),
            pltpu.VMEM((blocks, heads_wide, width), BF16),
            pltpu.VMEM((blocks, width, heads_wide), BF16),
            pltpu.VMEM((2, blocks, keys, width), BF16),
            pltpu.VMEM((2, blocks, width, keys), BF16),
            pltpu.VMEM((MATCHINGS, count, EXTRA), F32),
        ],
        limit=32,
        flops=10**10,
        nbytes=8 * 2**20,
    )
    keep, send, kvg, moves, query_total, hidden, activ, grad_hidden = made
    store = {}

    def first_stage(values):
        values, gradients = lax.optimization_barrier((values, kvg))
        store["back"] = call(
            lambda *r: back_kernel(merge_y, *r),
            [(square, F32)] + [(square, BF16)] * MATCHINGS + [((rim, width), BF16)] * rim_count,
            [pairing, gradients, moves, places, squares],
            smem=1,
            scratch=[pltpu.VMEM(square, F32)],
            flops=2 * 10**9,
            nbytes=4 * 2**20,
        )

        def waited():
            back = store["back"]
            store["m0"] = xor_permute(back[1], partner[0])
            store["m2"] = xor_permute(back[3], partner[2])
            return {}

        return values, waited

    def second_stage(values):
        back = store["back"]
        values, own_back = lax.optimization_barrier((values, back[0]))
        store["out"] = call(
            output_kernel,
            [(square, BF16), (square, F32), (square, BF16), (boundary.shape, boundary.dtype)],
            [counts, w_query, w_down, feats, boundary, own_back, query_total, hidden, activ],
            smem=1,
            hbm=4,
            flops=10**9,
            nbytes=2 * 2**20,
        )

        return values, lambda: {"out": tuple(store["out"])}

    def third_stage(values):
        back = store["back"]
        values, cargo = lax.optimization_barrier((values, (back[2], *back[4:])))
        m1, near, beyond, *sides = cargo
        store["m1"] = xor_permute(m1, partner[1])
        store["rims"] = [pair_permute(near, False), pair_permute(beyond, True)]
        if sides:
            store["rims"] += [from_behind(sides[1], "sy", 1), from_behind(sides[0], "sy", -1)]
        return values, lambda: {"m0": store["m0"], "m2": store["m2"]}

    def fourth_stage(values):
        return values, lambda: {"m1": store["m1"], "rims": store["rims"]}

    core_mask = 1 << core_bit
    own, other = all_sum(
        info, keep, xor_permute(send, core_mask), groups, core_mask, {0: first_stage, 1: second_stage, 2: third_stage, 3: fourth_stage}, store
    )
    layer_out, _, nodes_near, boundary_near = store["out"]
    grad_normed = store["out"][1]
    returned = [store["m0"], store["m1"], store["m2"]]
    rims = store["rims"]
    grad_nodes = call(
        nodes_kernel,
        [(square, BF16)],
        [info, nodes_near, boundary_near, grad_hidden, grad_normed, *returned, *rims],
        smem=1,
    )[0]
    shapes = [((width, width), F32)] * 4 + [((width, units), F32), ((units, width), F32)]
    weights = call(
        lambda *r: final_kernel(SIDES, *r),
        shapes,
        [info, own, other],
        smem=1,
        scratch=[pltpu.VMEM(*shape) for shape in shapes] + [pltpu.SemaphoreType.DMA((len(shapes),))],
        outside=True,
    )
    return (layer_out.reshape(nodes.shape), grad_nodes.reshape(nodes.shape), *weights)


def solution(mesh):
    grid = lambda n: P("sx", "sy", *([None] * n))
    return jax.shard_map(
        shards,
        mesh=mesh,
        in_specs=(grid(3), grid(3), P(), P(), P(), P(), P(), P(), grid(1), grid(3), grid(4), grid(2), grid(2)),
        out_specs=(grid(3), grid(3), P(), P(), P(), P(), P(), P()),
        check_vma=False,
    )
```

```python
import math

import jax
import jax.numpy as jnp
from jax import lax
from jax.experimental import pallas as pl
from jax.experimental.pallas import tpu as pltpu
from jax.sharding import PartitionSpec as P

HEADS = 8
HEAD_DIM = 32
EPSILON = 1e-06
NEG_FILL = -1e30
AXES = ("sx", "sy")
EXTRA = 16
MATCHINGS = 3
STEPS = 2
SIDES = 4
F32 = jnp.float32
BF16 = jnp.bfloat16
GELU_C = math.sqrt(2.0 / math.pi)
GELU_A = 0.044715


def nn(a, b):
    return lax.dot_general(a, b, (((1,), (0,)), ((), ())), preferred_element_type=F32)


def nt(a, b):
    return lax.dot_general(a, b, (((1,), (1,)), ((), ())), preferred_element_type=F32)


def tn(a, b):
    return lax.dot_general(a, b, (((0,), (0,)), ((), ())), preferred_element_type=F32)


def iota(shape, dim):
    return lax.broadcasted_iota(jnp.int32, shape, dim)


def to_bf(mask):
    return jnp.where(mask, 1.0, 0.0).astype(BF16)


def flip(value):
    return jnp.transpose(value.astype(F32), (1, 0))


def pair_permute(value, odd_first):
    count = lax.axis_size("sx")
    pairs = [(i, i + 1) for i in range(1 if odd_first else 0, count - 1, 2)]
    return lax.ppermute(value, "sx", pairs + [(b, a) for a, b in pairs])


def from_behind(block, axis, distance):
    devices = range(lax.axis_size(axis))
    return lax.ppermute(block, axis, [(i - distance, i) for i in devices if i - distance in devices])


def xor_permute(value, mask):
    count = lax.axis_size("sx") * lax.axis_size("sy")
    return lax.ppermute(value, AXES, [(i, i ^ mask) for i in range(count)])


def call(kernel, outs, args, smem=0, hbm=0, scratch=(), limit=16, flops=0, nbytes=0, outside=False):
    specs = [pl.BlockSpec(memory_space=pltpu.SMEM)] * smem
    specs += [pl.BlockSpec(memory_space=pltpu.HBM)] * hbm
    args = [pltpu.with_memory_space_constraint(a, pltpu.HBM) if smem <= i < smem + hbm else a for i, a in enumerate(args)]
    specs += [pl.BlockSpec(memory_space=pltpu.VMEM)] * (len(args) - smem - hbm)
    scratch = list(scratch)
    if hbm:
        scratch += [(pltpu.SMEM if a.ndim == 1 else pltpu.VMEM)(a.shape, a.dtype) for a in args[smem : smem + hbm]] + [pltpu.SemaphoreType.DMA((hbm,))]
    return pl.pallas_call(
        kernel,
        out_shape=[jax.ShapeDtypeStruct(s, d) for s, d in outs],
        in_specs=specs,
        out_specs=[pl.BlockSpec(memory_space=pltpu.HBM if outside else pltpu.VMEM)] * len(outs),
        scratch_shapes=list(scratch),
        compiler_params=pltpu.CompilerParams(vmem_limit_bytes=limit * 2**20),
        cost_estimate=pl.CostEstimate(flops=flops, bytes_accessed=nbytes, transcendentals=0),
    )(*args)


def fetched(sources, buffers, semaphores):
    copies = [pltpu.make_async_copy(a, b, semaphores.at[i]) for i, (a, b) in enumerate(zip(sources, buffers))]
    for copy in copies:
        copy.start()

    def ready(i):
        copies[i].wait()
        return buffers[i]

    return ready


def side_lines(boundary, odd):
    first, second = boundary[0:1, :], boundary[1:2, :]
    return [jnp.where(odd, first, second), jnp.where(odd, second, first), boundary[2:3, :], boundary[3:4, :]]


def prepare_kernel(info, *refs):
    pack, rims = refs[3], refs[4:-4]
    ready = fetched(refs[:3], refs[-4:-1], refs[-1])
    counts = ready(2)
    nodes = ready(0)
    count, width = nodes.shape
    blocks = counts.shape[0]
    size = count // blocks
    feats = nodes[...].astype(F32)
    normed = (feats * lax.rsqrt(jnp.mean(feats * feats, axis=1, keepdims=True) + EPSILON)).astype(BF16)
    pack[0:count, :] = normed
    lane = iota((EXTRA, count), 1)
    row = iota((EXTRA, count), 0)
    limit = jnp.zeros((EXTRA, count), jnp.int32)
    for b in range(blocks):
        limit = jnp.where(lane // size == b, counts[b], limit)
    extra = jnp.where((row == 0) & (lane % size < limit), 1.0, 0.0)
    boundary = ready(1)
    rim = boundary.shape[1]
    slots = boundary[...].astype(F32)
    for side in range(SIDES):
        line = slots[side : side + 1, :]
        if count > rim:
            line = jnp.concatenate([line, jnp.zeros((1, count - rim), F32)], axis=1)
        extra = jnp.where(row == side + 1, line, extra)
    pack[count : count + EXTRA, :] = extra.astype(BF16)
    lines = side_lines(boundary, info[SIDES] > 0)
    for side, out in enumerate(rims):
        place = to_bf(iota((count, rim), 0) == lines[side])
        out[...] = tn(place, normed).astype(BF16)


def head_rows(shape, dim):
    return iota(shape, dim) // HEAD_DIM


def early_kernel(info, *refs):
    copied = 6
    ready = fetched(refs[:copied], refs[-copied - 1 : -1], refs[-1])
    boundary, wq, wk, wv, adjacency, expander = refs[-copied - 1 : -1]
    pack = refs[copied]
    refs = refs[copied + 1 : -copied - 1]
    squares, places, there = refs
    count, width = squares.shape[1:]
    blocks, size = adjacency.shape[0], adjacency.shape[2]
    rim = places.shape[2]
    normed = pack[0:count, :]
    ready(0)
    lines = side_lines(boundary, info[SIDES] > 0)
    ones = jnp.ones((HEADS, rim), BF16)
    for s in range(SIDES):
        place = to_bf((iota((count, rim), 0) == lines[s]) & (info[s] > 0))
        places[s] = place
        there[s] = nt(ones, place)
    ready(1)
    queries = nn(normed, wq[...]).astype(BF16)
    squares[0] = queries
    squares[9] = flip(queries).astype(BF16)
    for k, weight in enumerate((wk, wv)):
        ready(2 + k)
        squares[1 + k] = weight[...]
        turned = flip(weight[...]).astype(BF16)
        squares[3 + k] = turned
        squares[5 + k] = nn(normed, weight[...]).astype(BF16)
        squares[7 + k] = nt(turned, normed).astype(BF16)
    ready(4)
    ready(5)
    flags = pack[count : count + EXTRA, :].astype(F32)[0:1, :]
    eye = iota((size, size), 0) == iota((size, size), 1)
    for b in range(blocks):
        real = flags[:, b * size : (b + 1) * size] > 0.5
        mask = ((adjacency[b] == 1) & real) | eye
        cols = slice(b * size, (b + 1) * size)
        squares[10, 0:size, cols] = flip(jnp.where(mask, 0.0, NEG_FILL)).astype(BF16)
        for m in range(MATCHINGS):
            lo = (m + 1) * size
            squares[10 + lo // count, lo % count : lo % count + size, cols] = flip(jnp.where(expander[m, b] == 1, 0.0, NEG_FILL)).astype(BF16)


def main_kernel(merge_y, info, counts, pairing, *refs):
    copied = 5
    ready = fetched(refs[:copied], refs[-copied - 1 : -1], refs[-1])
    nodes, wo, wup, wdown, gout = refs[-copied - 1 : -1]
    refs = refs[copied : -copied - 1]
    squares, places, there = refs[:3]
    refs = refs[3:]
    weights, weights_t, own_rows, own_cols = (squares.at[i : i + 2] for i in (1, 3, 5, 7))
    packs = [refs[0], *refs[MATCHINGS:0:-1]]
    rims = refs[MATCHINGS + 1 : MATCHINGS + 1 + (2 if merge_y else 4)]
    refs = refs[MATCHINGS + 1 + len(rims) :]
    keep, send, kvg, moves, query_out, hidden_out, activ_out, grad_hidden_out = refs[:8]
    grads, xcat, grown, dotted, pbf, sgrad, qstack, gstack, across, near_rows, near_cols, real_cols = refs[8:]

    count, width = nodes.shape
    hidden_units = wup.shape[1]
    blocks = counts.shape[0]
    size = count // blocks
    keys = (MATCHINGS + 1) * size
    rim = places.shape[2]
    scale = HEAD_DIM**-0.5
    log2e = math.log2(math.e)

    normed = packs[0][0:count, :]
    bias = []
    for m in range(MATCHINGS):
        real_cols[m] = flip(packs[m + 1][count : count + EXTRA, :])
    for b in range(blocks):
        xcat[b * keys : b * keys + size, :] = packs[0][b * size : (b + 1) * size, :]
        for m in range(MATCHINGS):
            start = pl.multiple_of(pairing[m, b] * size, size)
            lo = b * keys + (m + 1) * size
            xcat[lo : lo + size, :] = packs[m + 1][pl.ds(start, size), :]
            real = real_cols[m, pl.ds(start, size), :][:, 0:1]
            at = (m + 1) * size
            kept = squares[10 + at // count, at % count : at % count + size, b * size : (b + 1) * size]
            bias.append(kept.astype(F32) + jnp.where(real > 0.5, 0.0, NEG_FILL))
    base = blocks * keys
    for s in range(SIDES):
        if merge_y and s >= 2:
            other = 3 if s == 2 else 2
            far_slots = packs[2][count : count + EXTRA, :].astype(F32)[other + 1 : other + 2, 0:rim]
            spots = to_bf(iota((count, rim), 0).astype(F32) == far_slots)
            move = nt(places[s], spots).astype(BF16)
            moves[s - 2] = move
            rows = nn(move, packs[2][0:count, :])
        else:
            rows = nn(places[s], rims[s][...])
        xcat[base + s * count : base + (s + 1) * count, :] = rows.astype(BF16)

    queries = squares[0]
    for b in range(blocks):
        rows = xcat[b * keys + size : (b + 1) * keys, :]
        own = slice(b * size, (b + 1) * size)
        for k in range(2):
            near_rows[k, b, 0:size, :] = own_rows[k, own, :]
            near_rows[k, b, size:keys, :] = nn(rows, weights[k]).astype(BF16)
            near_cols[k, b, :, 0:size] = own_cols[k, :, own]
            near_cols[k, b, :, size:keys] = nt(weights_t[k], rows).astype(BF16)
    row_head = head_rows((width, size), 0)
    lane_head = head_rows((size, width), 1)
    for b in range(blocks):
        own, own_t = queries[b * size : (b + 1) * size, :], squares[9, :, b * size : (b + 1) * size]
        for h in range(HEADS):
            at = slice(h * size, (h + 1) * size)
            across[b, :, at] = jnp.where(row_head == h, own_t, jnp.zeros_like(own_t))
            qstack[b, at, :] = jnp.where(lane_head == h, own, jnp.zeros_like(own))
    rim_keys, rim_values = [], []
    for s in range(SIDES):
        rows = xcat[base + s * count : base + (s + 1) * count, :]
        rim_keys.append(nn(rows, weights[0]).astype(BF16).astype(F32))
        rim_values.append(nn(rows, weights[1]).astype(BF16).astype(F32))
    bias = [
        [squares[10, 0:size, b * size : (b + 1) * size].astype(F32)] + bias[b * MATCHINGS : (b + 1) * MATCHINGS]
        for b in range(blocks)
    ]

    spread = to_bf(head_rows((HEADS, width), 1) == iota((HEADS, width), 0))

    def head_sums(product):
        high = product.astype(BF16)
        low = (product - high.astype(F32)).astype(BF16)
        return nt(spread, high) + nt(spread, low)

    queries_f = queries.astype(F32)
    rim_scores = []
    for s in range(SIDES):
        score = head_sums(queries_f * rim_keys[s]) * (scale * log2e)
        rim_scores.append(jnp.where(there[s] > 0.5, score, NEG_FILL))
    rim_top = jnp.maximum(jnp.maximum(rim_scores[0], rim_scores[1]), jnp.maximum(rim_scores[2], rim_scores[3]))

    pairs = [(b, first) for b in range(blocks) for first in range(0, HEADS, 2)]
    groups = STEPS
    chunk = keys // groups

    def folded(value, combine):
        part = value[0:8]
        for lo in range(8, value.shape[0], 8):
            part = combine(part, value[lo : lo + 8])
        return part

    def both_heads(table, b, first):
        cols = slice(b * size, (b + 1) * size)
        return jnp.concatenate([table[first : first + 1, cols], table[first + 1 : first + 2, cols]], axis=1)

    tops, sums, inverses, att_parts = {}, {}, {}, {}

    def make_scores(u, c):
        b, first = pairs[u]
        at = slice(first * size, (first + 2) * size)
        rows = slice(c * chunk, (c + 1) * chunk)
        score = nn(near_rows[0, b, rows, :], across[b, :, at]) * (scale * log2e)
        barred = jnp.concatenate(bias[b][c * chunk // size : (c + 1) * chunk // size], axis=0)
        score = score + jnp.concatenate([barred, barred], axis=1)
        grown[b, rows, at] = score
        part = folded(score, jnp.maximum)
        tops[u] = part if c == 0 else jnp.maximum(tops[u], part)
        if c == groups - 1:
            tops[u] = jnp.maximum(jnp.max(tops[u], axis=0, keepdims=True), both_heads(rim_top, b, first))

    def make_exp(u, c):
        b, first = pairs[u]
        at = slice(first * size, (first + 2) * size)
        rows = slice(c * chunk, (c + 1) * chunk)
        raised = jnp.exp2(grown[b, rows, at] - tops[u])
        grown[b, rows, at] = raised
        part = folded(raised, jnp.add)
        sums[u] = part if c == 0 else sums[u] + part
        if c == groups - 1:
            total = jnp.sum(sums[u], axis=0, keepdims=True)
            for s in range(SIDES):
                total = total + jnp.exp2(both_heads(rim_scores[s], b, first) - tops[u])
            inverses[u] = 1.0 / total

    def make_probs(u, c):
        b, first = pairs[u]
        at = slice(first * size, (first + 2) * size)
        rows = slice(c * chunk, (c + 1) * chunk)
        pbf[b, rows, at] = (grown[b, rows, at] * inverses[u]).astype(BF16)

    def make_mix(u):
        b, first = pairs[u]
        rows = slice(first * HEAD_DIM, (first + 2) * HEAD_DIM)
        wide = nn(near_cols[1, b, rows, :], pbf[b, :, first * size : (first + 2) * size])
        att_parts[u] = [wide[0:HEAD_DIM, 0:size], wide[HEAD_DIM:, size:]]

    def staggered(stages, last):
        for t in range(len(pairs) + len(stages)):
            for c in range(groups):
                for late, stage in enumerate(stages):
                    if 0 <= t - late < len(pairs):
                        stage(t - late, c)
            if 0 <= t - len(stages) < len(pairs):
                last(t - len(stages))

    staggered([make_scores, make_exp, make_probs], make_mix)

    def by_block(values):
        per = HEADS // 2
        return jnp.concatenate(
            [jnp.concatenate(sum((values[b * per + i] for i in range(per)), []), axis=0) for b in range(blocks)], axis=1
        )

    def halves(values):
        return {u: [v[:, 0:size], v[:, size:]] for u, v in values.items()}

    top_all = by_block(halves(tops))
    inv_all = by_block(halves(inverses))
    mixed = flip(by_block(att_parts))
    rim_probs = [jnp.exp2(rim_scores[s] - top_all) * inv_all for s in range(SIDES)]
    rim_wide = [tn(rim_probs[s].astype(BF16), spread) for s in range(SIDES)]
    for s in range(SIDES):
        mixed = mixed + rim_wide[s] * rim_values[s]
    attended = mixed.astype(BF16)

    slot = iota((count, width), 0)
    limit = jnp.zeros((count, width), jnp.int32)
    for b in range(blocks):
        limit = jnp.where(slot // size == b, counts[b], limit)
    usable = jnp.where(slot % size < limit, 1.0, 0.0)
    for i in range(copied):
        ready(i)
    feats = nodes[...].astype(F32)
    hidden = feats + nn(attended, wo[...])
    factor = lax.rsqrt(jnp.mean(hidden * hidden, axis=1, keepdims=True) + EPSILON)
    mid = hidden * factor
    normed_mid = mid.astype(BF16)
    pre = nn(normed_mid, wup[...])
    square = pre * pre
    bent = jnp.tanh(GELU_C * pre * (1.0 + GELU_A * square))
    half = 0.5 * (1.0 + bent)
    activ = (pre * half).astype(BF16)
    hidden_out[...] = hidden
    activ_out[...] = activ
    upstream = gout[...].astype(F32) * usable
    upstream_bf = upstream.astype(BF16)
    grads[4 * width + hidden_units * 1 : 4 * width + 2 * hidden_units, :] = tn(activ, upstream_bf)
    slope = half + 0.5 * pre * (1.0 - bent * bent) * (GELU_C * (1.0 + 3.0 * GELU_A * square))
    grad_pre = (slope * nt(upstream_bf, wdown[...])).astype(BF16)
    grad_up = tn(normed_mid, grad_pre)
    for part in range(hidden_units // width):
        lo = 4 * width + part * width
        grads[lo : lo + width, :] = grad_up[:, part * width : (part + 1) * width]
    grad_mid = nt(grad_pre, wup[...])
    grad_hidden = upstream + factor * (grad_mid - mid * jnp.mean(grad_mid * mid, axis=1, keepdims=True))
    grad_hidden_out[...] = grad_hidden
    grad_hidden_bf = grad_hidden.astype(BF16)
    grads[3 * width : 4 * width, :] = tn(attended, grad_hidden_bf)
    grad_att = nt(grad_hidden_bf, wo[...]).astype(BF16)
    grad_att_f = grad_att.astype(F32)
    grad_att_t = flip(grad_att).astype(BF16)

    rim_dots = [head_sums(grad_att_f * rim_values[s]) for s in range(SIDES)]
    rim_inner = rim_probs[0] * rim_dots[0]
    for s in range(1, SIDES):
        rim_inner = rim_inner + rim_probs[s] * rim_dots[s]
    for b in range(blocks):
        own, own_t = grad_att[b * size : (b + 1) * size, :], grad_att_t[:, b * size : (b + 1) * size]
        for h in range(HEADS):
            at = slice(h * size, (h + 1) * size)
            across[b, :, at] = jnp.where(row_head == h, own_t, jnp.zeros_like(own_t))
            gstack[b, at, :] = jnp.where(lane_head == h, own, jnp.zeros_like(own))
    inners, query_parts = {}, {}

    def make_dots(u, c):
        b, first = pairs[u]
        at = slice(first * size, (first + 2) * size)
        rows = slice(c * chunk, (c + 1) * chunk)
        dots = nn(near_rows[1, b, rows, :], across[b, :, at])
        dotted[b, rows, at] = dots
        part = folded(grown[b, rows, at] * dots, jnp.add)
        inners[u] = part if c == 0 else inners[u] + part
        if c == groups - 1:
            inners[u] = jnp.sum(inners[u], axis=0, keepdims=True) * inverses[u] + both_heads(rim_inner, b, first)

    def make_grads(u, c):
        b, first = pairs[u]
        at = slice(first * size, (first + 2) * size)
        rows = slice(c * chunk, (c + 1) * chunk)
        graded = grown[b, rows, at] * ((dotted[b, rows, at] - inners[u]) * (inverses[u] * scale))
        sgrad[b, rows, at] = graded.astype(BF16)

    def make_query(u):
        b, first = pairs[u]
        rows = slice(first * HEAD_DIM, (first + 2) * HEAD_DIM)
        wide = nn(near_cols[0, b, rows, :], sgrad[b, :, first * size : (first + 2) * size])
        query_parts[u] = [wide[0:HEAD_DIM, 0:size], wide[HEAD_DIM:, size:]]

    staggered([make_dots, make_grads], make_query)
    for b in range(blocks):
        span = slice(b * keys, (b + 1) * keys)
        kvg[span, 0:width] = nn(sgrad[b], qstack[b]).astype(BF16)
        kvg[span, width : 2 * width] = nn(pbf[b], gstack[b]).astype(BF16)
    inner_all = by_block(halves(inners))
    query_grad = flip(by_block(query_parts))
    for s in range(SIDES):
        graded = (rim_probs[s] * (rim_dots[s] - inner_all) * scale).astype(BF16)
        wide = tn(graded, spread)
        query_grad = query_grad + wide * rim_keys[s]
        span = slice(base + s * count, base + (s + 1) * count)
        kvg[span, 0:width] = (wide * queries_f).astype(BF16)
        kvg[span, width : 2 * width] = (rim_wide[s] * grad_att_f).astype(BF16)
    query_total = query_grad.astype(BF16)

    query_out[...] = query_total
    grads[0:width, :] = tn(normed, query_total)
    both = tn(xcat[...], kvg[...])
    grads[width : 2 * width, :] = both[:, 0:width]
    grads[2 * width : 3 * width, :] = both[:, width : 2 * width]

    half_rows = grads.shape[0] // 2
    mine = info[SIDES]
    keep[...] = grads[pl.ds(pl.multiple_of(mine * half_rows, half_rows), half_rows), :]
    send[...] = grads[pl.ds(pl.multiple_of((1 - mine) * half_rows, half_rows), half_rows), :]


def back_kernel(merge_y, pairing, *refs):
    kvg, moves, places, squares = refs[:4]
    own_out, *rest = refs[4:]
    backs, rim_outs, extra = rest[:MATCHINGS], rest[MATCHINGS:-1], rest[-1]
    count, width = own_out.shape
    blocks = pairing.shape[1]
    size = count // blocks
    keys = (MATCHINGS + 1) * size
    base = blocks * keys
    wk_t, wv_t = squares[3], squares[4]
    extra_back = None
    for s in range(SIDES):
        span = slice(base + s * count, base + (s + 1) * count)
        back = (nn(kvg[span, 0:width], wk_t) + nn(kvg[span, width : 2 * width], wv_t)).astype(BF16)
        if merge_y and s >= 2:
            moved = tn(moves[s - 2], back)
            extra_back = moved if extra_back is None else extra_back + moved
        else:
            rim_outs[s][...] = tn(places[s], back).astype(BF16)
    if merge_y:
        extra[...] = extra_back
    for b in range(blocks):
        span = slice(b * keys, (b + 1) * keys)
        back = nn(kvg[span, 0:width], wk_t) + nn(kvg[span, width : 2 * width], wv_t)
        own_out[b * size : (b + 1) * size, :] = back[0:size]
        for m in range(MATCHINGS):
            start = pl.multiple_of(pairing[m, b] * size, size)
            piece = back[(m + 1) * size : (m + 2) * size]
            if merge_y and m == 1:
                piece = piece + extra[pl.ds(start, size), :]
            backs[m][pl.ds(start, size), :] = piece.astype(BF16)


def output_kernel(counts, *refs):
    copied = 4
    ready = fetched(refs[:copied], refs[-copied - 1 : -1], refs[-1])
    wq, wdown, nodes, boundary = refs[-copied - 1 : -1]
    own_back, query_total, hidden, activ = refs[copied : copied + 4]
    layer_out, grad_normed_out, nodes_out, boundary_out = refs[copied + 4 : -copied - 1]
    count, width = hidden.shape
    blocks = counts.shape[0]
    size = count // blocks
    slot = iota((count, width), 0)
    limit = jnp.zeros((count, width), jnp.int32)
    for b in range(blocks):
        limit = jnp.where(slot // size == b, counts[b], limit)
    usable = jnp.where(slot % size < limit, 1.0, 0.0)
    ready(0)
    grad_normed_out[...] = nt(query_total[...], wq[...]) + own_back[...]
    ready(1)
    layer_out[...] = ((hidden[...] + nn(activ[...], wdown[...])) * usable).astype(BF16)
    ready(2)
    nodes_out[...] = nodes[...]
    ready(3)
    boundary_out[...] = boundary[...]


def nodes_kernel(info, *refs):
    nodes, boundary, grad_hidden, grad_normed = refs[:4]
    backs, rims, out = refs[4 : 4 + MATCHINGS], refs[4 + MATCHINGS : -1], refs[-1]
    lines = side_lines(boundary, info[SIDES] > 0)
    count = nodes.shape[0]
    rim = boundary.shape[1]
    cot = grad_normed[...]
    for back in backs:
        cot = cot + back[...].astype(F32)
    for s, rows in enumerate(rims):
        place = to_bf(iota((count, rim), 0) == lines[s])
        cot = cot + nn(place, rows[...])
    feats = nodes[...].astype(F32)
    factor = lax.rsqrt(jnp.mean(feats * feats, axis=1, keepdims=True) + EPSILON)
    normed = feats * factor
    out[...] = (grad_hidden[...] + factor * (cot - normed * jnp.mean(cot * normed, axis=1, keepdims=True))).astype(BF16)


def reduce_kernel(place, parts, *refs):
    info, kept, received = refs[0], refs[1], refs[2 : -1 - parts]
    outs, total_ref = refs[-1 - parts : -1], refs[-1]
    total = kept[...].astype(F32)
    for piece in received:
        total = total + piece[...].astype(F32)
    if parts == 1:
        outs[0][...] = total.astype(BF16)
        return
    total_ref[...] = total
    rows = total.shape[0] // parts
    mine = info[place]
    outs[0][...] = total_ref[pl.ds(pl.multiple_of(mine * rows, rows), rows), :]
    for d in range(1, parts):
        outs[d][...] = total_ref[pl.ds(pl.multiple_of((mine ^ d) * rows, rows), rows), :].astype(outs[d].dtype)


def gather_kernel(place, turn, *refs):
    info, pieces, out = refs[0], [refs[1], *refs[2:-1][::turn]], refs[-1]
    mine = info[place]
    rows = pieces[0].shape[0]
    for d, piece in enumerate(pieces):
        out[pl.ds(pl.multiple_of((mine ^ d) * rows, rows), rows), :] = piece[...]


def final_kernel(place, info, own, other, *refs):
    count = (len(refs) - 1) // 2
    outs, buffers, semaphores = refs[:count], refs[count:-1], refs[-1]
    rows, width = own.shape
    mine = info[place]
    row = 0
    copies = []
    for i, (out, buffer) in enumerate(zip(outs, buffers)):
        for part in range(buffer.shape[1] // width):
            half, lo = divmod(row, rows)
            span = slice(lo, lo + buffer.shape[0])
            value = jnp.where(mine == half, own[span, :].astype(F32), other[span, :].astype(F32))
            buffer[:, part * width : (part + 1) * width] = value
            row += buffer.shape[0]
        copies.append(pltpu.make_async_copy(buffer, out, semaphores.at[i]))
        copies[-1].start()
    for copy in copies:
        copy.wait()


def bit_of(mask_bits, index):
    value = jnp.int32(0)
    for k, bit in enumerate(mask_bits):
        value = value | (((index >> bit) & 1) << k)
    return value


def offset_mask(bits, d):
    return sum(1 << bit for k, bit in enumerate(bits) if d >> k & 1)


def all_sum(info, keep, arrived, groups, core_mask, beside, store):
    width = keep.shape[1]
    kept, pieces = keep, [arrived]
    stage = 0

    def exchange(values, masks, whole):
        nonlocal stage
        work = beside.get(stage)
        stage += 1
        if work is None:
            return whole, [xor_permute(v, m) for v, m in zip(values, masks)]
        values, waited = work(tuple(values))
        turn = 1 if stage == 2 * len(groups) else -1
        moved = [xor_permute(v, m) for v, m in zip(values[::turn], masks[::turn])]
        moved, done = lax.optimization_barrier((tuple(moved), waited()))
        store.update(done)
        return whole, list(moved[::turn])

    for level, bits in enumerate(groups):
        parts = 2 ** len(bits)
        rows = kept.shape[0] // parts
        made = call(
            lambda *r, level=level, parts=parts: reduce_kernel(SIDES + 1 + level, parts, *r),
            [((rows, width), F32)] + [((rows, width), F32 if level else BF16)] * (parts - 1),
            [info, kept, *pieces[::-1]],
            smem=1,
            scratch=[pltpu.VMEM(kept.shape, F32)],
        )
        kept, pieces = exchange(made[1:], [offset_mask(bits, d) for d in range(1, parts)], made[0])
    whole = call(
        lambda *r: reduce_kernel(0, 1, *r),
        [(kept.shape, BF16)],
        [info, kept, *pieces[::-1]],
        smem=1,
        scratch=[pltpu.VMEM((8, 128), F32)],
    )[0]
    for level in reversed(range(len(groups))):
        masks = [offset_mask(groups[level], d) for d in range(1, 2 ** len(groups[level]))]
        whole, pieces = exchange([whole] * len(masks), masks, whole)
        whole = call(
            lambda *r, level=level, turn=-1 if level else 1: gather_kernel(SIDES + 1 + level, turn, *r),
            [((whole.shape[0] * (1 + len(masks)), width), BF16)],
            [info, whole, *pieces[:: -1 if level else 1]],
            smem=1,
        )[0]
    return whole, xor_permute(whole, core_mask)


def shards(nodes, grad_out, w_query, w_key, w_value, w_out, w_up, w_down, counts, adjacency, expander, pairing, boundary):
    batch, count, width = nodes.shape[2:]
    feats, gout = nodes.reshape(count, width), grad_out.reshape(count, width)
    counts, boundary, pairing = counts[0, 0], boundary[0, 0], pairing[0, 0]
    adjacency, expander = adjacency[0, 0], expander[0, 0]
    rim = boundary.shape[1]
    size_x, size_y = lax.axis_size("sx"), lax.axis_size("sy")
    bits_x, bits_y = size_x.bit_length() - 1, size_y.bit_length() - 1
    merge_y = size_y == 2
    partner = [1 << (bits_x - 1 + bits_y), 1 << (bits_y - 1), 1 << (bits_x - 2 + bits_y)]
    core_bit = bits_y
    rest = [bit for bit in range(bits_x + bits_y) if bit != core_bit]
    groups = [rest[i : i + 2] for i in range(0, len(rest), 2)]
    ix, iy = lax.axis_index("sx"), lax.axis_index("sy")
    index = ix * size_y + iy
    info = jnp.stack(
        [ix >= 0, jnp.where(ix % 2 == 0, ix > 0, ix < size_x - 1), iy > 0, iy < size_y - 1]
        + [bit_of([core_bit], index)]
        + [bit_of(bits, index) for bits in groups]
    ).astype(jnp.int32)

    rim_count = 2 if merge_y else 4
    prepared = call(
        prepare_kernel,
        [((count + EXTRA, width), BF16)] + [((rim, width), BF16)] * rim_count,
        [info, feats, boundary, counts],
        smem=1,
        hbm=3,
    )
    pack, sent = prepared[0], prepared[1:]
    arrived = [pair_permute(sent[0], False), pair_permute(sent[1], True)]
    if not merge_y:
        arrived += [from_behind(sent[3], "sy", 1), from_behind(sent[2], "sy", -1)]
    far = [xor_permute(pack, mask) for mask in reversed(partner)][::-1]

    blocks = counts.shape[0]
    size = count // blocks
    keys = (MATCHINGS + 1) * size
    units = w_up.shape[1]
    total_rows = 4 * width + 2 * units
    all_rows = blocks * keys + SIDES * count
    square = (count, width)
    heads_wide = HEADS * size
    early = call(
        early_kernel,
        [
            ((10 + keys // count, *square), BF16),
            ((SIDES, count, rim), BF16),
            ((SIDES, HEADS, count), F32),
        ],
        [info, boundary, w_query, w_key, w_value, adjacency, expander, pack],
        smem=1,
        hbm=6,
        flops=2 * 10**9,
        nbytes=4 * 2**20,
    )
    places, squares = early[1], early[0]
    moves_shape = (2, count, count)
    made = call(
        lambda *r: main_kernel(merge_y, *r),
        [
            ((total_rows // 2, width), F32),
            ((total_rows // 2, width), F32),
            ((all_rows, 2 * width), BF16),
            (moves_shape, BF16),
            (square, BF16),
            (square, F32),
            ((count, units), BF16),
            (square, F32),
        ],
        [info, counts, pairing, feats, w_out, w_up, w_down, gout, *early, pack, *far[::-1], *arrived],
        smem=3,
        hbm=5,
        scratch=[
            pltpu.VMEM((total_rows, width), F32),
            pltpu.VMEM((all_rows, width), BF16),
            pltpu.VMEM((blocks, keys, heads_wide), F32),
            pltpu.VMEM((blocks, keys, heads_wide), F32),
            pltpu.VMEM((blocks, keys, heads_wide), BF16),
            pltpu.VMEM((blocks, keys, heads_wide), BF16),
            pltpu.VMEM((blocks, heads_wide, width), BF16),
            pltpu.VMEM((blocks, heads_wide, width), BF16),
            pltpu.VMEM((blocks, width, heads_wide), BF16),
            pltpu.VMEM((2, blocks, keys, width), BF16),
            pltpu.VMEM((2, blocks, width, keys), BF16),
            pltpu.VMEM((MATCHINGS, count, EXTRA), F32),
        ],
        limit=32,
        flops=10**10,
        nbytes=8 * 2**20,
    )
    keep, send, kvg, moves, query_total, hidden, activ, grad_hidden = made
    store = {}

    def first_stage(values):
        values, gradients = lax.optimization_barrier((values, kvg))
        store["back"] = call(
            lambda *r: back_kernel(merge_y, *r),
            [(square, F32)] + [(square, BF16)] * MATCHINGS + [((rim, width), BF16)] * rim_count,
            [pairing, gradients, moves, places, squares],
            smem=1,
            scratch=[pltpu.VMEM(square, F32)],
            flops=2 * 10**9,
            nbytes=4 * 2**20,
        )

        def waited():
            back = store["back"]
            store["m0"] = xor_permute(back[1], partner[0])
            store["m2"] = xor_permute(back[3], partner[2])
            return {}

        return values, waited

    def second_stage(values):
        back = store["back"]
        values, own_back = lax.optimization_barrier((values, back[0]))
        store["out"] = call(
            output_kernel,
            [(square, BF16), (square, F32), (square, BF16), (boundary.shape, boundary.dtype)],
            [counts, w_query, w_down, feats, boundary, own_back, query_total, hidden, activ],
            smem=1,
            hbm=4,
            flops=10**9,
            nbytes=2 * 2**20,
        )

        return values, lambda: {"out": tuple(store["out"])}

    def third_stage(values):
        back = store["back"]
        values, cargo = lax.optimization_barrier((values, (back[2], *back[4:])))
        m1, near, beyond, *sides = cargo
        store["m1"] = xor_permute(m1, partner[1])
        store["rims"] = [pair_permute(near, False), pair_permute(beyond, True)]
        if sides:
            store["rims"] += [from_behind(sides[1], "sy", 1), from_behind(sides[0], "sy", -1)]
        return values, lambda: {"m0": store["m0"], "m2": store["m2"]}

    def fourth_stage(values):
        return values, lambda: {"m1": store["m1"], "rims": store["rims"]}

    core_mask = 1 << core_bit
    own, other = all_sum(
        info, keep, xor_permute(send, core_mask), groups, core_mask, {0: first_stage, 1: second_stage, 2: third_stage, 3: fourth_stage}, store
    )
    layer_out, _, nodes_near, boundary_near = store["out"]
    grad_normed = store["out"][1]
    returned = [store["m0"], store["m1"], store["m2"]]
    rims = store["rims"]
    grad_nodes = call(
        nodes_kernel,
        [(square, BF16)],
        [info, nodes_near, boundary_near, grad_hidden, grad_normed, *returned, *rims],
        smem=1,
    )[0]
    shapes = [((width, width), F32)] * 4 + [((width, units), F32), ((units, width), F32)]
    weights = call(
        lambda *r: final_kernel(SIDES, *r),
        shapes,
        [info, own, other],
        smem=1,
        scratch=[pltpu.VMEM(*shape) for shape in shapes] + [pltpu.SemaphoreType.DMA((len(shapes),))],
        outside=True,
    )
    return (layer_out.reshape(nodes.shape), grad_nodes.reshape(nodes.shape), *weights)


def solution(mesh):
    grid = lambda n: P("sx", "sy", *([None] * n))
    return jax.shard_map(
        shards,
        mesh=mesh,
        in_specs=(grid(3), grid(3), P(), P(), P(), P(), P(), P(), grid(1), grid(3), grid(4), grid(2), grid(2)),
        out_specs=(grid(3), grid(3), P(), P(), P(), P(), P(), P()),
        check_vma=False,
    )
```

```python
import math

import jax
import jax.numpy as jnp
from jax import lax
from jax.experimental import pallas as pl
from jax.experimental.pallas import tpu as pltpu
from jax.sharding import PartitionSpec as P

HEADS = 8
HEAD_DIM = 32
EPSILON = 1e-06
NEG_FILL = -1e30
AXES = ("sx", "sy")
EXTRA = 16
MATCHINGS = 3
STEPS = 2
SIDES = 4
F32 = jnp.float32
BF16 = jnp.bfloat16
GELU_C = math.sqrt(2.0 / math.pi)
GELU_A = 0.044715


def nn(a, b):
    return lax.dot_general(a, b, (((1,), (0,)), ((), ())), preferred_element_type=F32)


def nt(a, b):
    return lax.dot_general(a, b, (((1,), (1,)), ((), ())), preferred_element_type=F32)


def tn(a, b):
    return lax.dot_general(a, b, (((0,), (0,)), ((), ())), preferred_element_type=F32)


def iota(shape, dim):
    return lax.broadcasted_iota(jnp.int32, shape, dim)


def to_bf(mask):
    return jnp.where(mask, 1.0, 0.0).astype(BF16)


def flip(value):
    return jnp.transpose(value.astype(F32), (1, 0))


def pair_permute(value, odd_first):
    count = lax.axis_size("sx")
    pairs = [(i, i + 1) for i in range(1 if odd_first else 0, count - 1, 2)]
    return lax.ppermute(value, "sx", pairs + [(b, a) for a, b in pairs])


def from_behind(block, axis, distance):
    devices = range(lax.axis_size(axis))
    return lax.ppermute(block, axis, [(i - distance, i) for i in devices if i - distance in devices])


def xor_permute(value, mask):
    count = lax.axis_size("sx") * lax.axis_size("sy")
    return lax.ppermute(value, AXES, [(i, i ^ mask) for i in range(count)])


def call(kernel, outs, args, smem=0, hbm=0, scratch=(), limit=16, flops=0, nbytes=0, outside=False):
    specs = [pl.BlockSpec(memory_space=pltpu.SMEM)] * smem
    specs += [pl.BlockSpec(memory_space=pltpu.HBM)] * hbm
    args = [pltpu.with_memory_space_constraint(a, pltpu.HBM) if smem <= i < smem + hbm else a for i, a in enumerate(args)]
    specs += [pl.BlockSpec(memory_space=pltpu.VMEM)] * (len(args) - smem - hbm)
    scratch = list(scratch)
    if hbm:
        scratch += [(pltpu.SMEM if a.ndim == 1 else pltpu.VMEM)(a.shape, a.dtype) for a in args[smem : smem + hbm]] + [pltpu.SemaphoreType.DMA((hbm,))]
    return pl.pallas_call(
        kernel,
        out_shape=[jax.ShapeDtypeStruct(s, d) for s, d in outs],
        in_specs=specs,
        out_specs=[pl.BlockSpec(memory_space=pltpu.HBM if outside else pltpu.VMEM)] * len(outs),
        scratch_shapes=list(scratch),
        compiler_params=pltpu.CompilerParams(vmem_limit_bytes=limit * 2**20),
        cost_estimate=pl.CostEstimate(flops=flops, bytes_accessed=nbytes, transcendentals=0),
    )(*args)


def fetched(sources, buffers, semaphores):
    copies = [pltpu.make_async_copy(a, b, semaphores.at[i]) for i, (a, b) in enumerate(zip(sources, buffers))]
    for copy in copies:
        copy.start()

    def ready(i):
        copies[i].wait()
        return buffers[i]

    return ready


def side_lines(boundary, odd):
    first, second = boundary[0:1, :], boundary[1:2, :]
    return [jnp.where(odd, first, second), jnp.where(odd, second, first), boundary[2:3, :], boundary[3:4, :]]


def prepare_kernel(info, *refs):
    pack, rims = refs[3], refs[4:-4]
    ready = fetched(refs[:3], refs[-4:-1], refs[-1])
    counts = ready(2)
    nodes = ready(0)
    count, width = nodes.shape
    blocks = counts.shape[0]
    size = count // blocks
    feats = nodes[...].astype(F32)
    normed = (feats * lax.rsqrt(jnp.mean(feats * feats, axis=1, keepdims=True) + EPSILON)).astype(BF16)
    pack[0:count, :] = normed
    lane = iota((EXTRA, count), 1)
    row = iota((EXTRA, count), 0)
    limit = jnp.zeros((EXTRA, count), jnp.int32)
    for b in range(blocks):
        limit = jnp.where(lane // size == b, counts[b], limit)
    extra = jnp.where((row == 0) & (lane % size < limit), 1.0, 0.0)
    boundary = ready(1)
    rim = boundary.shape[1]
    slots = boundary[...].astype(F32)
    for side in range(SIDES):
        line = slots[side : side + 1, :]
        if count > rim:
            line = jnp.concatenate([line, jnp.zeros((1, count - rim), F32)], axis=1)
        extra = jnp.where(row == side + 1, line, extra)
    pack[count : count + EXTRA, :] = extra.astype(BF16)
    lines = side_lines(boundary, info[SIDES] > 0)
    for side, out in enumerate(rims):
        place = to_bf(iota((count, rim), 0) == lines[side])
        out[...] = tn(place, normed).astype(BF16)


def head_rows(shape, dim):
    return iota(shape, dim) // HEAD_DIM


def early_kernel(info, *refs):
    copied = 6
    ready = fetched(refs[:copied], refs[-copied - 1 : -1], refs[-1])
    boundary, wq, wk, wv, adjacency, expander = refs[-copied - 1 : -1]
    pack = refs[copied]
    refs = refs[copied + 1 : -copied - 1]
    squares, places, there = refs
    count, width = squares.shape[1:]
    blocks, size = adjacency.shape[0], adjacency.shape[2]
    rim = places.shape[2]
    normed = pack[0:count, :]
    ready(0)
    lines = side_lines(boundary, info[SIDES] > 0)
    ones = jnp.ones((HEADS, rim), BF16)
    for s in range(SIDES):
        place = to_bf((iota((count, rim), 0) == lines[s]) & (info[s] > 0))
        places[s] = place
        there[s] = nt(ones, place)
    ready(1)
    queries = nn(normed, wq[...]).astype(BF16)
    squares[0] = queries
    squares[9] = flip(queries).astype(BF16)
    for k, weight in enumerate((wk, wv)):
        ready(2 + k)
        squares[1 + k] = weight[...]
        turned = flip(weight[...]).astype(BF16)
        squares[3 + k] = turned
        squares[5 + k] = nn(normed, weight[...]).astype(BF16)
        squares[7 + k] = nt(turned, normed).astype(BF16)
    ready(4)
    ready(5)
    flags = pack[count : count + EXTRA, :].astype(F32)[0:1, :]
    eye = iota((size, size), 0) == iota((size, size), 1)
    for b in range(blocks):
        real = flags[:, b * size : (b + 1) * size] > 0.5
        mask = ((adjacency[b] == 1) & real) | eye
        cols = slice(b * size, (b + 1) * size)
        squares[10, 0:size, cols] = flip(jnp.where(mask, 0.0, NEG_FILL)).astype(BF16)
        for m in range(MATCHINGS):
            lo = (m + 1) * size
            squares[10 + lo // count, lo % count : lo % count + size, cols] = flip(jnp.where(expander[m, b] == 1, 0.0, NEG_FILL)).astype(BF16)


def main_kernel(merge_y, info, counts, pairing, *refs):
    copied = 5
    ready = fetched(refs[:copied], refs[-copied - 1 : -1], refs[-1])
    nodes, wo, wup, wdown, gout = refs[-copied - 1 : -1]
    refs = refs[copied : -copied - 1]
    squares, places, there = refs[:3]
    refs = refs[3:]
    weights, weights_t, own_rows, own_cols = (squares.at[i : i + 2] for i in (1, 3, 5, 7))
    packs = [refs[0], *refs[MATCHINGS:0:-1]]
    rims = refs[MATCHINGS + 1 : MATCHINGS + 1 + (2 if merge_y else 4)]
    refs = refs[MATCHINGS + 1 + len(rims) :]
    keep, send, kvg, moves, query_out, hidden_out, activ_out, grad_hidden_out = refs[:8]
    grads, xcat, grown, dotted, pbf, sgrad, qstack, gstack, across, near_rows, near_cols, real_cols = refs[8:]

    count, width = nodes.shape
    hidden_units = wup.shape[1]
    blocks = counts.shape[0]
    size = count // blocks
    keys = (MATCHINGS + 1) * size
    rim = places.shape[2]
    scale = HEAD_DIM**-0.5
    log2e = math.log2(math.e)

    normed = packs[0][0:count, :]
    bias = []
    for m in range(MATCHINGS):
        real_cols[m] = flip(packs[m + 1][count : count + EXTRA, :])
    for b in range(blocks):
        xcat[b * keys : b * keys + size, :] = packs[0][b * size : (b + 1) * size, :]
        for m in range(MATCHINGS):
            start = pl.multiple_of(pairing[m, b] * size, size)
            lo = b * keys + (m + 1) * size
            xcat[lo : lo + size, :] = packs[m + 1][pl.ds(start, size), :]
            real = real_cols[m, pl.ds(start, size), :][:, 0:1]
            at = (m + 1) * size
            kept = squares[10 + at // count, at % count : at % count + size, b * size : (b + 1) * size]
            bias.append(kept.astype(F32) + jnp.where(real > 0.5, 0.0, NEG_FILL))
    base = blocks * keys
    for s in range(SIDES):
        if merge_y and s >= 2:
            other = 3 if s == 2 else 2
            far_slots = packs[2][count : count + EXTRA, :].astype(F32)[other + 1 : other + 2, 0:rim]
            spots = to_bf(iota((count, rim), 0).astype(F32) == far_slots)
            move = nt(places[s], spots).astype(BF16)
            moves[s - 2] = move
            rows = nn(move, packs[2][0:count, :])
        else:
            rows = nn(places[s], rims[s][...])
        xcat[base + s * count : base + (s + 1) * count, :] = rows.astype(BF16)

    queries = squares[0]
    for b in range(blocks):
        rows = xcat[b * keys + size : (b + 1) * keys, :]
        own = slice(b * size, (b + 1) * size)
        for k in range(2):
            near_rows[k, b, 0:size, :] = own_rows[k, own, :]
            near_rows[k, b, size:keys, :] = nn(rows, weights[k]).astype(BF16)
            near_cols[k, b, :, 0:size] = own_cols[k, :, own]
            near_cols[k, b, :, size:keys] = nt(weights_t[k], rows).astype(BF16)
    row_head = head_rows((width, size), 0)
    lane_head = head_rows((size, width), 1)
    for b in range(blocks):
        own, own_t = queries[b * size : (b + 1) * size, :], squares[9, :, b * size : (b + 1) * size]
        for h in range(HEADS):
            at = slice(h * size, (h + 1) * size)
            across[b, :, at] = jnp.where(row_head == h, own_t, jnp.zeros_like(own_t))
            qstack[b, at, :] = jnp.where(lane_head == h, own, jnp.zeros_like(own))
    rim_keys, rim_values = [], []
    for s in range(SIDES):
        rows = xcat[base + s * count : base + (s + 1) * count, :]
        rim_keys.append(nn(rows, weights[0]).astype(BF16).astype(F32))
        rim_values.append(nn(rows, weights[1]).astype(BF16).astype(F32))
    bias = [
        [squares[10, 0:size, b * size : (b + 1) * size].astype(F32)] + bias[b * MATCHINGS : (b + 1) * MATCHINGS]
        for b in range(blocks)
    ]

    spread = to_bf(head_rows((HEADS, width), 1) == iota((HEADS, width), 0))

    def head_sums(product):
        high = product.astype(BF16)
        low = (product - high.astype(F32)).astype(BF16)
        return nt(spread, high) + nt(spread, low)

    queries_f = queries.astype(F32)
    rim_scores = []
    for s in range(SIDES):
        score = head_sums(queries_f * rim_keys[s]) * (scale * log2e)
        rim_scores.append(jnp.where(there[s] > 0.5, score, NEG_FILL))
    rim_top = jnp.maximum(jnp.maximum(rim_scores[0], rim_scores[1]), jnp.maximum(rim_scores[2], rim_scores[3]))

    pairs = [(b, first) for b in range(blocks) for first in range(0, HEADS, 2)]
    groups = STEPS
    chunk = keys // groups

    def folded(value, combine):
        part = value[0:8]
        for lo in range(8, value.shape[0], 8):
            part = combine(part, value[lo : lo + 8])
        return part

    def both_heads(table, b, first):
        cols = slice(b * size, (b + 1) * size)
        return jnp.concatenate([table[first : first + 1, cols], table[first + 1 : first + 2, cols]], axis=1)

    tops, sums, inverses, att_parts = {}, {}, {}, {}

    def make_scores(u, c):
        b, first = pairs[u]
        at = slice(first * size, (first + 2) * size)
        rows = slice(c * chunk, (c + 1) * chunk)
        score = nn(near_rows[0, b, rows, :], across[b, :, at]) * (scale * log2e)
        barred = jnp.concatenate(bias[b][c * chunk // size : (c + 1) * chunk // size], axis=0)
        score = score + jnp.concatenate([barred, barred], axis=1)
        grown[b, rows, at] = score
        part = folded(score, jnp.maximum)
        tops[u] = part if c == 0 else jnp.maximum(tops[u], part)
        if c == groups - 1:
            tops[u] = jnp.maximum(jnp.max(tops[u], axis=0, keepdims=True), both_heads(rim_top, b, first))

    def make_exp(u, c):
        b, first = pairs[u]
        at = slice(first * size, (first + 2) * size)
        rows = slice(c * chunk, (c + 1) * chunk)
        raised = jnp.exp2(grown[b, rows, at] - tops[u])
        grown[b, rows, at] = raised
        part = folded(raised, jnp.add)
        sums[u] = part if c == 0 else sums[u] + part
        if c == groups - 1:
            total = jnp.sum(sums[u], axis=0, keepdims=True)
            for s in range(SIDES):
                total = total + jnp.exp2(both_heads(rim_scores[s], b, first) - tops[u])
            inverses[u] = 1.0 / total

    def make_probs(u, c):
        b, first = pairs[u]
        at = slice(first * size, (first + 2) * size)
        rows = slice(c * chunk, (c + 1) * chunk)
        pbf[b, rows, at] = (grown[b, rows, at] * inverses[u]).astype(BF16)

    def make_mix(u):
        b, first = pairs[u]
        rows = slice(first * HEAD_DIM, (first + 2) * HEAD_DIM)
        wide = nn(near_cols[1, b, rows, :], pbf[b, :, first * size : (first + 2) * size])
        att_parts[u] = [wide[0:HEAD_DIM, 0:size], wide[HEAD_DIM:, size:]]

    def staggered(stages, last):
        for t in range(len(pairs) + len(stages)):
            for c in range(groups):
                for late, stage in enumerate(stages):
                    if 0 <= t - late < len(pairs):
                        stage(t - late, c)
            if 0 <= t - len(stages) < len(pairs):
                last(t - len(stages))

    staggered([make_scores, make_exp, make_probs], make_mix)

    def by_block(values):
        per = HEADS // 2
        return jnp.concatenate(
            [jnp.concatenate(sum((values[b * per + i] for i in range(per)), []), axis=0) for b in range(blocks)], axis=1
        )

    def halves(values):
        return {u: [v[:, 0:size], v[:, size:]] for u, v in values.items()}

    top_all = by_block(halves(tops))
    inv_all = by_block(halves(inverses))
    mixed = flip(by_block(att_parts))
    rim_probs = [jnp.exp2(rim_scores[s] - top_all) * inv_all for s in range(SIDES)]
    rim_wide = [tn(rim_probs[s].astype(BF16), spread) for s in range(SIDES)]
    for s in range(SIDES):
        mixed = mixed + rim_wide[s] * rim_values[s]
    attended = mixed.astype(BF16)

    slot = iota((count, width), 0)
    limit = jnp.zeros((count, width), jnp.int32)
    for b in range(blocks):
        limit = jnp.where(slot // size == b, counts[b], limit)
    usable = jnp.where(slot % size < limit, 1.0, 0.0)
    for i in range(copied):
        ready(i)
    feats = nodes[...].astype(F32)
    hidden = feats + nn(attended, wo[...])
    factor = lax.rsqrt(jnp.mean(hidden * hidden, axis=1, keepdims=True) + EPSILON)
    mid = hidden * factor
    normed_mid = mid.astype(BF16)
    pre = nn(normed_mid, wup[...])
    square = pre * pre
    bent = jnp.tanh(GELU_C * pre * (1.0 + GELU_A * square))
    half = 0.5 * (1.0 + bent)
    activ = (pre * half).astype(BF16)
    hidden_out[...] = hidden
    activ_out[...] = activ
    upstream = gout[...].astype(F32) * usable
    upstream_bf = upstream.astype(BF16)
    grads[4 * width + hidden_units * 1 : 4 * width + 2 * hidden_units, :] = tn(activ, upstream_bf)
    slope = half + 0.5 * pre * (1.0 - bent * bent) * (GELU_C * (1.0 + 3.0 * GELU_A * square))
    grad_pre = (slope * nt(upstream_bf, wdown[...])).astype(BF16)
    grad_up = tn(normed_mid, grad_pre)
    for part in range(hidden_units // width):
        lo = 4 * width + part * width
        grads[lo : lo + width, :] = grad_up[:, part * width : (part + 1) * width]
    grad_mid = nt(grad_pre, wup[...])
    grad_hidden = upstream + factor * (grad_mid - mid * jnp.mean(grad_mid * mid, axis=1, keepdims=True))
    grad_hidden_out[...] = grad_hidden
    grad_hidden_bf = grad_hidden.astype(BF16)
    grads[3 * width : 4 * width, :] = tn(attended, grad_hidden_bf)
    grad_att = nt(grad_hidden_bf, wo[...]).astype(BF16)
    grad_att_f = grad_att.astype(F32)
    grad_att_t = flip(grad_att).astype(BF16)

    rim_dots = [head_sums(grad_att_f * rim_values[s]) for s in range(SIDES)]
    rim_inner = rim_probs[0] * rim_dots[0]
    for s in range(1, SIDES):
        rim_inner = rim_inner + rim_probs[s] * rim_dots[s]
    for b in range(blocks):
        own, own_t = grad_att[b * size : (b + 1) * size, :], grad_att_t[:, b * size : (b + 1) * size]
        for h in range(HEADS):
            at = slice(h * size, (h + 1) * size)
            across[b, :, at] = jnp.where(row_head == h, own_t, jnp.zeros_like(own_t))
            gstack[b, at, :] = jnp.where(lane_head == h, own, jnp.zeros_like(own))
    inners, query_parts = {}, {}

    def make_dots(u, c):
        b, first = pairs[u]
        at = slice(first * size, (first + 2) * size)
        rows = slice(c * chunk, (c + 1) * chunk)
        dots = nn(near_rows[1, b, rows, :], across[b, :, at])
        dotted[b, rows, at] = dots
        part = folded(grown[b, rows, at] * dots, jnp.add)
        inners[u] = part if c == 0 else inners[u] + part
        if c == groups - 1:
            inners[u] = jnp.sum(inners[u], axis=0, keepdims=True) * inverses[u] + both_heads(rim_inner, b, first)

    def make_grads(u, c):
        b, first = pairs[u]
        at = slice(first * size, (first + 2) * size)
        rows = slice(c * chunk, (c + 1) * chunk)
        graded = grown[b, rows, at] * ((dotted[b, rows, at] - inners[u]) * (inverses[u] * scale))
        sgrad[b, rows, at] = graded.astype(BF16)

    def make_query(u):
        b, first = pairs[u]
        rows = slice(first * HEAD_DIM, (first + 2) * HEAD_DIM)
        wide = nn(near_cols[0, b, rows, :], sgrad[b, :, first * size : (first + 2) * size])
        query_parts[u] = [wide[0:HEAD_DIM, 0:size], wide[HEAD_DIM:, size:]]

    staggered([make_dots, make_grads], make_query)
    for b in range(blocks):
        span = slice(b * keys, (b + 1) * keys)
        kvg[span, 0:width] = nn(sgrad[b], qstack[b]).astype(BF16)
        kvg[span, width : 2 * width] = nn(pbf[b], gstack[b]).astype(BF16)
    inner_all = by_block(halves(inners))
    query_grad = flip(by_block(query_parts))
    for s in range(SIDES):
        graded = (rim_probs[s] * (rim_dots[s] - inner_all) * scale).astype(BF16)
        wide = tn(graded, spread)
        query_grad = query_grad + wide * rim_keys[s]
        span = slice(base + s * count, base + (s + 1) * count)
        kvg[span, 0:width] = (wide * queries_f).astype(BF16)
        kvg[span, width : 2 * width] = (rim_wide[s] * grad_att_f).astype(BF16)
    query_total = query_grad.astype(BF16)

    query_out[...] = query_total
    grads[0:width, :] = tn(normed, query_total)
    both = tn(xcat[...], kvg[...])
    grads[width : 2 * width, :] = both[:, 0:width]
    grads[2 * width : 3 * width, :] = both[:, width : 2 * width]

    half_rows = grads.shape[0] // 2
    mine = info[SIDES]
    keep[...] = grads[pl.ds(pl.multiple_of(mine * half_rows, half_rows), half_rows), :]
    send[...] = grads[pl.ds(pl.multiple_of((1 - mine) * half_rows, half_rows), half_rows), :].astype(BF16)


def back_kernel(merge_y, pairing, *refs):
    kvg, moves, places, squares = refs[:4]
    own_out, *rest = refs[4:]
    backs, rim_outs, extra = rest[:MATCHINGS], rest[MATCHINGS:-1], rest[-1]
    count, width = own_out.shape
    blocks = pairing.shape[1]
    size = count // blocks
    keys = (MATCHINGS + 1) * size
    base = blocks * keys
    wk_t, wv_t = squares[3], squares[4]
    extra_back = None
    for s in range(SIDES):
        span = slice(base + s * count, base + (s + 1) * count)
        back = (nn(kvg[span, 0:width], wk_t) + nn(kvg[span, width : 2 * width], wv_t)).astype(BF16)
        if merge_y and s >= 2:
            moved = tn(moves[s - 2], back)
            extra_back = moved if extra_back is None else extra_back + moved
        else:
            rim_outs[s][...] = tn(places[s], back).astype(BF16)
    if merge_y:
        extra[...] = extra_back
    for b in range(blocks):
        span = slice(b * keys, (b + 1) * keys)
        back = nn(kvg[span, 0:width], wk_t) + nn(kvg[span, width : 2 * width], wv_t)
        own_out[b * size : (b + 1) * size, :] = back[0:size]
        for m in range(MATCHINGS):
            start = pl.multiple_of(pairing[m, b] * size, size)
            piece = back[(m + 1) * size : (m + 2) * size]
            if merge_y and m == 1:
                piece = piece + extra[pl.ds(start, size), :]
            backs[m][pl.ds(start, size), :] = piece.astype(BF16)


def output_kernel(counts, *refs):
    copied = 4
    ready = fetched(refs[:copied], refs[-copied - 1 : -1], refs[-1])
    wq, wdown, nodes, boundary = refs[-copied - 1 : -1]
    own_back, query_total, hidden, activ = refs[copied : copied + 4]
    layer_out, grad_normed_out, nodes_out, boundary_out = refs[copied + 4 : -copied - 1]
    count, width = hidden.shape
    blocks = counts.shape[0]
    size = count // blocks
    slot = iota((count, width), 0)
    limit = jnp.zeros((count, width), jnp.int32)
    for b in range(blocks):
        limit = jnp.where(slot // size == b, counts[b], limit)
    usable = jnp.where(slot % size < limit, 1.0, 0.0)
    ready(0)
    grad_normed_out[...] = nt(query_total[...], wq[...]) + own_back[...]
    ready(1)
    layer_out[...] = ((hidden[...] + nn(activ[...], wdown[...])) * usable).astype(BF16)
    ready(2)
    nodes_out[...] = nodes[...]
    ready(3)
    boundary_out[...] = boundary[...]


def nodes_kernel(info, *refs):
    nodes, boundary, grad_hidden, grad_normed = refs[:4]
    backs, rims, out = refs[4 : 4 + MATCHINGS], refs[4 + MATCHINGS : -1], refs[-1]
    lines = side_lines(boundary, info[SIDES] > 0)
    count = nodes.shape[0]
    rim = boundary.shape[1]
    cot = grad_normed[...]
    for back in backs:
        cot = cot + back[...].astype(F32)
    for s, rows in enumerate(rims):
        place = to_bf(iota((count, rim), 0) == lines[s])
        cot = cot + nn(place, rows[...])
    feats = nodes[...].astype(F32)
    factor = lax.rsqrt(jnp.mean(feats * feats, axis=1, keepdims=True) + EPSILON)
    normed = feats * factor
    out[...] = (grad_hidden[...] + factor * (cot - normed * jnp.mean(cot * normed, axis=1, keepdims=True))).astype(BF16)


def reduce_kernel(place, parts, *refs):
    info, kept, received = refs[0], refs[1], refs[2 : -1 - parts]
    outs, total_ref = refs[-1 - parts : -1], refs[-1]
    total = kept[...].astype(F32)
    for piece in received:
        total = total + piece[...].astype(F32)
    if parts == 1:
        outs[0][...] = total.astype(BF16)
        return
    total_ref[...] = total
    rows = total.shape[0] // parts
    mine = info[place]
    outs[0][...] = total_ref[pl.ds(pl.multiple_of(mine * rows, rows), rows), :]
    for d in range(1, parts):
        outs[d][...] = total_ref[pl.ds(pl.multiple_of((mine ^ d) * rows, rows), rows), :].astype(outs[d].dtype)


def gather_kernel(place, turn, *refs):
    info, pieces, out = refs[0], [refs[1], *refs[2:-1][::turn]], refs[-1]
    mine = info[place]
    rows = pieces[0].shape[0]
    for d, piece in enumerate(pieces):
        out[pl.ds(pl.multiple_of((mine ^ d) * rows, rows), rows), :] = piece[...]


def final_kernel(place, info, own, other, *refs):
    count = (len(refs) - 1) // 2
    outs, buffers, semaphores = refs[:count], refs[count:-1], refs[-1]
    rows, width = own.shape
    mine = info[place]
    row = 0
    copies = []
    for i, (out, buffer) in enumerate(zip(outs, buffers)):
        for part in range(buffer.shape[1] // width):
            half, lo = divmod(row, rows)
            span = slice(lo, lo + buffer.shape[0])
            value = jnp.where(mine == half, own[span, :].astype(F32), other[span, :].astype(F32))
            buffer[:, part * width : (part + 1) * width] = value
            row += buffer.shape[0]
        copies.append(pltpu.make_async_copy(buffer, out, semaphores.at[i]))
        copies[-1].start()
    for copy in copies:
        copy.wait()


def bit_of(mask_bits, index):
    value = jnp.int32(0)
    for k, bit in enumerate(mask_bits):
        value = value | (((index >> bit) & 1) << k)
    return value


def offset_mask(bits, d):
    return sum(1 << bit for k, bit in enumerate(bits) if d >> k & 1)


def all_sum(info, keep, arrived, groups, core_mask, beside, store):
    width = keep.shape[1]
    kept, pieces = keep, [arrived]
    stage = 0

    def exchange(values, masks, whole):
        nonlocal stage
        work = beside.get(stage)
        stage += 1
        if work is None:
            return whole, [xor_permute(v, m) for v, m in zip(values, masks)]
        values, waited = work(tuple(values))
        turn = 1 if stage == 2 * len(groups) else -1
        moved = [xor_permute(v, m) for v, m in zip(values[::turn], masks[::turn])]
        moved, done = lax.optimization_barrier((tuple(moved), waited()))
        store.update(done)
        return whole, list(moved[::turn])

    for level, bits in enumerate(groups):
        parts = 2 ** len(bits)
        rows = kept.shape[0] // parts
        made = call(
            lambda *r, level=level, parts=parts: reduce_kernel(SIDES + 1 + level, parts, *r),
            [((rows, width), F32)] + [((rows, width), F32 if level else BF16)] * (parts - 1),
            [info, kept, *pieces[::-1]],
            smem=1,
            scratch=[pltpu.VMEM(kept.shape, F32)],
        )
        kept, pieces = exchange(made[1:], [offset_mask(bits, d) for d in range(1, parts)], made[0])
    whole = call(
        lambda *r: reduce_kernel(0, 1, *r),
        [(kept.shape, BF16)],
        [info, kept, *pieces[::-1]],
        smem=1,
        scratch=[pltpu.VMEM((8, 128), F32)],
    )[0]
    for level in reversed(range(len(groups))):
        masks = [offset_mask(groups[level], d) for d in range(1, 2 ** len(groups[level]))]
        whole, pieces = exchange([whole] * len(masks), masks, whole)
        whole = call(
            lambda *r, level=level, turn=-1 if level else 1: gather_kernel(SIDES + 1 + level, turn, *r),
            [((whole.shape[0] * (1 + len(masks)), width), BF16)],
            [info, whole, *pieces[:: -1 if level else 1]],
            smem=1,
        )[0]
    return whole, xor_permute(whole, core_mask)


def shards(nodes, grad_out, w_query, w_key, w_value, w_out, w_up, w_down, counts, adjacency, expander, pairing, boundary):
    batch, count, width = nodes.shape[2:]
    feats, gout = nodes.reshape(count, width), grad_out.reshape(count, width)
    counts, boundary, pairing = counts[0, 0], boundary[0, 0], pairing[0, 0]
    adjacency, expander = adjacency[0, 0], expander[0, 0]
    rim = boundary.shape[1]
    size_x, size_y = lax.axis_size("sx"), lax.axis_size("sy")
    bits_x, bits_y = size_x.bit_length() - 1, size_y.bit_length() - 1
    merge_y = size_y == 2
    partner = [1 << (bits_x - 1 + bits_y), 1 << (bits_y - 1), 1 << (bits_x - 2 + bits_y)]
    core_bit = bits_y
    rest = [bit for bit in range(bits_x + bits_y) if bit != core_bit]
    groups = [rest[i : i + 2] for i in range(0, len(rest), 2)]
    ix, iy = lax.axis_index("sx"), lax.axis_index("sy")
    index = ix * size_y + iy
    info = jnp.stack(
        [ix >= 0, jnp.where(ix % 2 == 0, ix > 0, ix < size_x - 1), iy > 0, iy < size_y - 1]
        + [bit_of([core_bit], index)]
        + [bit_of(bits, index) for bits in groups]
    ).astype(jnp.int32)

    rim_count = 2 if merge_y else 4
    prepared = call(
        prepare_kernel,
        [((count + EXTRA, width), BF16)] + [((rim, width), BF16)] * rim_count,
        [info, feats, boundary, counts],
        smem=1,
        hbm=3,
    )
    pack, sent = prepared[0], prepared[1:]
    arrived = [pair_permute(sent[0], False), pair_permute(sent[1], True)]
    if not merge_y:
        arrived += [from_behind(sent[3], "sy", 1), from_behind(sent[2], "sy", -1)]
    far = [xor_permute(pack, mask) for mask in reversed(partner)][::-1]

    blocks = counts.shape[0]
    size = count // blocks
    keys = (MATCHINGS + 1) * size
    units = w_up.shape[1]
    total_rows = 4 * width + 2 * units
    all_rows = blocks * keys + SIDES * count
    square = (count, width)
    heads_wide = HEADS * size
    early = call(
        early_kernel,
        [
            ((10 + keys // count, *square), BF16),
            ((SIDES, count, rim), BF16),
            ((SIDES, HEADS, count), F32),
        ],
        [info, boundary, w_query, w_key, w_value, adjacency, expander, pack],
        smem=1,
        hbm=6,
        flops=2 * 10**9,
        nbytes=4 * 2**20,
    )
    places, squares = early[1], early[0]
    moves_shape = (2, count, count)
    made = call(
        lambda *r: main_kernel(merge_y, *r),
        [
            ((total_rows // 2, width), F32),
            ((total_rows // 2, width), BF16),
            ((all_rows, 2 * width), BF16),
            (moves_shape, BF16),
            (square, BF16),
            (square, F32),
            ((count, units), BF16),
            (square, F32),
        ],
        [info, counts, pairing, feats, w_out, w_up, w_down, gout, *early, pack, *far[::-1], *arrived],
        smem=3,
        hbm=5,
        scratch=[
            pltpu.VMEM((total_rows, width), F32),
            pltpu.VMEM((all_rows, width), BF16),
            pltpu.VMEM((blocks, keys, heads_wide), F32),
            pltpu.VMEM((blocks, keys, heads_wide), F32),
            pltpu.VMEM((blocks, keys, heads_wide), BF16),
            pltpu.VMEM((blocks, keys, heads_wide), BF16),
            pltpu.VMEM((blocks, heads_wide, width), BF16),
            pltpu.VMEM((blocks, heads_wide, width), BF16),
            pltpu.VMEM((blocks, width, heads_wide), BF16),
            pltpu.VMEM((2, blocks, keys, width), BF16),
            pltpu.VMEM((2, blocks, width, keys), BF16),
            pltpu.VMEM((MATCHINGS, count, EXTRA), F32),
        ],
        limit=32,
        flops=10**10,
        nbytes=8 * 2**20,
    )
    keep, send, kvg, moves, query_total, hidden, activ, grad_hidden = made
    store = {}

    def first_stage(values):
        values, gradients = lax.optimization_barrier((values, kvg))
        store["back"] = call(
            lambda *r: back_kernel(merge_y, *r),
            [(square, F32)] + [(square, BF16)] * MATCHINGS + [((rim, width), BF16)] * rim_count,
            [pairing, gradients, moves, places, squares],
            smem=1,
            scratch=[pltpu.VMEM(square, F32)],
            flops=2 * 10**9,
            nbytes=4 * 2**20,
        )

        def waited():
            back = store["back"]
            store["m0"] = xor_permute(back[1], partner[0])
            store["m2"] = xor_permute(back[3], partner[2])
            return {}

        return values, waited

    def second_stage(values):
        back = store["back"]
        values, own_back = lax.optimization_barrier((values, back[0]))
        store["out"] = call(
            output_kernel,
            [(square, BF16), (square, F32), (square, BF16), (boundary.shape, boundary.dtype)],
            [counts, w_query, w_down, feats, boundary, own_back, query_total, hidden, activ],
            smem=1,
            hbm=4,
            flops=10**9,
            nbytes=2 * 2**20,
        )

        return values, lambda: {"out": tuple(store["out"])}

    def third_stage(values):
        back = store["back"]
        values, cargo = lax.optimization_barrier((values, (back[2], *back[4:])))
        m1, near, beyond, *sides = cargo
        store["m1"] = xor_permute(m1, partner[1])
        store["rims"] = [pair_permute(near, False), pair_permute(beyond, True)]
        if sides:
            store["rims"] += [from_behind(sides[1], "sy", 1), from_behind(sides[0], "sy", -1)]
        return values, lambda: {"m0": store["m0"], "m2": store["m2"]}

    def fourth_stage(values):
        return values, lambda: {"m1": store["m1"], "rims": store["rims"]}

    core_mask = 1 << core_bit
    own, other = all_sum(
        info, keep, xor_permute(send, core_mask), groups, core_mask, {0: first_stage, 1: second_stage, 2: third_stage, 3: fourth_stage}, store
    )
    layer_out, _, nodes_near, boundary_near = store["out"]
    grad_normed = store["out"][1]
    returned = [store["m0"], store["m1"], store["m2"]]
    rims = store["rims"]
    grad_nodes = call(
        nodes_kernel,
        [(square, BF16)],
        [info, nodes_near, boundary_near, grad_hidden, grad_normed, *returned, *rims],
        smem=1,
    )[0]
    shapes = [((width, width), F32)] * 4 + [((width, units), F32), ((units, width), F32)]
    weights = call(
        lambda *r: final_kernel(SIDES, *r),
        shapes,
        [info, own, other],
        smem=1,
        scratch=[pltpu.VMEM(*shape) for shape in shapes] + [pltpu.SemaphoreType.DMA((len(shapes),))],
        outside=True,
    )
    return (layer_out.reshape(nodes.shape), grad_nodes.reshape(nodes.shape), *weights)


def solution(mesh):
    grid = lambda n: P("sx", "sy", *([None] * n))
    return jax.shard_map(
        shards,
        mesh=mesh,
        in_specs=(grid(3), grid(3), P(), P(), P(), P(), P(), P(), grid(1), grid(3), grid(4), grid(2), grid(2)),
        out_specs=(grid(3), grid(3), P(), P(), P(), P(), P(), P()),
        check_vma=False,
    )
```
